32 devices in a mesh: section: 2 (over core), replica: 4 (over z), shard: 4 (over y, x).
Axes of the slice: x: 2, y: 2, z: 4, core: 2. Of those that a mesh axis runs over, the one named last changes fastest.
Arguments:
- inputs: bfloat16 [4, 2, 1024, 384], P('replica', None, 'shard'), may hold values from -6 to 6
- cotangent: bfloat16 [4, 2, 1024, 384], P('replica', None, 'shard'), may hold values from -6 to 6
- clip_present: int32 [4, 2], P('replica'), may hold values 0 or 1
- qkv_weight: bfloat16 [2, 384, 1152], P('section', 'shard'), may hold values from -0.4375 to 0.4375
- out_weight: bfloat16 [2, 384, 384], P('section', 'shard'), may hold values from -0.875 to 0.875
- up_weight: bfloat16 [2, 384, 1536], P('section', 'shard'), may hold values from -0.3125 to 0.3125
- down_weight: bfloat16 [2, 1536, 384], P('section', 'shard'), may hold values from -0.15625 to 0.15625
- norm_gains: float32 [2, 2, 384], P('section'), may hold values from 0.5 to 1.5
- biases: float32 [2, 6, 384], P('section'), may hold values from -3 to 3
- up_bias: float32 [2, 1536], P('section'), may hold values from -3 to 3
Outputs:
- section_outputs: bfloat16 [2, 4, 2, 1024, 384], P('section', 'replica', None, 'shard')
- input_grads: bfloat16 [2, 4, 2, 1024, 384], P('section', 'replica', None, 'shard')
- qkv_grad: float32 [2, 384, 1152], P('section', ('replica', 'shard'))
- out_grad: float32 [2, 384, 384], P('section', ('replica', 'shard'))
- up_grad: float32 [2, 384, 1536], P('section', ('replica', 'shard'))
- down_grad: float32 [2, 1536, 384], P('section', ('replica', 'shard'))
- gain_grad: float32 [2, 2, 384], P('section', None, ('replica', 'shard'))
- bias_grad: float32 [2, 6, 384], P('section', None, ('replica', 'shard'))
- up_bias_grad: float32 [2, 1536], P('section', ('replica', 'shard'))
The draws below stay inside these ranges and needn't reach their ends.
All inputs are finite; a program needn't handle non-finite values. No bound on the sum of `clip_present` on one device may be relied on, other than what follows from the above.
Results may differ from the reference program's by a relative error of at most 0.019.
Values may be sent and summed in bfloat16 or wider, within the bound.
No kernel may reach another device: no remote copies, remote signals or barrier semaphores. Data moves between devices by JAX's collectives and lax.ppermute only.
A program may use at most 128 MiB of HBM per device.

```python
import jax
import jax.numpy as jnp
from jax import lax

D = 384
HEADS = 6
HEAD_DIM = 64
FF = 1536
MICRO = 2
FRAMES = 1024
N_REPLICA = 4


def with_ends(entries, key, smallest, largest):
    longest = entries.shape.index(max(entries.shape))
    spots = []
    for shift in (0, 1):
        where = [jax.random.randint(jax.random.fold_in(key, axis), (), 0, length) for axis, length in enumerate(entries.shape)]
        where[longest] = (where[longest] + shift) % entries.shape[longest]
        spots.append(tuple(where))
    return entries.at[spots[0]].set(smallest).at[spots[1]].set(largest)


def spiked(array, stream_key, source, target, blocks, factor):
    owner, partner = [(jnp.arange(array.shape[axis_at]) // (array.shape[axis_at] // blocks)).reshape([-1 if axis == axis_at else 1 for axis in range(array.ndim)]) for axis_at in (source, target)]
    chosen = jax.random.permutation(stream_key, blocks)[partner]
    strong = (owner == chosen) | (owner == (partner + blocks // 2) % blocks)
    return jnp.where(strong, factor * array, array)


def shard_levels(own_key, dims, shards, least, largest):
    factor_of = 1.0
    for axis_at, shards_of in shards:
        draws = jax.random.uniform(jax.random.fold_in(jax.random.fold_in(own_key, 6), axis_at), (shards_of,), jnp.float32, least / len(shards), largest / len(shards))
        factor_of = factor_of * jnp.repeat(jnp.exp(draws), dims[axis_at] // shards_of).reshape((-1,) + (1,) * (len(dims) - 1 - axis_at))
    return factor_of


def noise(rng, dims, deviation, limit, shards=(), dtype=jnp.bfloat16):
    values = jax.random.normal(rng, dims, jnp.float32) * deviation
    if len(shards) > 0:
        values = shard_levels(rng, dims, shards, -0.22, 0.18) * values
    return jnp.clip(values, min=-limit, max=limit).astype(dtype)


def bell_draw_with(key, dims, scale, most, split, heavy, kind=jnp.bfloat16):
    drawn = scale * jax.random.normal(key, dims, jnp.float32)
    if split:
        drawn = drawn * shard_levels(key, dims, split, -0.22, 0.18)
    return jnp.clip(spiked(drawn, jax.random.fold_in(key, 3), *heavy), -most, most).astype(kind)


def setup_inputs(seed: int = 0) -> dict:
    streams_of = jax.random.split(jax.random.key(seed), 11)
    inputs = noise(streams_of[0], (N_REPLICA, MICRO, FRAMES, D), 1.0, 6.0, ((0, 4), (2, 4)))
    cotangent = bell_draw_with(streams_of[1], (N_REPLICA, MICRO, FRAMES, D), 1.0, 6.0, ((0, 4), (2, 4)), (0, 3, 4, 2.0))
    clip_present = with_ends((jax.random.randint(streams_of[2], (N_REPLICA, MICRO), 0, 4) < 3).astype(jnp.int32), jax.random.fold_in(streams_of[2], 1), 0, 1)
    qkv_weight = noise(streams_of[3], (2, D, 3 * D), (D // 2) ** -0.5, 0.4375, ((0, 2), (1, 4)))
    out_weight = noise(streams_of[4], (2, D, D), (D // 8) ** -0.5, 0.875, ((0, 2), (1, 4)))
    up_weight = noise(streams_of[5], (2, D, FF), D ** -0.5, 0.3125, ((0, 2), (1, 4)))
    down_weight = noise(streams_of[6], (2, FF, D), FF ** -0.5, 0.15625, ((0, 2), (1, 4)))
    norm_gains = jnp.clip(1.0 + 0.1 * jax.random.normal(streams_of[7], (2, 2, D), jnp.float32), 0.5, 1.5)
    biases = noise(streams_of[8], (2, 6, D), 0.5, 3.0, ((0, 2),), jnp.float32)
    up_bias = noise(streams_of[9], (2, FF), 0.5, 3.0, ((0, 2),), jnp.float32)
    return {"inputs": inputs, "cotangent": cotangent, "clip_present": clip_present, "qkv_weight": qkv_weight, "out_weight": out_weight, "up_weight": up_weight, "down_weight": down_weight, "norm_gains": norm_gains, "biases": biases, "up_bias": up_bias}


@jax.custom_vjp
def low(v):
    return lax.optimization_barrier(v.astype(jnp.bfloat16)).astype(jnp.float32)

@jax.custom_vjp
def low_back(v):
    return v

def low_keep(v):
    return (low(v), None)

def low_pass(kept, grad):
    return (grad,)

def back_keep(v):
    return (v, None)

def back_low(kept, grad):
    return (low(grad),)
low.defvjp(low_keep, low_pass)
low_back.defvjp(back_keep, back_low)

def matmul(left, right):
    return jnp.dot(left, right, precision=lax.Precision.HIGHEST, preferred_element_type=jnp.float32)

def norm_apply(values, gain, shift):
    center = values - lax.optimization_barrier(jnp.mean(values, axis=-1, keepdims=True))
    spread = lax.optimization_barrier(jnp.mean(center * center, axis=-1, keepdims=True))
    return center * lax.rsqrt(spread + 1e-05) * gain + shift

def layer(frames, qkv_w, out_w, up_w, down_w, gains, biases, up_b):
    length = frames.shape[0]
    a_low = low(norm_apply(frames, gains[0], biases[0]))
    bias_three = jnp.concatenate([biases[1], jnp.zeros_like(biases[1]), biases[2]])
    qkv = low_back(low(matmul(a_low, qkv_w) + bias_three))
    query = qkv[:, :D].reshape(length, HEADS, HEAD_DIM)
    keys = qkv[:, D:2 * D].reshape(length, HEADS, HEAD_DIM)
    values = qkv[:, 2 * D:].reshape(length, HEADS, HEAD_DIM)
    scores = low_back(jnp.einsum('qhd,khd->hqk', query, keys, precision=lax.Precision.HIGHEST) * HEAD_DIM ** (-0.5))
    probs = low(jax.nn.softmax(scores, axis=-1))
    mixed = jnp.einsum('hqk,khd->qhd', probs, values, precision=lax.Precision.HIGHEST).reshape(length, D)
    mixed = low_back(low(mixed))
    resid = frames + low_back(matmul(mixed, out_w) + biases[3])
    c_low = low(norm_apply(resid, gains[1], biases[4]))
    upper = low_back(matmul(c_low, up_w) + up_b)
    z_low = low(jax.nn.gelu(upper, approximate=False))
    return resid + low_back(matmul(z_low, down_w) + biases[5])

def run_section(clips, params):

    def one_clip(frames):
        return low(layer(frames, *params))
    return lax.map(jax.checkpoint(one_clip), clips)

def reference(inputs, cotangent, clip_present, qkv_weight, out_weight, up_weight, down_weight, norm_gains, biases, up_bias):
    count = N_REPLICA * MICRO
    mask = clip_present.reshape(count).astype(jnp.float32)[:, None, None]
    every = (qkv_weight, out_weight, up_weight, down_weight, norm_gains, biases, up_bias)

    def params(index):
        return tuple((w[index].astype(jnp.float32) for w in every))

    def masked(frames, weights):
        return run_section(frames, weights) * mask
    start = inputs.reshape(count, FRAMES, D).astype(jnp.float32)
    first_out, first_back = jax.vjp(masked, start, params(0))
    second_out, second_back = jax.vjp(masked, first_out, params(1))
    middle_grad, second_grads = second_back(cotangent.reshape(count, FRAMES, D).astype(jnp.float32))
    middle_grad = low(middle_grad)
    start_grad, first_grads = first_back(middle_grad)
    shape = (N_REPLICA, MICRO, FRAMES, D)
    section_outputs = jnp.stack([first_out.reshape(shape), second_out.reshape(shape)]).astype(jnp.bfloat16)
    input_grads = jnp.stack([start_grad.reshape(shape), middle_grad.reshape(shape)]).astype(jnp.bfloat16)
    stacked = tuple((jnp.stack([first_grads[i], second_grads[i]]) for i in range(7)))
    return (section_outputs, input_grads, stacked[0], stacked[1], stacked[2], stacked[3], stacked[4], stacked[5], stacked[6])
```

```python
import functools

import jax
import jax.numpy as jnp
from jax import lax
from jax.experimental import pallas as pl
from jax.experimental.pallas import tpu as pltpu
from jax.sharding import PartitionSpec as P

D = 384
HEADS = 6
HEAD_DIM = 64
FF = 1536
PAIR = 2 * HEAD_DIM
HALF = 768
SHARDS = 4
BF = jnp.bfloat16
F32 = jnp.float32
VEC_ROWS = 16

NT = (((1,), (1,)), ((), ()))
TN = (((0,), (0,)), ((), ()))


def dot(left, right, dims=(((1,), (0,)), ((), ()))):
    return lax.dot_general(left, right, dims, preferred_element_type=F32)


def xor_pass(x, axis, by):
    pairs = [(i, i ^ by) for i in range(lax.axis_size(axis))]
    return lax.ppermute(x, axis, pairs)


def call(kernel, outs, args, name, flops, scalars=1, scratch=()):
    smem = pl.BlockSpec(memory_space=pltpu.SMEM)
    vmem = pl.BlockSpec(memory_space=pltpu.VMEM)
    size = sum(a.size * a.dtype.itemsize for a in args)
    size += sum(o.size * o.dtype.itemsize for o in outs)
    return pl.pallas_call(
        kernel,
        out_shape=outs,
        in_specs=[smem] * scalars + [vmem] * (len(args) - scalars),
        out_specs=[vmem] * len(outs),
        scratch_shapes=list(scratch),
        compiler_params=pltpu.CompilerParams(vmem_limit_bytes=48 * 1024 * 1024),
        cost_estimate=pl.CostEstimate(flops=flops, bytes_accessed=size, transcendentals=0),
        name=name,
    )(*args)


def sds(shape, dtype):
    return jax.ShapeDtypeStruct(shape, dtype)


def normed(values):
    center = values - jnp.mean(values, axis=-1, keepdims=True)
    spread = jnp.mean(center * center, axis=-1, keepdims=True)
    rstd = lax.rsqrt(spread + 1e-05)
    return center * rstd, rstd


def norm_back(d, xhat, rstd, gain):
    dg = d * gain
    first = jnp.mean(dg, axis=-1, keepdims=True)
    second = jnp.mean(dg * xhat, axis=-1, keepdims=True)
    return rstd * (dg - first - xhat * second)


def col_sum(values):
    return jnp.sum(values, axis=0, keepdims=True)


def half_mask(rows, half):
    lane = lax.broadcasted_iota(jnp.int32, (rows, PAIR), 1)
    return (lane >= HEAD_DIM) if half else (lane < HEAD_DIM)


def place_rows(me, full_ref, parts):
    for k, part in enumerate(parts):
        rows = part.shape[0]
        at = pl.multiple_of((me ^ k) * rows, rows)
        full_ref[pl.ds(at, rows), :] = part


def attend_kernel(
    ids, x0, x1, x2, x3, w0, w1, w2, w3a, w3b, gains, biases,
    w_ref, xhat_ref, q_ref, k_ref, v_ref, lse_ref, mixed_ref,
):
    me = ids[0]
    rows = x0.shape[0]
    third = jnp.concatenate([w3a[...], w3b[...]], axis=0)
    place_rows(me, w_ref, [w0[...], w1[...], w2[...], third])
    gain, shift = gains[0:1, :], biases[0:1, :]
    for r, x in enumerate((x0, x1, x2, x3)):
        xhat, unused = normed(x[...].astype(F32))
        xhat_ref[r * rows : (r + 1) * rows, :] = xhat.astype(BF)
        a = (xhat * gain + shift).astype(BF)
        if r == 0:
            q = (dot(a, w_ref[:, :D]) + biases[1:2, :]).astype(BF)
            q_ref[...] = (q.astype(F32) * (HEAD_DIM ** (-0.5))).astype(BF)
        k_ref[r * rows : (r + 1) * rows, :] = dot(a, w_ref[:, D : 2 * D]).astype(BF)
        v_ref[r * rows : (r + 1) * rows, :] = (
            dot(a, w_ref[:, 2 * D :]) + biases[2:3, :]
        ).astype(BF)
    mixed_t = []
    for pair in range(HEADS // 2):
        cols = slice(pair * PAIR, (pair + 1) * PAIR)
        k_pair = k_ref[:, cols]
        v_t = v_ref[:, cols].T
        q_pair = q_ref[:, cols].astype(F32)
        for half in range(2):
            head = 2 * pair + half
            qm = jnp.where(half_mask(rows, half), q_pair, 0.0).astype(BF)
            s = dot(k_pair, qm, NT)
            top = jnp.max(s, axis=0, keepdims=True)
            e = jnp.exp(s - top)
            total = jnp.sum(e, axis=0, keepdims=True)
            lse_ref[head : head + 1, :] = top + jnp.log(total)
            o = dot(v_t[half * HEAD_DIM : (half + 1) * HEAD_DIM, :], e.astype(BF))
            mixed_t.append(o * (1.0 / total))
    mixed_ref[...] = jnp.concatenate(mixed_t, axis=0).T.astype(BF)


def mlp_kernel(
    ids, mask, x0, mixed, g0, g1, g2, g3a, g3b, gains, biases, up_b,
    out_ref, resid_ref, z_ref, slope_ref, wo_ref, w1_ref, w2_ref,
):
    me = ids[0]
    third = jnp.concatenate([g3a[...], g3b[...]], axis=0)
    for k, part in enumerate((g0[...], g1[...], g2[...], third)):
        rows = part.shape[0]
        at = pl.multiple_of((me ^ k) * rows, rows)
        wo_ref[pl.ds(at, rows), :] = part[:, :D]
        w1_ref[pl.ds(at, rows), :] = part[:, D : D + FF]
        for j in range(4):
            down = pl.multiple_of((me ^ k) * (4 * rows) + j * rows, rows)
            w2_ref[pl.ds(down, rows), :] = part[:, D + FF + j * D : D + FF + (j + 1) * D]
    resid = x0[...].astype(F32) + (dot(mixed[...], wo_ref[...]) + biases[3:4, :])
    resid_ref[...] = resid
    xhat, unused = normed(resid)
    c = (xhat * gains[1:2, :] + biases[4:5, :]).astype(BF)
    upper = dot(c, w1_ref[...]) + up_b[...]
    phi = 0.5 * (1.0 + lax.erf(upper * (2.0 ** -0.5)))
    z = (upper * phi).astype(BF)
    z_ref[...] = z
    bell = jnp.exp(-0.5 * upper * upper) * 0.3989422804014327
    slope_ref[...] = (phi + upper * bell).astype(BF)
    out = resid + (dot(z, w2_ref[...]) + biases[5:6, :])
    out_ref[...] = (out * mask[0]).astype(BF)


def mlp_back_kernel(
    gout, z, slope, resid, mixed, wo, w1, w2, gains, biases,
    dresid_ref, ga_ref, du_ref, c_ref, dmixed_ref, vec_ref, upvec_ref,
):
    gm = gout[...]
    dz = dot(gm, w2[...], NT)
    du = (dz * slope[...].astype(F32)).astype(BF)
    du_ref[...] = du
    dc = dot(du, w1[...], NT)
    xhat, rstd = normed(resid[...])
    gain = gains[1:2, :]
    c_ref[...] = (xhat * gain + biases[4:5, :]).astype(BF)
    g_full = gm.astype(F32)
    dresid = g_full + norm_back(dc, xhat, rstd, gain)
    dresid_ref[...] = dresid
    ga = dresid.astype(BF)
    ga_ref[...] = ga
    dmixed_ref[...] = dot(ga, wo[...], NT).astype(BF)
    vec_ref[...] = jnp.concatenate(
        [
            col_sum(dc * xhat),
            col_sum(dc),
            col_sum(ga.astype(F32)),
            col_sum(g_full),
            jnp.zeros((4, D), F32),
        ],
        axis=0,
    )
    upvec_ref[...] = col_sum(du.astype(F32))


def attend_back_kernel(
    q_ref, k_ref, v_ref, lse, mixed, dmixed, xhat_ref, w_ref,
    da0_ref, da1_ref, da2_ref, da3_ref, dq_ref, dkv_ref, vec_ref,
):
    rows = q_ref.shape[0]
    prod = mixed[...].astype(F32) * dmixed[...].astype(F32)
    prod_t = prod.T
    dq_t = []
    for pair in range(HEADS // 2):
        cols = slice(pair * PAIR, (pair + 1) * PAIR)
        k_pair, v_pair = k_ref[:, cols], v_ref[:, cols]
        k_t = k_pair.T
        q_pair = q_ref[:, cols].astype(F32)
        do_pair = dmixed[:, cols].astype(F32)
        ps, dss, qms, doms = [], [], [], []
        for half in range(2):
            head = 2 * pair + half
            keep = half_mask(rows, half)
            qm = jnp.where(keep, q_pair, 0.0).astype(BF)
            dom = jnp.where(keep, do_pair, 0.0).astype(BF)
            p = jnp.exp(dot(k_pair, qm, NT) - lse[head : head + 1, :])
            dp = dot(v_pair, dom, NT)
            delta = col_sum(prod_t[head * HEAD_DIM : (head + 1) * HEAD_DIM, :])
            ds = (p * (dp - delta)).astype(BF)
            dq_t.append(
                dot(k_t[half * HEAD_DIM : (half + 1) * HEAD_DIM, :], ds) * (HEAD_DIM ** (-0.5))
            )
            ps.append(p.astype(BF))
            dss.append(ds)
            qms.append(qm)
            doms.append(dom)
        dkv_ref[:, cols] = dot(
            jnp.concatenate(dss, axis=1), jnp.concatenate(qms, axis=0)
        ).astype(BF)
        dkv_ref[:, D + pair * PAIR : D + (pair + 1) * PAIR] = dot(
            jnp.concatenate(ps, axis=1), jnp.concatenate(doms, axis=0)
        ).astype(BF)
    dq = jnp.concatenate(dq_t, axis=0).T.astype(BF)
    dq_ref[...] = dq
    gain_sum = jnp.zeros((1, D), F32)
    shift_sum = jnp.zeros((1, D), F32)
    for r, da_ref in enumerate((da0_ref, da1_ref, da2_ref, da3_ref)):
        at = slice(r * rows, (r + 1) * rows)
        da = dot(dkv_ref[at, :], w_ref[:, D:], NT)
        if r == 0:
            da = da + dot(dq, w_ref[:, :D], NT)
        gain_sum = gain_sum + col_sum(da * xhat_ref[at, :].astype(F32))
        shift_sum = shift_sum + col_sum(da)
        da_ref[...] = da.astype(da_ref.dtype)
    vec_ref[...] = jnp.concatenate(
        [
            gain_sum,
            shift_sum,
            col_sum(dq.astype(F32)),
            col_sum(dkv_ref[:, D:].astype(F32)),
            jnp.zeros((4, D), F32),
        ],
        axis=0,
    )


def norm_back_kernel(da0, da1, da2, da3, x0, dresid, gains, out_ref):
    da = da0[...] + da1[...].astype(F32) + da2[...].astype(F32) + da3[...].astype(F32)
    xhat, rstd = normed(x0[...].astype(F32))
    out_ref[...] = (dresid[...] + norm_back(da, xhat, rstd, gains[0:1, :])).astype(BF)


def regroup(grad, s, replicas):
    rows = grad.shape[0] // (replicas * SHARDS)
    pieces = []
    for r in range(replicas):
        start = (r * SHARDS + s) * rows
        pieces.append(grad[start : start + rows, :])
    return pieces


def store_halves(ids, replicas, grad, keep_ref, send_ref, base):
    me, section = ids[0], ids[1]
    first = section == 0
    left, right = grad[:, :HALF], grad[:, HALF:]
    own = jnp.where(first, left, right)
    other = jnp.where(first, right, left)
    for s in range(SHARDS):
        for half, ref in ((own, keep_ref), (other, send_ref)):
            block = jnp.concatenate(regroup(half, s, replicas), axis=0)
            ref[me ^ s, base : base + block.shape[0], :] = block.astype(BF)


def mlp_grad_kernel(replicas, ids, c, du, z, gm, keep_ref, send_ref):
    me, section = ids[0], ids[1]
    first = section == 0
    store_halves(ids, replicas, dot(c[...], du[...], TN), keep_ref, send_ref, 0)
    grad = dot(z[...], gm[...], TN)
    rows = FF // (replicas * SHARDS)
    sub = rows // 4
    base = D // SHARDS
    for s in range(SHARDS):
        sides = ([], [])
        for r in range(replicas):
            start = (r * SHARDS + s) * rows
            parts = [grad[start + j * sub : start + (j + 1) * sub, :] for j in range(4)]
            sides[0].append(jnp.concatenate(parts[:2], axis=1))
            sides[1].append(jnp.concatenate(parts[2:], axis=1))
        low, high = (jnp.concatenate(side, axis=0) for side in sides)
        keep_ref[me ^ s, base : 2 * base, :] = jnp.where(first, low, high).astype(BF)
        send_ref[me ^ s, base : 2 * base, :] = jnp.where(first, high, low).astype(BF)


def attend_grad_kernel(
    replicas, ids, xhat, dq, dkv, mixed, ga, gains, biases, vec_one, vec_two, upvec,
    keep_ref, send_ref,
):
    me = ids[0]
    rows = dq.shape[0]
    a = (xhat[...].astype(F32) * gains[0:1, :] + biases[0:1, :]).astype(BF)
    grad = jnp.concatenate(
        [
            dot(a[:rows, :], dq[...], TN),
            dot(a, dkv[...], TN),
            dot(mixed[...], ga[...], TN),
        ],
        axis=1,
    )
    store_halves(ids, replicas, grad, keep_ref, send_ref, 0)
    one, two, up = vec_one[...], vec_two[...], upvec[...]

    def wide(left, right):
        return jnp.concatenate([left, right], axis=1)

    vec = jnp.concatenate(
        [
            wide(one[0:1], two[0:1]),
            wide(one[1:2], one[2:3]),
            wide(one[3:4], two[2:3]),
            wide(two[1:2], two[3:4]),
            up[:, :HALF],
            up[:, HALF:],
            jnp.zeros((VEC_ROWS - 6, HALF), F32),
        ],
        axis=0,
    ).astype(BF)
    base = D // SHARDS
    for s in range(SHARDS):
        keep_ref[s, base : base + VEC_ROWS, :] = vec
        send_ref[s, base : base + VEC_ROWS, :] = vec


def shard_spread(block):
    near = xor_pass(block, "shard", 1)
    far = xor_pass(block, "shard", 2)
    cut = block.shape[0] // 2
    return (
        block,
        near,
        far,
        xor_pass(near[:cut], "shard", 2),
        xor_pass(far[cut:], "shard", 1),
    )


def both_layers(parts, first):
    other = [xor_pass(p, "section", 1) for p in parts]
    layers = []
    for layer in range(2):
        mine = first if layer == 0 else jnp.logical_not(first)
        layers.append([jnp.where(mine, p, q) for p, q in zip(parts, other)])
    return layers


def reduce_grads(keep, send, fixed):
    size = lax.axis_size("replica")
    me = lax.axis_index("replica")
    got = xor_pass(send, "section", 1)
    groups = (keep.shape[1] - fixed) // (D // SHARDS)
    rows = D // SHARDS // size
    total = keep.astype(F32) + got.astype(F32)
    parts = [total[0]]
    for k in range(1, SHARDS):
        parts.append(xor_pass(total[k].astype(BF), "shard", k).astype(F32))
    summed = parts[0] + parts[1] + parts[2] + parts[3]
    blocks = summed[: groups * size * rows].reshape(groups, size, rows, HALF)
    blocks = blocks.transpose(1, 0, 2, 3).reshape(size, groups * rows, HALF)
    tail = summed[groups * size * rows :]
    if size > SHARDS:
        mine = lax.psum_scatter(blocks.astype(BF), "replica", scatter_dimension=0, tiled=False)
        fixed_sum = lax.psum(tail, "replica") if fixed else tail
        return mine.astype(F32), fixed_sum
    out = lax.dynamic_index_in_dim(blocks, me, 0, keepdims=False)
    out_tail = tail
    for k in range(1, size):
        piece = lax.dynamic_index_in_dim(blocks, me ^ k, 0, keepdims=False)
        message = jnp.concatenate([piece, tail], axis=0).astype(BF)
        back = xor_pass(message, "replica", k).astype(F32)
        out = out + back[: groups * rows]
        out_tail = out_tail + back[groups * rows :]
    return out, out_tail


def local(
    inputs,
    cotangent,
    clip_present,
    qkv_weight,
    out_weight,
    up_weight,
    down_weight,
    norm_gains,
    biases,
    up_bias,
):
    section = lax.axis_index("section")
    shard = lax.axis_index("shard")
    replica = lax.axis_index("replica")
    replicas = lax.axis_size("replica")
    first = section == 0
    rows = inputs.shape[2]
    ids = jnp.stack([shard, section]).astype(jnp.int32)
    own_rows = D // SHARDS

    def mine(pair):
        return lax.dynamic_index_in_dim(pair, section, 0, keepdims=False)

    x_first = mine(inputs[0])
    mask = mine(clip_present[0]).astype(F32).reshape(1)
    gout_last = (mine(cotangent[0]).astype(F32) * mask[0]).astype(BF)
    frames = [x_first] + [xor_pass(x_first, "shard", k) for k in (1, 2, 3)]

    qkv_parts = both_layers(shard_spread(qkv_weight[0]), first)
    down = down_weight[0].reshape(4, own_rows, D)
    rest = jnp.concatenate(
        [out_weight[0], up_weight[0]] + [down[j] for j in range(4)], axis=1
    )
    rest_parts = both_layers(shard_spread(rest), first)
    small = [norm_gains[0], biases[0], up_bias[0][None]]
    small_layers = both_layers(small, first)

    whole = SHARDS * rows
    saved = []
    outs = []
    for layer in range(2):
        gains, shifts, up_b = small_layers[layer]
        w_qkv, xhat, q, k, v, lse, mixed = call(
            attend_kernel,
            [
                sds((D, 3 * D), BF),
                sds((whole, D), BF),
                sds((rows, D), BF),
                sds((whole, D), BF),
                sds((whole, D), BF),
                sds((8, rows), F32),
                sds((rows, D), BF),
            ],
            [ids, *frames, *qkv_parts[layer], gains, shifts],
            "attend",
            4_000_000_000,
        )
        out, resid, z, slope, w_out, w_up, w_down = call(
            mlp_kernel,
            [
                sds((rows, D), BF),
                sds((rows, D), F32),
                sds((rows, FF), BF),
                sds((rows, FF), BF),
                sds((D, D), BF),
                sds((D, FF), BF),
                sds((FF, D), BF),
            ],
            [ids, mask, frames[0], mixed, *rest_parts[layer], gains, shifts, up_b],
            "mlp",
            2_000_000_000,
            scalars=2,
        )
        saved.append(
            (frames[0], w_qkv, xhat, q, k, v, lse, mixed, resid, z, slope, w_out, w_up, w_down)
        )
        outs.append(out)
        if layer == 0:
            frames = [out] + [xor_pass(out, "shard", k) for k in (1, 2, 3)]

    gout = gout_last
    shares = [None, None]
    grads = [None, None]
    for layer in (1, 0):
        gains, shifts, up_b = small_layers[layer]
        x0, w_qkv, xhat, q, k, v, lse, mixed, resid, z, slope, w_out, w_up, w_down = saved[layer]
        dresid, ga, du, c, dmixed, vec_two, upvec = call(
            mlp_back_kernel,
            [
                sds((rows, D), F32),
                sds((rows, D), BF),
                sds((rows, FF), BF),
                sds((rows, D), BF),
                sds((rows, D), BF),
                sds((8, D), F32),
                sds((1, FF), F32),
            ],
            [gout, z, slope, resid, mixed, w_out, w_up, w_down, gains, shifts],
            "mlp_back",
            2_000_000_000,
            scalars=0,
        )
        da0, da1, da2, da3, dq, dkv, vec_one = call(
            attend_back_kernel,
            [
                sds((rows, D), F32),
                sds((rows, D), BF),
                sds((rows, D), BF),
                sds((rows, D), BF),
                sds((rows, D), BF),
                sds((whole, 2 * D), BF),
                sds((8, D), F32),
            ],
            [q, k, v, lse, mixed, dmixed, xhat, w_qkv],
            "attend_back",
            8_000_000_000,
            scalars=0,
        )
        back = [xor_pass(part, "shard", j) for j, part in ((1, da1), (2, da2), (3, da3))]
        pair = sds((SHARDS, 2 * own_rows, HALF), BF)
        keep_one, send_one = call(
            functools.partial(mlp_grad_kernel, replicas),
            [pair, pair],
            [ids, c, du, z, gout],
            "mlp_grad",
            2_000_000_000,
        )
        pair = sds((SHARDS, own_rows + VEC_ROWS, HALF), BF)
        keep_two, send_two = call(
            functools.partial(attend_grad_kernel, replicas),
            [pair, pair],
            [ids, xhat, dq, dkv, mixed, ga, gains, shifts, vec_one, vec_two, upvec],
            "attend_grad",
            2_000_000_000,
        )
        (gin,) = call(
            norm_back_kernel,
            [sds((rows, D), BF)],
            [da0, *back, x0, dresid, gains],
            "norm_back",
            100_000_000,
            scalars=0,
        )
        grads[layer] = gin
        gout = gin
        one, unused = reduce_grads(keep_one, send_one, 0)
        two, vec = reduce_grads(keep_two, send_two, VEC_ROWS)
        shares[layer] = (jnp.concatenate([one, two], axis=0), vec)

    def swapped(pair):
        own = jnp.where(first, pair[0], pair[1])
        other = xor_pass(jnp.where(first, pair[1], pair[0]), "section", 1)
        return jnp.stack([jnp.where(first, own, other), jnp.where(first, other, own)])

    outputs_local = swapped(outs)
    grads_local = swapped(grads)
    halves = swapped([shares[0][0], shares[1][0]])
    vec = jnp.where(first, shares[0][1], shares[1][1])
    n = D // (SHARDS * replicas)
    up_grad = jnp.concatenate([halves[0, :n], halves[1, :n]], axis=1)
    down_grad = halves[:, n : 2 * n].reshape(2, n, 2, D).transpose(0, 2, 1, 3).reshape(4 * n, D)
    attn = jnp.concatenate([halves[0, 2 * n :], halves[1, 2 * n :]], axis=1)
    place = replica * SHARDS + shard
    rows_of = vec[:4].reshape(8, D)
    rows_own = lax.dynamic_slice_in_dim(rows_of, place * n, n, axis=1)
    gain_own = rows_own[:2]
    bias_own = jnp.stack(
        [rows_own[2], rows_own[3], rows_own[4], rows_own[5], rows_own[6], rows_own[7]]
    )
    up_own = lax.dynamic_slice_in_dim(vec[4:6].reshape(FF), place * 4 * n, 4 * n, axis=0)
    return (
        outputs_local[None, None],
        grads_local[None, None],
        attn[None, :, : 3 * D],
        attn[None, :, 3 * D :],
        up_grad[None],
        down_grad[None],
        gain_own[None],
        bias_own[None],
        up_own[None],
    )


def solution(mesh):
    return jax.shard_map(
        local,
        mesh=mesh,
        in_specs=(
            P("replica", None, "shard", None),
            P("replica", None, "shard", None),
            P("replica", None),
            P("section", "shard", None),
            P("section", "shard", None),
            P("section", "shard", None),
            P("section", "shard", None),
            P("section", None, None),
            P("section", None, None),
            P("section", None),
        ),
        out_specs=(
            P("section", "replica", None, "shard", None),
            P("section", "replica", None, "shard", None),
            P("section", ("replica", "shard"), None),
            P("section", ("replica", "shard"), None),
            P("section", ("replica", "shard"), None),
            P("section", ("replica", "shard"), None),
            P("section", None, ("replica", "shard")),
            P("section", None, ("replica", "shard")),
            P("section", ("replica", "shard")),
        ),
        check_vma=False,
    )
```

```python
import functools

import jax
import jax.numpy as jnp
from jax import lax
from jax.experimental import pallas as pl
from jax.experimental.pallas import tpu as pltpu
from jax.sharding import PartitionSpec as P

D = 384
HEADS = 6
HEAD_DIM = 64
FF = 1536
PAIR = 2 * HEAD_DIM
HALF = 768
SHARDS = 4
BF = jnp.bfloat16
F32 = jnp.float32
VEC_ROWS = 16
COST = 1000

NT = (((1,), (1,)), ((), ()))
TN = (((0,), (0,)), ((), ()))


def dot(left, right, dims=(((1,), (0,)), ((), ()))):
    return lax.dot_general(left, right, dims, preferred_element_type=F32)


def xor_pass(x, axis, by):
    pairs = [(i, i ^ by) for i in range(lax.axis_size(axis))]
    return lax.ppermute(x, axis, pairs)


def call(kernel, outs, args, name, flops, scalars=1, ties=(), raw=0, scratch=()):
    smem = pl.BlockSpec(memory_space=pltpu.SMEM)
    vmem = pl.BlockSpec(memory_space=pltpu.VMEM)
    apart = pl.BlockSpec(memory_space=pl.ANY)
    size = sum(a.size * a.dtype.itemsize for a in args)
    size += sum(o.size * o.dtype.itemsize for o in outs)
    count = len(args)

    def body(*refs):
        kernel(*refs[:count], *refs[count + len(ties) :])

    return pl.pallas_call(
        body,
        out_shape=outs,
        in_specs=[smem] * scalars
        + [vmem] * (count - scalars - raw)
        + [apart] * (raw + len(ties)),
        out_specs=[vmem] * len(outs),
        scratch_shapes=list(scratch),
        compiler_params=pltpu.CompilerParams(vmem_limit_bytes=20 * 1024 * 1024),
        cost_estimate=pl.CostEstimate(
            flops=flops // COST, bytes_accessed=size // COST, transcendentals=0
        ),
        name=name,
    )(*args, *ties)


def after(x, *ties):
    apart = pl.BlockSpec(memory_space=pl.ANY)
    return pl.pallas_call(
        lambda *refs: None,
        out_shape=jax.ShapeDtypeStruct(x.shape, x.dtype),
        in_specs=[apart] * (1 + len(ties)),
        out_specs=apart,
        input_output_aliases={0: 0},
        compiler_params=pltpu.CompilerParams(vmem_limit_bytes=1024 * 1024),
        name="after",
    )(x, *ties)


def sds(shape, dtype):
    return jax.ShapeDtypeStruct(shape, dtype)


def normed(values):
    center = values - jnp.mean(values, axis=-1, keepdims=True)
    spread = jnp.mean(center * center, axis=-1, keepdims=True)
    rstd = lax.rsqrt(spread + 1e-05)
    return center * rstd, rstd


def norm_back(d, xhat, rstd, gain):
    dg = d * gain
    first = jnp.mean(dg, axis=-1, keepdims=True)
    second = jnp.mean(dg * xhat, axis=-1, keepdims=True)
    return rstd * (dg - first - xhat * second)


def col_sum(values):
    return jnp.sum(values, axis=0, keepdims=True)


def half_mask(rows, half):
    lane = lax.broadcasted_iota(jnp.int32, (rows, PAIR), 1)
    return (lane >= HEAD_DIM) if half else (lane < HEAD_DIM)


def place_rows(ids, full_ref, parts, first_col):
    me, section = ids[0], ids[1]
    width = full_ref.shape[1]
    for side in range(2):
        half = section ^ side
        for k, part in enumerate(parts[side]):
            rows = part.shape[0]
            at = pl.multiple_of(((me ^ k) * 2 + half) * rows, rows)
            full_ref[pl.ds(at, rows), :] = part[:, first_col : first_col + width]


def pack_kernel(ids, out, up, down, stay_ref, swap_ref, sems):
    section = ids[1]
    rows = out.shape[0] // 2
    copies = []

    def move(source, target):
        copy = pltpu.make_async_copy(source, target, sems.at[len(copies)])
        copy.start()
        copies.append(copy)

    for half, ref in ((1 - section, swap_ref), (section, stay_ref)):
        at = pl.ds(pl.multiple_of(half * rows, rows), rows)
        move(out.at[at, :], ref.at[:, :D])
        move(up.at[at, :], ref.at[:, D : D + FF])
        for j in range(4):
            at = pl.ds(pl.multiple_of(half * (4 * rows) + j * rows, rows), rows)
            move(down.at[at, :], ref.at[:, D + FF + j * D : D + FF + (j + 1) * D])
    for copy in copies:
        copy.wait()


def small_kernel(gains, biases, up_b, small_ref):
    bias = up_b[...]
    small_ref[...] = jnp.concatenate(
        [gains[...], biases[...]]
        + [bias[:, j * D : (j + 1) * D] for j in range(4)]
        + [jnp.zeros((4, D), F32)],
        axis=0,
    )


def pick_kernel(ids, stay, got, zero_ref, one_ref):
    first = ids[1] == 0
    here, there = stay[...], got[...]
    zero_ref[...] = jnp.where(first, here, there)
    one_ref[...] = jnp.where(first, there, here)


def finish_kernel(ids, fin_zero, fin_one, got, vec_zero, vec_one, qkv, out, up, down, vec, up_vec):
    first = ids[1] == 0
    own = jnp.where(first, fin_zero[...], fin_one[...])
    other = got[...]
    low, high = jnp.where(first, own, other), jnp.where(first, other, own)
    n = low.shape[0] // 3
    up[:, :HALF] = low[:n]
    up[:, HALF:] = high[:n]
    for t, side in enumerate((low, high)):
        for j in range(2):
            at = (2 * t + j) * n
            down[at : at + n, :] = side[n : 2 * n, j * D : (j + 1) * D]
    qkv[:, :HALF] = low[2 * n :]
    qkv[:, HALF:] = high[2 * n :, :D]
    out[...] = high[2 * n :, D:]
    sums = jnp.where(first, vec_zero[...], vec_one[...])

    def taken(values, width):
        length = values.shape[1]
        source = lax.broadcasted_iota(jnp.int32, (length, width), 0)
        target = lax.broadcasted_iota(jnp.int32, (length, width), 1) + ids[2] * width
        spots = jnp.where(source == target, 1.0, 0.0)
        return lax.dot_general(
            values, spots, (((1,), (0,)), ((), ())),
            preferred_element_type=F32, precision=lax.Precision.HIGHEST,
        )

    rows = []
    for r in range(4):
        rows += [sums[r : r + 1, :D], sums[r : r + 1, D:]]
    vec[...] = taken(jnp.concatenate(rows, axis=0), n)
    both = jnp.concatenate([sums[4:5], sums[5:6]], axis=1)
    up_vec[...] = taken(jnp.broadcast_to(both, (8, FF)), 4 * n)


def attend_kernel(
    layer, ids, x0, x1, x2, x3, w0, w1, w2, w3, o0, o1, o2, o3, small,
    w_ref, xhat_ref, q_ref, k_ref, v_ref, lse_ref, mixed_ref,
):
    me = ids[0]
    rows = x0.shape[0]
    own_layer = ids[1] == layer
    for k, (own, other) in enumerate(((w0, o0), (w1, o1), (w2, o2), (w3, o3))):
        count = own.shape[0]
        at = pl.multiple_of((me ^ k) * count, count)
        w_ref[pl.ds(at, count), :] = jnp.where(own_layer, own[...], other[...])
    gains, biases = small[0:2, :], small[2:8, :]
    gain, shift = gains[0:1, :], biases[0:1, :]
    for r, x in enumerate((x0, x1, x2, x3)):
        xhat, unused = normed(x[...].astype(F32))
        xhat_ref[r * rows : (r + 1) * rows, :] = xhat.astype(BF)
        a = (xhat * gain + shift).astype(BF)
        if r == 0:
            q = (dot(a, w_ref[:, :D]) + biases[1:2, :]).astype(BF)
            q_ref[...] = (q.astype(F32) * (HEAD_DIM ** (-0.5))).astype(BF)
        k_ref[r * rows : (r + 1) * rows, :] = dot(a, w_ref[:, D : 2 * D]).astype(BF)
        v_ref[r * rows : (r + 1) * rows, :] = (
            dot(a, w_ref[:, 2 * D :]) + biases[2:3, :]
        ).astype(BF)
    mixed_t = []
    for pair in range(HEADS // 2):
        cols = slice(pair * PAIR, (pair + 1) * PAIR)
        k_pair = k_ref[:, cols]
        v_t = v_ref[:, cols].T
        q_pair = q_ref[:, cols].astype(F32)
        for half in range(2):
            head = 2 * pair + half
            qm = jnp.where(half_mask(rows, half), q_pair, 0.0).astype(BF)
            s = dot(k_pair, qm, NT)
            top = jnp.max(s, axis=0, keepdims=True)
            e = jnp.exp(s - top)
            total = jnp.sum(e, axis=0, keepdims=True)
            lse_ref[head : head + 1, :] = top + jnp.log(total)
            o = dot(v_t[half * HEAD_DIM : (half + 1) * HEAD_DIM, :], e.astype(BF))
            mixed_t.append(o * (1.0 / total))
    mixed_ref[...] = jnp.concatenate(mixed_t, axis=0).T.astype(BF)


def mlp_kernel(
    ids, mask, x0, mixed, w0, w1, w2, w3, o0, o1, o2, o3, small,
    out_ref, resid_ref, z_ref, slope_ref, wo_ref, w1_ref, w2_ref,
):
    parts = ((w0, w1, w2, w3), (o0, o1, o2, o3))
    place_rows(ids, wo_ref, parts, 0)
    place_rows(ids, w1_ref, parts, D)
    me, section = ids[0], ids[1]
    for side in range(2):
        half = section ^ side
        for k, part in enumerate(parts[side]):
            rows = part.shape[0]
            for j in range(4):
                at = (((me ^ k) * 2 + half) * 4 + j) * rows
                left = D + FF + j * D
                w2_ref[pl.ds(pl.multiple_of(at, rows), rows), :] = part[:, left : left + D]
    gains, biases = small[0:2, :], small[2:8, :]
    up_b = jnp.concatenate([small[8 + j : 9 + j, :] for j in range(4)], axis=1)
    resid = x0[...].astype(F32) + (dot(mixed[...], wo_ref[...]) + biases[3:4, :])
    resid_ref[...] = resid
    xhat, unused = normed(resid)
    c = (xhat * gains[1:2, :] + biases[4:5, :]).astype(BF)
    upper = dot(c, w1_ref[...]) + up_b
    phi = 0.5 * (1.0 + lax.erf(upper * (2.0 ** -0.5)))
    z = (upper * phi).astype(BF)
    z_ref[...] = z
    bell = jnp.exp(-0.5 * upper * upper) * 0.3989422804014327
    slope_ref[...] = (phi + upper * bell).astype(BF)
    out = resid + (dot(z, w2_ref[...]) + biases[5:6, :])
    out_ref[...] = (out * mask[0]).astype(BF)


def mlp_back_kernel(
    gout, z, slope, resid, wo, w1, w2, small,
    dresid_ref, ga_ref, du_ref, c_ref, dmixed_ref, vec_ref, upvec_ref,
):
    gains, biases = small[0:2, :], small[2:8, :]
    gm = gout[...]
    dz = dot(gm, w2[...], NT)
    du = (dz * slope[...].astype(F32)).astype(BF)
    du_ref[...] = du
    dc = dot(du, w1[...], NT)
    xhat, rstd = normed(resid[...])
    gain = gains[1:2, :]
    c_ref[...] = (xhat * gain + biases[4:5, :]).astype(BF)
    g_full = gm.astype(F32)
    dresid = g_full + norm_back(dc, xhat, rstd, gain)
    dresid_ref[...] = dresid
    ga = dresid.astype(BF)
    ga_ref[...] = ga
    dmixed_ref[...] = dot(ga, wo[...], NT).astype(BF)
    vec_ref[...] = jnp.concatenate(
        [
            col_sum(dc * xhat),
            col_sum(dc),
            col_sum(ga.astype(F32)),
            col_sum(g_full),
            jnp.zeros((4, D), F32),
        ],
        axis=0,
    )
    upvec_ref[...] = col_sum(du.astype(F32))


def attend_back_kernel(
    q_ref, k_ref, v_ref, lse, mixed, dmixed, xhat_ref, w_ref,
    own_ref, near_ref, swap_ref, dq_ref, dkv_ref, vec_ref,
):
    rows = q_ref.shape[0]
    prod = mixed[...].astype(F32) * dmixed[...].astype(F32)
    prod_t = prod.T
    dq_t = []
    for pair in range(HEADS // 2):
        cols = slice(pair * PAIR, (pair + 1) * PAIR)
        k_pair, v_pair = k_ref[:, cols], v_ref[:, cols]
        k_t = k_pair.T
        q_pair = q_ref[:, cols].astype(F32)
        do_pair = dmixed[:, cols].astype(F32)
        ps, dss, qms, doms = [], [], [], []
        for half in range(2):
            head = 2 * pair + half
            keep = half_mask(rows, half)
            qm = jnp.where(keep, q_pair, 0.0).astype(BF)
            dom = jnp.where(keep, do_pair, 0.0).astype(BF)
            p = jnp.exp(dot(k_pair, qm, NT) - lse[head : head + 1, :])
            dp = dot(v_pair, dom, NT)
            delta = col_sum(prod_t[head * HEAD_DIM : (head + 1) * HEAD_DIM, :])
            ds = (p * (dp - delta)).astype(BF)
            dq_t.append(
                dot(k_t[half * HEAD_DIM : (half + 1) * HEAD_DIM, :], ds) * (HEAD_DIM ** (-0.5))
            )
            ps.append(p.astype(BF))
            dss.append(ds)
            qms.append(qm)
            doms.append(dom)
        dkv_ref[:, cols] = dot(
            jnp.concatenate(dss, axis=1), jnp.concatenate(qms, axis=0)
        ).astype(BF)
        dkv_ref[:, D + pair * PAIR : D + (pair + 1) * PAIR] = dot(
            jnp.concatenate(ps, axis=1), jnp.concatenate(doms, axis=0)
        ).astype(BF)
    dq = jnp.concatenate(dq_t, axis=0).T.astype(BF)
    dq_ref[...] = dq
    gain_sum = jnp.zeros((1, D), F32)
    shift_sum = jnp.zeros((1, D), F32)
    outs = (own_ref, swap_ref.at[0], near_ref, swap_ref.at[1])
    for r, da_ref in enumerate(outs):
        at = slice(r * rows, (r + 1) * rows)
        da = dot(dkv_ref[at, :], w_ref[:, D:], NT)
        if r == 0:
            da = da + dot(dq, w_ref[:, :D], NT)
        gain_sum = gain_sum + col_sum(da * xhat_ref[at, :].astype(F32))
        shift_sum = shift_sum + col_sum(da)
        da_ref[...] = da.astype(da_ref.dtype)
    vec_ref[...] = jnp.concatenate(
        [
            gain_sum,
            shift_sum,
            col_sum(dq.astype(F32)),
            col_sum(dkv_ref[:, D:].astype(F32)),
            jnp.zeros((4, D), F32),
        ],
        axis=0,
    )


def norm_back_kernel(da_own, da_core, da_near, x0, dresid, small, out_ref):
    da = da_own[...] + da_core[0].astype(F32) + da_near[...].astype(F32)
    xhat, rstd = normed(x0[...].astype(F32))
    out_ref[...] = (dresid[...] + norm_back(da, xhat, rstd, small[0:1, :])).astype(BF)


def regroup(grad, s, replicas):
    rows = grad.shape[0] // (replicas * SHARDS)
    pieces = []
    for r in range(replicas):
        start = (r * SHARDS + s) * rows
        pieces.append(grad[start : start + rows, :])
    return pieces


def slot_of(ids, s, side):
    by = ids[0] ^ s
    turned = jnp.where(side == 0, by, ((by & 1) << 1) | (by >> 1))
    return turned ^ (turned >> 1)


def store_halves(ids, replicas, grad, keep_ref, send_ref, base):
    section = ids[1]
    first = section == 0
    left, right = grad[:, :HALF], grad[:, HALF:]
    own = jnp.where(first, left, right)
    other = jnp.where(first, right, left)
    for s in range(SHARDS):
        for half, ref, side in ((own, keep_ref, section), (other, send_ref, 1 - section)):
            block = jnp.concatenate(regroup(half, s, replicas), axis=0)
            ref[slot_of(ids, s, side), base : base + block.shape[0], :] = block.astype(BF)


def grad_kernel(
    replicas, ids, c, du, z, gm, xhat, dq, dkv, mixed, ga, small, vec_one, vec_two, upvec,
    keep_ref, send_ref,
):
    section = ids[1]
    first = section == 0
    store_halves(ids, replicas, dot(c[...], du[...], TN), keep_ref, send_ref, 0)
    grad = dot(z[...], gm[...], TN)
    rows = FF // (replicas * SHARDS)
    sub = rows // 4
    base = D // SHARDS
    for s in range(SHARDS):
        sides = ([], [])
        for r in range(replicas):
            start = (r * SHARDS + s) * rows
            parts = [grad[start + j * sub : start + (j + 1) * sub, :] for j in range(4)]
            sides[0].append(jnp.concatenate(parts[:2], axis=1))
            sides[1].append(jnp.concatenate(parts[2:], axis=1))
        low, high = (jnp.concatenate(side, axis=0) for side in sides)
        keep_ref[slot_of(ids, s, section), base : 2 * base, :] = jnp.where(
            first, low, high
        ).astype(BF)
        send_ref[slot_of(ids, s, 1 - section), base : 2 * base, :] = jnp.where(
            first, high, low
        ).astype(BF)
    rows = dq.shape[0]
    a = (xhat[...].astype(F32) * small[0:1, :] + small[2:3, :]).astype(BF)
    grad = jnp.concatenate(
        [
            dot(a[:rows, :], dq[...], TN),
            dot(a, dkv[...], TN),
            dot(mixed[...], ga[...], TN),
        ],
        axis=1,
    )
    store_halves(ids, replicas, grad, keep_ref, send_ref, 2 * base)
    one, two, up = vec_one[...], vec_two[...], upvec[...]

    def wide(left, right):
        return jnp.concatenate([left, right], axis=1)

    vec = jnp.concatenate(
        [
            wide(one[0:1], two[0:1]),
            wide(one[1:2], one[2:3]),
            wide(one[3:4], two[2:3]),
            wide(two[1:2], two[3:4]),
            up[:, :HALF],
            up[:, HALF:],
            jnp.zeros((VEC_ROWS - 6, HALF), F32),
        ],
        axis=0,
    ).astype(BF)
    for s in range(SHARDS):
        keep_ref[s, 3 * base : 3 * base + VEC_ROWS, :] = vec
        send_ref[s, 3 * base : 3 * base + VEC_ROWS, :] = vec


def shard_spread(block, first, relay):
    near = xor_pass(block, "shard", 1)
    far = xor_pass(block, "shard", 2)
    if relay:
        diagonal = lax.ppermute(
            jnp.where(first, near, far), ("section", "shard"), split_pairs(2, 1)
        )
    else:
        diagonal = xor_pass(block, "shard", 3)
    parts = [block, near, far, diagonal]
    return parts + [xor_pass(p, "section", 1) for p in parts]


def clip_frames(own):
    near = xor_pass(own, "shard", 1)
    return [own, xor_pass(own, "section", 1), near, xor_pass(near, "section", 1)]


def to_clip(pair, first, upper):
    count = lax.axis_size("shard")
    pairs = [((i >> 1) * count + i, (i >> 1) * count + (i ^ 2)) for i in range(count)]
    away = lax.dynamic_index_in_dim(pair, 1 - upper, 0, keepdims=False)
    here = lax.dynamic_index_in_dim(pair, upper, 0, keepdims=False)
    got = lax.ppermute(away, ("section", "shard"), pairs)
    return jnp.where(jnp.where(first, 0, 1) == upper, here, got)


def from_clip(pair, first, upper):
    count = lax.axis_size("shard")

    def pairs(flip):
        out = []
        for sec in range(2):
            for i in range(count):
                clip, low = i >> 1, i & 1
                out.append((sec * count + i, (clip ^ flip) * count + sec * 2 + low))
        return out

    low_clip = upper == 0
    same = lax.ppermute(jnp.where(low_clip, pair[0], pair[1]), ("section", "shard"), pairs(0))
    swap = lax.ppermute(jnp.where(low_clip, pair[1], pair[0]), ("section", "shard"), pairs(1))
    return jnp.stack([jnp.where(first, same, swap), jnp.where(first, swap, same)])


def section_sum(keep, send):
    got = xor_pass(send, "section", 1)
    total = keep.astype(F32) + got.astype(F32)
    return total[0], total[1:3].astype(BF), total[3]


def split_pairs(low, high):
    count = lax.axis_size("shard")
    return [(i, i ^ low) for i in range(count)] + [
        (count + i, count + (i ^ high)) for i in range(count)
    ]


def shard_sum(stays, first_out, second_out):
    both = ("section", "shard")
    got = lax.ppermute(first_out, both, split_pairs(1, 2)).astype(F32)
    message = (second_out + got[1]).astype(BF)
    return stays + got[0] + lax.ppermute(message, both, split_pairs(2, 1)).astype(F32)


def replica_sum(summed, fixed):
    size = lax.axis_size("replica")
    me = lax.axis_index("replica")
    groups = (summed.shape[0] - fixed) // (D // SHARDS)
    rows = D // SHARDS // size
    blocks = summed[: groups * size * rows].reshape(groups, size, rows, HALF)
    tail = summed[groups * size * rows :]
    if size > SHARDS:
        blocks = blocks.transpose(1, 0, 2, 3).reshape(size, groups * rows, HALF)
        mine = lax.psum_scatter(blocks.astype(BF), "replica", scatter_dimension=0, tiled=False)
        return mine.astype(F32), lax.psum(tail, "replica")

    def block_of(index):
        part = lax.dynamic_index_in_dim(blocks, index, 1, keepdims=False)
        return jnp.concatenate([part.reshape(groups * rows, HALF), tail], axis=0)

    out = block_of(me)
    for k in range(1, size):
        out = out + xor_pass(block_of(me ^ k).astype(BF), "replica", k).astype(F32)
    return out[: groups * rows], out[groups * rows :]


def local(
    inputs,
    cotangent,
    clip_present,
    qkv_weight,
    out_weight,
    up_weight,
    down_weight,
    norm_gains,
    biases,
    up_bias,
):
    section = lax.axis_index("section")
    shard = lax.axis_index("shard")
    replica = lax.axis_index("replica")
    replicas = lax.axis_size("replica")
    first = section == 0
    rows = inputs.shape[2]
    place = replica * SHARDS + shard
    ids = jnp.stack([shard, section, place]).astype(jnp.int32)
    own_rows = D // SHARDS

    upper = shard >> 1
    present = lax.dynamic_index_in_dim(clip_present[0], upper, 0, keepdims=False)
    mask = present.astype(F32).reshape(1)
    x_first = to_clip(inputs[0], first, upper)

    half_rows = own_rows // 2
    packed = sds((half_rows, 9 * D), BF)
    stay, swap = call(
        pack_kernel,
        [packed, packed],
        [ids, out_weight[0], up_weight[0], down_weight[0]],
        "pack",
        1_000_000,
        raw=3,
        scratch=[pltpu.SemaphoreType.DMA((12,))],
    )
    got = xor_pass(swap, "section", 1)
    qkv_part = shard_spread(qkv_weight[0], first, False)
    frames = clip_frames(x_first)
    (small,) = call(
        small_kernel,
        [sds((16, D), F32)],
        [norm_gains[0], biases[0], up_bias[0][None]],
        "small",
        1_000_000,
        scalars=0,
        ties=(x_first,),
    )
    other_small = xor_pass(small, "section", 1)
    small_layers = [jnp.where(first, small, other_small), jnp.where(first, other_small, small)]
    rest_zero, rest_one = call(
        pick_kernel, [packed, packed], [ids, stay, got], "pick", 1_000_000,
        ties=(frames[2], qkv_part[1], qkv_part[2]),
    )
    rest_part = shard_spread(rest_zero, first, False)
    gout_last = to_clip(after(cotangent[0], frames[2]), first, upper) * mask.astype(BF)

    whole = SHARDS * rows
    saved = []
    outs = []
    for layer in range(2):
        small = small_layers[layer]
        w_qkv, xhat, q, k, v, lse, mixed = call(
            functools.partial(attend_kernel, layer),
            [
                sds((D, 3 * D), BF),
                sds((whole, D), BF),
                sds((rows, D), BF),
                sds((whole, D), BF),
                sds((whole, D), BF),
                sds((8, rows), F32),
                sds((rows, D), BF),
            ],
            [ids, *frames, *qkv_part, small],
            "attend",
            4_000_000_000,
        )
        if layer == 0:
            next_part = shard_spread(after(rest_one, mixed), first, False)
        out, resid, z, slope, w_out, w_up, w_down = call(
            mlp_kernel,
            [
                sds((rows, D), BF),
                sds((rows, D), F32),
                sds((rows, FF), BF),
                sds((rows, FF), BF),
                sds((D, D), BF),
                sds((D, FF), BF),
                sds((FF, D), BF),
            ],
            [ids, mask, frames[0], mixed, *rest_part, small],
            "mlp",
            2_000_000_000,
            scalars=2,
        )
        saved.append(
            (frames[0], w_qkv, xhat, q, k, v, lse, mixed, resid, z, slope, w_out, w_up, w_down)
        )
        outs.append(out)
        if layer == 0:
            frames = clip_frames(out)
            rest_part = next_part

    gout = gout_last
    shares = [None, None]
    grads = [None, None]
    before, along = (), ()
    for layer in (1, 0):
        small = small_layers[layer]
        x0, w_qkv, xhat, q, k, v, lse, mixed, resid, z, slope, w_out, w_up, w_down = saved[layer]
        dresid, ga, du, c, dmixed, vec_two, upvec = call(
            mlp_back_kernel,
            [
                sds((rows, D), F32),
                sds((rows, D), BF),
                sds((rows, FF), BF),
                sds((rows, D), BF),
                sds((rows, D), BF),
                sds((8, D), F32),
                sds((1, FF), F32),
            ],
            [gout, z, slope, resid, w_out, w_up, w_down, small],
            "mlp_back",
            2_000_000_000,
            scalars=0,
        )
        da_own, da_near, da_swap, dq, dkv, vec_one = call(
            attend_back_kernel,
            [
                sds((rows, D), F32),
                sds((rows, D), F32),
                sds((2, rows, D), BF),
                sds((rows, D), BF),
                sds((whole, 2 * D), BF),
                sds((8, D), F32),
            ],
            [q, k, v, lse, mixed, dmixed, xhat, w_qkv],
            "attend_back",
            8_000_000_000,
            scalars=0,
            ties=before,
        )
        got = xor_pass(da_swap, "section", 1)
        near = (da_near + got[1].astype(F32)).astype(BF)
        back = xor_pass(near, "shard", 1)
        pair = sds((SHARDS, 3 * own_rows + VEC_ROWS, HALF), BF)
        keep, send = call(
            functools.partial(grad_kernel, replicas),
            [pair, pair],
            [ids, c, du, z, gout, xhat, dq, dkv, mixed, ga, small, vec_one, vec_two, upvec],
            "grad",
            4_000_000_000,
            ties=(near,),
        )
        send = after(send, back, *along)
        stays, first_out, second_out = section_sum(keep, send)
        (gin,) = call(
            norm_back_kernel,
            [sds((rows, D), BF)],
            [da_own, got, back, x0, dresid, small],
            "norm_back",
            100_000_000,
            scalars=0,
            ties=along,
        )
        grads[layer] = gin
        gout = gin
        summed = shard_sum(stays, first_out, second_out)
        if layer == 0:
            summed = after(summed, shares[1][0])
        shares[layer] = replica_sum(summed, VEC_ROWS)
        before, along = (first_out,), (summed,)

    outputs_local = from_clip(outs, first, upper)
    grads_local = from_clip(grads, first, upper)
    got = xor_pass(jnp.where(first, shares[1][0], shares[0][0]), "section", 1)
    n = own_rows // replicas
    qkv_grad, out_grad, up_grad, down_grad, vec, up_vec = call(
        finish_kernel,
        [
            sds((n, 3 * D), F32),
            sds((n, D), F32),
            sds((n, FF), F32),
            sds((4 * n, D), F32),
            sds((8, n), F32),
            sds((8, 4 * n), F32),
        ],
        [ids, shares[0][0], shares[1][0], got, shares[0][1], shares[1][1]],
        "finish",
        1_000_000,
    )
    return (
        outputs_local[None, None],
        grads_local[None, None],
        qkv_grad[None],
        out_grad[None],
        up_grad[None],
        down_grad[None],
        vec[None, :2],
        vec[None, 2:],
        up_vec[:1],
    )


def solution(mesh):
    return jax.shard_map(
        local,
        mesh=mesh,
        in_specs=(
            P("replica", None, "shard", None),
            P("replica", None, "shard", None),
            P("replica", None),
            P("section", "shard", None),
            P("section", "shard", None),
            P("section", "shard", None),
            P("section", "shard", None),
            P("section", None, None),
            P("section", None, None),
            P("section", None),
        ),
        out_specs=(
            P("section", "replica", None, "shard", None),
            P("section", "replica", None, "shard", None),
            P("section", ("replica", "shard"), None),
            P("section", ("replica", "shard"), None),
            P("section", ("replica", "shard"), None),
            P("section", ("replica", "shard"), None),
            P("section", None, ("replica", "shard")),
            P("section", None, ("replica", "shard")),
            P("section", ("replica", "shard")),
        ),
        check_vma=False,
    )
```

```python
import functools

import jax
import jax.numpy as jnp
from jax import lax
from jax.experimental import pallas as pl
from jax.experimental.pallas import tpu as pltpu
from jax.sharding import PartitionSpec as P

D = 384
HEADS = 6
HEAD_DIM = 64
FF = 1536
PAIR = 2 * HEAD_DIM
HALF = 768
SHARDS = 4
BF = jnp.bfloat16
F32 = jnp.float32
VEC_ROWS = 16
COST = 1000

NT = (((1,), (1,)), ((), ()))
TN = (((0,), (0,)), ((), ()))


def dot(left, right, dims=(((1,), (0,)), ((), ()))):
    return lax.dot_general(left, right, dims, preferred_element_type=F32)


def xor_pass(x, axis, by):
    pairs = [(i, i ^ by) for i in range(lax.axis_size(axis))]
    return lax.ppermute(x, axis, pairs)


def call(kernel, outs, args, name, flops, scalars=1, ties=(), raw=0, scratch=()):
    smem = pl.BlockSpec(memory_space=pltpu.SMEM)
    vmem = pl.BlockSpec(memory_space=pltpu.VMEM)
    apart = pl.BlockSpec(memory_space=pl.ANY)
    size = sum(a.size * a.dtype.itemsize for a in args)
    size += sum(o.size * o.dtype.itemsize for o in outs)
    count = len(args)

    def body(*refs):
        kernel(*refs[:count], *refs[count + len(ties) :])

    return pl.pallas_call(
        body,
        out_shape=outs,
        in_specs=[smem] * scalars
        + [vmem] * (count - scalars - raw)
        + [apart] * (raw + len(ties)),
        out_specs=[vmem] * len(outs),
        scratch_shapes=list(scratch),
        compiler_params=pltpu.CompilerParams(vmem_limit_bytes=20 * 1024 * 1024),
        cost_estimate=pl.CostEstimate(
            flops=flops // COST, bytes_accessed=size // COST, transcendentals=0
        ),
        name=name,
    )(*args, *ties)


def after(arrays, *ties):
    apart = pl.BlockSpec(memory_space=pl.ANY)
    count = len(arrays)
    return pl.pallas_call(
        lambda *refs: None,
        out_shape=[jax.ShapeDtypeStruct(x.shape, x.dtype) for x in arrays],
        in_specs=[apart] * (count + len(ties)),
        out_specs=[apart] * count,
        input_output_aliases={i: i for i in range(count)},
        compiler_params=pltpu.CompilerParams(vmem_limit_bytes=1024 * 1024),
        name="after",
    )(*arrays, *ties)


def sds(shape, dtype):
    return jax.ShapeDtypeStruct(shape, dtype)


def normed(values):
    center = values - jnp.mean(values, axis=-1, keepdims=True)
    spread = jnp.mean(center * center, axis=-1, keepdims=True)
    rstd = lax.rsqrt(spread + 1e-05)
    return center * rstd, rstd


def norm_back(d, xhat, rstd, gain):
    dg = d * gain
    first = jnp.mean(dg, axis=-1, keepdims=True)
    second = jnp.mean(dg * xhat, axis=-1, keepdims=True)
    return rstd * (dg - first - xhat * second)


def col_sum(values):
    return jnp.sum(values, axis=0, keepdims=True)


def half_mask(rows, half):
    lane = lax.broadcasted_iota(jnp.int32, (rows, PAIR), 1)
    return (lane >= HEAD_DIM) if half else (lane < HEAD_DIM)


def place_rows(ids, full_ref, parts, first_col):
    me, section = ids[0], ids[1]
    width = full_ref.shape[1]
    for side in range(2):
        half = section ^ side
        for k, part in enumerate(parts[side]):
            rows = part.shape[0]
            at = pl.multiple_of(((me ^ k) * 2 + half) * rows, rows)
            full_ref[pl.ds(at, rows), :] = part[:, first_col : first_col + width]


def pack_kernel(ids, out, up, down, stay_ref, swap_ref, sems):
    section = ids[1]
    rows = out.shape[0] // 2
    copies = []

    def move(source, target):
        copy = pltpu.make_async_copy(source, target, sems.at[len(copies)])
        copy.start()
        copies.append(copy)

    for half, ref in ((1 - section, swap_ref), (section, stay_ref)):
        at = pl.ds(pl.multiple_of(half * rows, rows), rows)
        move(out.at[at, :], ref.at[:, :D])
        move(up.at[at, :], ref.at[:, D : D + FF])
        for j in range(4):
            at = pl.ds(pl.multiple_of(half * (4 * rows) + j * rows, rows), rows)
            move(down.at[at, :], ref.at[:, D + FF + j * D : D + FF + (j + 1) * D])
    for copy in copies:
        copy.wait()


def small_kernel(gains, biases, up_b, small_ref):
    bias = up_b[...]
    small_ref[...] = jnp.concatenate(
        [gains[...], biases[...]]
        + [bias[:, j * D : (j + 1) * D] for j in range(4)]
        + [jnp.zeros((4, D), F32)],
        axis=0,
    )


def pick_kernel(ids, stay, got, zero_ref, one_ref):
    first = ids[1] == 0
    here, there = stay[...], got[...]
    zero_ref[...] = jnp.where(first, here, there)
    one_ref[...] = jnp.where(first, there, here)


def away_kernel(ids, pair, out_ref):
    out_ref[...] = jnp.where(ids[0] < 2, pair[1], pair[0])


def home_kernel(masked, ids, present, pair, got, out_ref):
    here = jnp.where(ids[0] < 2, pair[0], pair[1])
    value = jnp.where(ids[1] == ids[0] >> 1, here, got[...])
    if masked:
        mask = present[0, ids[0] >> 1].astype(F32)
        value = (value.astype(F32) * mask).astype(BF)
    out_ref[...] = value


def order_kernel(ids, zero, one, same_ref, swap_ref):
    low = ids[0] < 2
    same_ref[...] = jnp.where(low, zero[...], one[...])
    swap_ref[...] = jnp.where(low, one[...], zero[...])


def clips_kernel(ids, same, swap, out_ref):
    first = ids[1] == 0
    out_ref[0, 0, 0] = jnp.where(first, same[...], swap[...])
    out_ref[0, 0, 1] = jnp.where(first, swap[...], same[...])


def choose_kernel(ids, zero, one, out_ref):
    out_ref[...] = jnp.where(ids[1] == 0, one[...], zero[...])


def section_sum_kernel(keep, got_one, got_two, stays_ref, first_ref, second_ref):
    stays_ref[...] = keep[0].astype(F32) + got_one[0].astype(F32)
    first_ref[0] = (keep[1].astype(F32) + got_one[1].astype(F32)).astype(BF)
    first_ref[1] = (keep[2].astype(F32) + got_two[0].astype(F32)).astype(BF)
    second_ref[...] = keep[3].astype(F32) + got_two[1].astype(F32)


def second_kernel(second, got, out_ref):
    out_ref[...] = (second[...] + got[1].astype(F32)).astype(BF)


def spread_kernel(ids, stays, got, late, own_ref, *message_refs):
    total = stays[...] + got[0].astype(F32) + late[...].astype(F32)
    refs = (own_ref, *message_refs)
    size = len(refs)
    rows = D // SHARDS // size
    me = ids[3]
    tail = total[3 * size * rows :, :]
    for k, ref in enumerate(refs):
        ref[3 * rows :, :] = tail.astype(ref.dtype)
    for r in range(size):
        block = jnp.concatenate(
            [total[(g * size + r) * rows : (g * size + r + 1) * rows, :] for g in range(3)], axis=0
        )
        for k, ref in enumerate(refs):

            @pl.when(me ^ k == r)
            def _():
                ref[: 3 * rows, :] = block.astype(ref.dtype)


def finish_kernel(ids, fin_zero, fin_one, got, vec_zero, vec_one, qkv, out, up, down, vec, up_vec):
    first = ids[1] == 0
    own = jnp.where(first, fin_zero[...], fin_one[...])
    other = got[...]
    low, high = jnp.where(first, own, other), jnp.where(first, other, own)
    n = low.shape[0] // 3
    up[:, :HALF] = low[:n]
    up[:, HALF:] = high[:n]
    for t, side in enumerate((low, high)):
        for j in range(2):
            at = (2 * t + j) * n
            down[at : at + n, :] = side[n : 2 * n, j * D : (j + 1) * D]
    qkv[:, :HALF] = low[2 * n :]
    qkv[:, HALF:] = high[2 * n :, :D]
    out[...] = high[2 * n :, D:]
    sums = jnp.where(first, vec_zero[...], vec_one[...])

    def taken(values, width):
        length = values.shape[1]
        source = lax.broadcasted_iota(jnp.int32, (length, width), 0)
        target = lax.broadcasted_iota(jnp.int32, (length, width), 1) + ids[2] * width
        spots = jnp.where(source == target, 1.0, 0.0)
        return lax.dot_general(
            values, spots, (((1,), (0,)), ((), ())),
            preferred_element_type=F32, precision=lax.Precision.HIGHEST,
        )

    rows = []
    for r in range(4):
        rows += [sums[r : r + 1, :D], sums[r : r + 1, D:]]
    vec[...] = taken(jnp.concatenate(rows, axis=0), n)
    both = jnp.concatenate([sums[4:5], sums[5:6]], axis=1)
    up_vec[...] = taken(jnp.broadcast_to(both, (8, FF)), 4 * n)


def attend_kernel(
    layer, ids, x0, x1, x2, x3, w0, w1, w2, w3, o0, o1, o2, o3, small,
    w_ref, xhat_ref, q_ref, k_ref, v_ref, lse_ref, mixed_ref,
):
    me = ids[0]
    rows = x0.shape[0]
    own_layer = ids[1] == layer
    for k, (own, other) in enumerate(((w0, o0), (w1, o1), (w2, o2), (w3, o3))):
        count = own.shape[0]
        at = pl.multiple_of((me ^ k) * count, count)
        w_ref[pl.ds(at, count), :] = jnp.where(own_layer, own[...], other[...])
    gains, biases = small[0:2, :], small[2:8, :]
    gain, shift = gains[0:1, :], biases[0:1, :]
    for r, x in enumerate((x0, x1, x2, x3)):
        xhat, unused = normed(x[...].astype(F32))
        xhat_ref[r * rows : (r + 1) * rows, :] = xhat.astype(BF)
        a = (xhat * gain + shift).astype(BF)
        if r == 0:
            q = (dot(a, w_ref[:, :D]) + biases[1:2, :]).astype(BF)
            q_ref[...] = (q.astype(F32) * (HEAD_DIM ** (-0.5))).astype(BF)
        k_ref[r * rows : (r + 1) * rows, :] = dot(a, w_ref[:, D : 2 * D]).astype(BF)
        v_ref[r * rows : (r + 1) * rows, :] = (
            dot(a, w_ref[:, 2 * D :]) + biases[2:3, :]
        ).astype(BF)
    mixed_t = []
    for pair in range(HEADS // 2):
        cols = slice(pair * PAIR, (pair + 1) * PAIR)
        k_pair = k_ref[:, cols]
        v_t = v_ref[:, cols].T
        q_pair = q_ref[:, cols].astype(F32)
        for half in range(2):
            head = 2 * pair + half
            qm = jnp.where(half_mask(rows, half), q_pair, 0.0).astype(BF)
            s = dot(k_pair, qm, NT)
            top = jnp.max(s, axis=0, keepdims=True)
            e = jnp.exp(s - top)
            total = jnp.sum(e, axis=0, keepdims=True)
            lse_ref[head : head + 1, :] = top + jnp.log(total)
            o = dot(v_t[half * HEAD_DIM : (half + 1) * HEAD_DIM, :], e.astype(BF))
            mixed_t.append(o * (1.0 / total))
    mixed_ref[...] = jnp.concatenate(mixed_t, axis=0).T.astype(BF)


def mlp_kernel(
    ids, present, x0, mixed, w0, w1, w2, w3, o0, o1, o2, o3, small,
    out_ref, resid_ref, z_ref, slope_ref, wo_ref, w1_ref, w2_ref,
):
    parts = ((w0, w1, w2, w3), (o0, o1, o2, o3))
    place_rows(ids, wo_ref, parts, 0)
    place_rows(ids, w1_ref, parts, D)
    me, section = ids[0], ids[1]
    for side in range(2):
        half = section ^ side
        for k, part in enumerate(parts[side]):
            rows = part.shape[0]
            for j in range(4):
                at = (((me ^ k) * 2 + half) * 4 + j) * rows
                left = D + FF + j * D
                w2_ref[pl.ds(pl.multiple_of(at, rows), rows), :] = part[:, left : left + D]
    gains, biases = small[0:2, :], small[2:8, :]
    up_b = jnp.concatenate([small[8 + j : 9 + j, :] for j in range(4)], axis=1)
    resid = x0[...].astype(F32) + (dot(mixed[...], wo_ref[...]) + biases[3:4, :])
    resid_ref[...] = resid
    xhat, unused = normed(resid)
    c = (xhat * gains[1:2, :] + biases[4:5, :]).astype(BF)
    upper = dot(c, w1_ref[...]) + up_b
    phi = 0.5 * (1.0 + lax.erf(upper * (2.0 ** -0.5)))
    z = (upper * phi).astype(BF)
    z_ref[...] = z
    bell = jnp.exp(-0.5 * upper * upper) * 0.3989422804014327
    slope_ref[...] = (phi + upper * bell).astype(BF)
    out = resid + (dot(z, w2_ref[...]) + biases[5:6, :])
    out_ref[...] = (out * present[0, ids[0] >> 1].astype(F32)).astype(BF)


def mlp_back_kernel(
    gout, z, slope, resid, wo, w1, w2, small,
    dresid_ref, ga_ref, du_ref, c_ref, dmixed_ref, vec_ref, upvec_ref,
):
    gains, biases = small[0:2, :], small[2:8, :]
    gm = gout[...]
    dz = dot(gm, w2[...], NT)
    du = (dz * slope[...].astype(F32)).astype(BF)
    du_ref[...] = du
    dc = dot(du, w1[...], NT)
    xhat, rstd = normed(resid[...])
    gain = gains[1:2, :]
    c_ref[...] = (xhat * gain + biases[4:5, :]).astype(BF)
    g_full = gm.astype(F32)
    dresid = g_full + norm_back(dc, xhat, rstd, gain)
    dresid_ref[...] = dresid
    ga = dresid.astype(BF)
    ga_ref[...] = ga
    dmixed_ref[...] = dot(ga, wo[...], NT).astype(BF)
    vec_ref[...] = jnp.concatenate(
        [
            col_sum(dc * xhat),
            col_sum(dc),
            col_sum(ga.astype(F32)),
            col_sum(g_full),
            jnp.zeros((4, D), F32),
        ],
        axis=0,
    )
    upvec_ref[...] = col_sum(du.astype(F32))


def attend_back_kernel(
    q_ref, k_ref, v_ref, lse, mixed, dmixed, xhat_ref, w_ref,
    own_ref, near_ref, swap_ref, dq_ref, dkv_ref, vec_ref,
):
    rows = q_ref.shape[0]
    prod = mixed[...].astype(F32) * dmixed[...].astype(F32)
    prod_t = prod.T
    dq_t = []
    for pair in range(HEADS // 2):
        cols = slice(pair * PAIR, (pair + 1) * PAIR)
        k_pair, v_pair = k_ref[:, cols], v_ref[:, cols]
        k_t = k_pair.T
        q_pair = q_ref[:, cols].astype(F32)
        do_pair = dmixed[:, cols].astype(F32)
        ps, dss, qms, doms = [], [], [], []
        for half in range(2):
            head = 2 * pair + half
            keep = half_mask(rows, half)
            qm = jnp.where(keep, q_pair, 0.0).astype(BF)
            dom = jnp.where(keep, do_pair, 0.0).astype(BF)
            p = jnp.exp(dot(k_pair, qm, NT) - lse[head : head + 1, :])
            dp = dot(v_pair, dom, NT)
            delta = col_sum(prod_t[head * HEAD_DIM : (head + 1) * HEAD_DIM, :])
            ds = (p * (dp - delta)).astype(BF)
            dq_t.append(
                dot(k_t[half * HEAD_DIM : (half + 1) * HEAD_DIM, :], ds) * (HEAD_DIM ** (-0.5))
            )
            ps.append(p.astype(BF))
            dss.append(ds)
            qms.append(qm)
            doms.append(dom)
        dkv_ref[:, cols] = dot(
            jnp.concatenate(dss, axis=1), jnp.concatenate(qms, axis=0)
        ).astype(BF)
        dkv_ref[:, D + pair * PAIR : D + (pair + 1) * PAIR] = dot(
            jnp.concatenate(ps, axis=1), jnp.concatenate(doms, axis=0)
        ).astype(BF)
    dq = jnp.concatenate(dq_t, axis=0).T.astype(BF)
    dq_ref[...] = dq
    gain_sum = jnp.zeros((1, D), F32)
    shift_sum = jnp.zeros((1, D), F32)
    outs = (own_ref, swap_ref.at[0], near_ref, swap_ref.at[1])
    for r, da_ref in enumerate(outs):
        at = slice(r * rows, (r + 1) * rows)
        da = dot(dkv_ref[at, :], w_ref[:, D:], NT)
        if r == 0:
            da = da + dot(dq, w_ref[:, :D], NT)
        gain_sum = gain_sum + col_sum(da * xhat_ref[at, :].astype(F32))
        shift_sum = shift_sum + col_sum(da)
        da_ref[...] = da.astype(da_ref.dtype)
    vec_ref[...] = jnp.concatenate(
        [
            gain_sum,
            shift_sum,
            col_sum(dq.astype(F32)),
            col_sum(dkv_ref[:, D:].astype(F32)),
            jnp.zeros((4, D), F32),
        ],
        axis=0,
    )


def norm_back_kernel(da_own, da_core, da_near, x0, dresid, small, out_ref):
    da = da_own[...] + da_core[0].astype(F32) + da_near[...].astype(F32)
    xhat, rstd = normed(x0[...].astype(F32))
    out_ref[...] = (dresid[...] + norm_back(da, xhat, rstd, small[0:1, :])).astype(BF)


def regroup(grad, s, replicas):
    rows = grad.shape[0] // (replicas * SHARDS)
    pieces = []
    for r in range(replicas):
        start = (r * SHARDS + s) * rows
        pieces.append(grad[start : start + rows, :])
    return pieces


def slot_of(ids, s, side):
    by = ids[0] ^ s
    turned = jnp.where(side == 0, by, ((by & 1) << 1) | (by >> 1))
    return turned ^ (turned >> 1)


def store_halves(ids, replicas, grad, keep_ref, send_ref, base):
    section = ids[1]
    first = section == 0
    left, right = grad[:, :HALF], grad[:, HALF:]
    own = jnp.where(first, left, right)
    other = jnp.where(first, right, left)
    for s in range(SHARDS):
        block = jnp.concatenate(regroup(own, s, replicas), axis=0).astype(BF)
        at = slice(base, base + block.shape[0])
        keep_ref[slot_of(ids, s, section), at, :] = block
        block = jnp.concatenate(regroup(other, s, replicas), axis=0).astype(BF)
        put(send_ref, slot_of(ids, s, 1 - section), at, block)


def put(refs, slot, at, block):
    @pl.when(slot < 2)
    def _():
        refs[0][slot, at, :] = block

    @pl.when(slot >= 2)
    def _():
        refs[1][slot - 2, at, :] = block


def grad_kernel(
    replicas, ids, c, du, z, gm, xhat, dq, dkv, mixed, ga, small, vec_one, vec_two, upvec,
    keep_ref, send_one, send_two,
):
    send_ref = (send_one, send_two)
    section = ids[1]
    first = section == 0
    store_halves(ids, replicas, dot(c[...], du[...], TN), keep_ref, send_ref, 0)
    grad = dot(z[...], gm[...], TN)
    rows = FF // (replicas * SHARDS)
    sub = rows // 4
    base = D // SHARDS
    for s in range(SHARDS):
        sides = ([], [])
        for r in range(replicas):
            start = (r * SHARDS + s) * rows
            parts = [grad[start + j * sub : start + (j + 1) * sub, :] for j in range(4)]
            sides[0].append(jnp.concatenate(parts[:2], axis=1))
            sides[1].append(jnp.concatenate(parts[2:], axis=1))
        low, high = (jnp.concatenate(side, axis=0) for side in sides)
        keep_ref[slot_of(ids, s, section), base : 2 * base, :] = jnp.where(
            first, low, high
        ).astype(BF)
        block = jnp.where(first, high, low).astype(BF)
        put(send_ref, slot_of(ids, s, 1 - section), slice(base, 2 * base), block)
    rows = dq.shape[0]
    a = (xhat[...].astype(F32) * small[0:1, :] + small[2:3, :]).astype(BF)
    grad = jnp.concatenate(
        [
            dot(a[:rows, :], dq[...], TN),
            dot(a, dkv[...], TN),
            dot(mixed[...], ga[...], TN),
        ],
        axis=1,
    )
    store_halves(ids, replicas, grad, keep_ref, send_ref, 2 * base)
    one, two, up = vec_one[...], vec_two[...], upvec[...]

    def wide(left, right):
        return jnp.concatenate([left, right], axis=1)

    vec = jnp.concatenate(
        [
            wide(one[0:1], two[0:1]),
            wide(one[1:2], one[2:3]),
            wide(one[3:4], two[2:3]),
            wide(two[1:2], two[3:4]),
            up[:, :HALF],
            up[:, HALF:],
            jnp.zeros((VEC_ROWS - 6, HALF), F32),
        ],
        axis=0,
    ).astype(BF)
    for s in range(SHARDS):
        keep_ref[s, 3 * base : 3 * base + VEC_ROWS, :] = vec
        send_ref[s // 2][s % 2, 3 * base : 3 * base + VEC_ROWS, :] = vec


def shard_spread(block):
    return [block] + [xor_pass(block, "shard", k) for k in (1, 2, 3)]


def both_cores(parts):
    return [*parts, *(xor_pass(part, "section", 1) for part in parts)]


def clip_frames(own):
    near = xor_pass(own, "shard", 1)
    return [own, xor_pass(own, "section", 1), near, xor_pass(near, "section", 1)]


def to_clip(ids, present, pair, masked):
    count = lax.axis_size("shard")
    pairs = [((i >> 1) * count + i, (i >> 1) * count + (i ^ 2)) for i in range(count)]
    rows = sds(pair.shape[1:], BF)
    (away,) = call(away_kernel, [rows], [ids, pair], "away", 1_000_000)
    got = lax.ppermute(away, ("section", "shard"), pairs)
    (home,) = call(
        functools.partial(home_kernel, masked),
        [rows],
        [ids, present, pair, got],
        "home",
        1_000_000,
        scalars=2,
    )
    return away, home


def from_clip(ids, pair):
    count = lax.axis_size("shard")

    def pairs(flip):
        out = []
        for sec in range(2):
            for i in range(count):
                clip, low = i >> 1, i & 1
                out.append((sec * count + i, (clip ^ flip) * count + sec * 2 + low))
        return out

    both = ("section", "shard")
    rows = sds(pair[0].shape, BF)
    same, swap = call(order_kernel, [rows, rows], [ids, *pair], "order", 1_000_000)
    return lax.ppermute(same, both, pairs(0)), lax.ppermute(swap, both, pairs(1))


def clips_of(ids, same, swap):
    out = sds((1, 1, 2) + same.shape, BF)
    return call(clips_kernel, [out], [ids, same, swap], "clips", 1_000_000)[0]


def section_sum(keep, send, ties):
    got = [xor_pass(part, "section", 1) for part in send]
    rows = keep.shape[1]
    return call(
        section_sum_kernel,
        [sds((rows, HALF), F32), sds((2, rows, HALF), BF), sds((rows, HALF), F32)],
        [keep, *got],
        "section_sum",
        1_000_000,
        scalars=0,
        ties=ties,
    )


def split_pairs(low, high):
    count = lax.axis_size("shard")
    return [(i, i ^ low) for i in range(count)] + [
        (count + i, count + (i ^ high)) for i in range(count)
    ]


def shard_sum(first_out, second_out, ties):
    both = ("section", "shard")
    got = lax.ppermute(first_out, both, split_pairs(1, 2))
    (message,) = call(
        second_kernel,
        [sds(second_out.shape, BF)],
        [second_out, got],
        "second",
        1_000_000,
        scalars=0,
        ties=ties,
    )
    return got, lax.ppermute(message, both, split_pairs(2, 1))


def replica_sum(ids, stays, got, late, fixed, ties):
    size = lax.axis_size("replica")
    groups = 3
    rows = D // SHARDS // size
    if size > SHARDS:
        summed = stays + got[0].astype(F32) + late.astype(F32)
        blocks = summed[: groups * size * rows].reshape(groups, size, rows, HALF)
        blocks = blocks.transpose(1, 0, 2, 3).reshape(size, groups * rows, HALF)
        mine = lax.psum_scatter(blocks.astype(BF), "replica", scatter_dimension=0, tiled=False)
        return mine.astype(F32), lax.psum(summed[groups * size * rows :], "replica")
    count = groups * rows + fixed
    own, *messages = call(
        spread_kernel,
        [sds((count, HALF), F32)] + [sds((count, HALF), BF)] * (size - 1),
        [ids, stays, got, late],
        "spread",
        1_000_000,
        ties=ties,
    )
    for k, message in enumerate(messages):
        own = own + xor_pass(message, "replica", k + 1).astype(F32)
    return own[: groups * rows], own[groups * rows :]


def local(
    inputs,
    cotangent,
    clip_present,
    qkv_weight,
    out_weight,
    up_weight,
    down_weight,
    norm_gains,
    biases,
    up_bias,
):
    section = lax.axis_index("section")
    shard = lax.axis_index("shard")
    replica = lax.axis_index("replica")
    replicas = lax.axis_size("replica")
    first = section == 0
    rows = inputs.shape[2]
    place = replica * SHARDS + shard
    ids = jnp.stack([shard, section, place, replica]).astype(jnp.int32)
    own_rows = D // SHARDS

    away, x_first = to_clip(ids, clip_present, inputs[0], False)

    half_rows = own_rows // 2
    packed = sds((half_rows, 9 * D), BF)
    stay, swap = call(
        pack_kernel,
        [packed, packed],
        [ids, out_weight[0], up_weight[0], down_weight[0]],
        "pack",
        1_000_000,
        raw=3,
        ties=(away,),
        scratch=[pltpu.SemaphoreType.DMA((12,))],
    )
    got = xor_pass(swap, "section", 1)
    qkv_part = both_cores(shard_spread(qkv_weight[0]))
    frames = clip_frames(x_first)
    (small,) = call(
        small_kernel,
        [sds((16, D), F32)],
        [norm_gains[0], biases[0], up_bias[0][None]],
        "small",
        1_000_000,
        scalars=0,
        ties=(x_first,),
    )
    other_small = xor_pass(small, "section", 1)
    both = sds((16, D), F32)
    small_layers = call(
        pick_kernel, [both, both], [ids, small, other_small], "small_pick", 1_000_000
    )
    rest_zero, rest_one = call(
        pick_kernel, [packed, packed], [ids, stay, got], "pick", 1_000_000,
        ties=(frames[2], qkv_part[1], qkv_part[2]),
    )
    rest_parts = [shard_spread(rest_zero), None]

    whole = SHARDS * rows
    saved = []
    outs = []
    for layer in range(2):
        small = small_layers[layer]
        w_qkv, xhat, q, k, v, lse, mixed = call(
            functools.partial(attend_kernel, layer),
            [
                sds((D, 3 * D), BF),
                sds((whole, D), BF),
                sds((rows, D), BF),
                sds((whole, D), BF),
                sds((whole, D), BF),
                sds((8, rows), F32),
                sds((rows, D), BF),
            ],
            [ids, *frames, *qkv_part, small],
            "attend",
            4_000_000_000,
            ties=(gout_last,) if layer == 1 else (),
        )
        if layer == 0:
            rest_parts[1] = shard_spread(after([rest_one], mixed)[0])
        rest_part = both_cores([rest_parts[layer][0], *after(rest_parts[layer][1:], mixed)])
        out, resid, z, slope, w_out, w_up, w_down = call(
            mlp_kernel,
            [
                sds((rows, D), BF),
                sds((rows, D), F32),
                sds((rows, FF), BF),
                sds((rows, FF), BF),
                sds((D, D), BF),
                sds((D, FF), BF),
                sds((FF, D), BF),
            ],
            [ids, clip_present, frames[0], mixed, *rest_part, small],
            "mlp",
            2_000_000_000,
            scalars=2,
        )
        saved.append(
            (frames[0], w_qkv, xhat, q, k, v, lse, mixed, resid, z, slope, w_out, w_up, w_down)
        )
        outs.append(out)
        if layer == 0:
            frames = clip_frames(out)
            (late,) = after([cotangent[0]], out)
            unused, gout_last = to_clip(ids, clip_present, late, True)

    outs_back = from_clip(ids, outs)
    gout = gout_last
    shares = [None, None]
    grads = [None, None]
    before = ()
    for layer in (1, 0):
        small = small_layers[layer]
        x0, w_qkv, xhat, q, k, v, lse, mixed, resid, z, slope, w_out, w_up, w_down = saved[layer]
        dresid, ga, du, c, dmixed, vec_two, upvec = call(
            mlp_back_kernel,
            [
                sds((rows, D), F32),
                sds((rows, D), BF),
                sds((rows, FF), BF),
                sds((rows, D), BF),
                sds((rows, D), BF),
                sds((8, D), F32),
                sds((1, FF), F32),
            ],
            [gout, z, slope, resid, w_out, w_up, w_down, small],
            "mlp_back",
            2_000_000_000,
            scalars=0,
        )
        da_own, da_near, da_swap, dq, dkv, vec_one = call(
            attend_back_kernel,
            [
                sds((rows, D), F32),
                sds((rows, D), F32),
                sds((2, rows, D), BF),
                sds((rows, D), BF),
                sds((whole, 2 * D), BF),
                sds((8, D), F32),
            ],
            [q, k, v, lse, mixed, dmixed, xhat, w_qkv],
            "attend_back",
            8_000_000_000,
            scalars=0,
            ties=before,
        )
        got = xor_pass(da_swap, "section", 1)
        near = (da_near + got[1].astype(F32)).astype(BF)
        back = xor_pass(near, "shard", 1)
        pair = sds((2, 3 * own_rows + VEC_ROWS, HALF), BF)
        keep, *send = call(
            functools.partial(grad_kernel, replicas),
            [sds((SHARDS,) + pair.shape[1:], BF), pair, pair],
            [ids, c, du, z, gout, xhat, dq, dkv, mixed, ga, small, vec_one, vec_two, upvec],
            "grad",
            4_000_000_000,
            ties=(near,) if layer == 1 else (),
        )
        if layer == 1:
            send = after(send, back, *outs_back)
        ties = () if layer == 1 else (back, late)
        stays, first_out, second_out = section_sum(keep, send, ties)
        (gin,) = call(
            norm_back_kernel,
            [sds((rows, D), BF)],
            [da_own, got, back, x0, dresid, small],
            "norm_back",
            100_000_000,
            scalars=0,
        )
        grads[layer] = gin
        gout = gin
        if layer == 0:
            grads_back = from_clip(ids, grads)
            first_got, late = shard_sum(first_out, second_out, (shares[1][0],))
            shares[0] = replica_sum(ids, stays, first_got, late, VEC_ROWS, grads_back)
        else:
            first_got, late = shard_sum(first_out, second_out, ())
            shares[1] = replica_sum(ids, stays, first_got, late, VEC_ROWS, ())
            before = (first_out,)

    outputs_local = clips_of(ids, *outs_back)
    grads_local = clips_of(ids, *grads_back)
    n = own_rows // replicas
    (away,) = call(
        choose_kernel,
        [sds((3 * n, HALF), F32)],
        [ids, shares[0][0], shares[1][0]],
        "choose",
        1_000_000,
    )
    got = xor_pass(away, "section", 1)
    qkv_grad, out_grad, up_grad, down_grad, vec, up_vec = call(
        finish_kernel,
        [
            sds((n, 3 * D), F32),
            sds((n, D), F32),
            sds((n, FF), F32),
            sds((4 * n, D), F32),
            sds((8, n), F32),
            sds((8, 4 * n), F32),
        ],
        [ids, shares[0][0], shares[1][0], got, shares[0][1], shares[1][1]],
        "finish",
        1_000_000,
    )
    return (
        outputs_local,
        grads_local,
        qkv_grad[None],
        out_grad[None],
        up_grad[None],
        down_grad[None],
        vec[None, :2],
        vec[None, 2:],
        up_vec[:1],
    )


def solution(mesh):
    return jax.shard_map(
        local,
        mesh=mesh,
        in_specs=(
            P("replica", None, "shard", None),
            P("replica", None, "shard", None),
            P("replica", None),
            P("section", "shard", None),
            P("section", "shard", None),
            P("section", "shard", None),
            P("section", "shard", None),
            P("section", None, None),
            P("section", None, None),
            P("section", None),
        ),
        out_specs=(
            P("section", "replica", None, "shard", None),
            P("section", "replica", None, "shard", None),
            P("section", ("replica", "shard"), None),
            P("section", ("replica", "shard"), None),
            P("section", ("replica", "shard"), None),
            P("section", ("replica", "shard"), None),
            P("section", None, ("replica", "shard")),
            P("section", None, ("replica", "shard")),
            P("section", ("replica", "shard")),
        ),
        check_vma=False,
    )
```

```python
import functools

import jax
import jax.numpy as jnp
from jax import lax
from jax.experimental import pallas as pl
from jax.experimental.pallas import tpu as pltpu
from jax.sharding import PartitionSpec as P

D = 384
HEADS = 6
HEAD_DIM = 64
FF = 1536
PAIR = 2 * HEAD_DIM
HALF = 768
SHARDS = 4
BF = jnp.bfloat16
F32 = jnp.float32
VEC_ROWS = 16
COST = 1000

NT = (((1,), (1,)), ((), ()))
TN = (((0,), (0,)), ((), ()))


def dot(left, right, dims=(((1,), (0,)), ((), ()))):
    return lax.dot_general(left, right, dims, preferred_element_type=F32)


def xor_pass(x, axis, by):
    pairs = [(i, i ^ by) for i in range(lax.axis_size(axis))]
    return lax.ppermute(x, axis, pairs)


def call(kernel, outs, args, name, flops, scalars=1, ties=(), raw=0, scratch=()):
    smem = pl.BlockSpec(memory_space=pltpu.SMEM)
    vmem = pl.BlockSpec(memory_space=pltpu.VMEM)
    apart = pl.BlockSpec(memory_space=pl.ANY)
    size = sum(a.size * a.dtype.itemsize for a in args)
    size += sum(o.size * o.dtype.itemsize for o in outs)
    count = len(args)

    def body(*refs):
        kernel(*refs[:count], *refs[count + len(ties) :])

    return pl.pallas_call(
        body,
        out_shape=outs,
        in_specs=[smem] * scalars
        + [vmem] * (count - scalars - raw)
        + [apart] * (raw + len(ties)),
        out_specs=[vmem] * len(outs),
        scratch_shapes=list(scratch),
        compiler_params=pltpu.CompilerParams(vmem_limit_bytes=20 * 1024 * 1024),
        cost_estimate=pl.CostEstimate(
            flops=flops // COST, bytes_accessed=size // COST, transcendentals=0
        ),
        name=name,
    )(*args, *ties)


def after(arrays, *ties):
    apart = pl.BlockSpec(memory_space=pl.ANY)
    count = len(arrays)
    return pl.pallas_call(
        lambda *refs: None,
        out_shape=[jax.ShapeDtypeStruct(x.shape, x.dtype) for x in arrays],
        in_specs=[apart] * (count + len(ties)),
        out_specs=[apart] * count,
        input_output_aliases={i: i for i in range(count)},
        compiler_params=pltpu.CompilerParams(vmem_limit_bytes=1024 * 1024),
        name="after",
    )(*arrays, *ties)


def sds(shape, dtype):
    return jax.ShapeDtypeStruct(shape, dtype)


def normed(values):
    center = values - jnp.mean(values, axis=-1, keepdims=True)
    spread = jnp.mean(center * center, axis=-1, keepdims=True)
    rstd = lax.rsqrt(spread + 1e-05)
    return center * rstd, rstd


def norm_back(d, xhat, rstd, gain):
    dg = d * gain
    first = jnp.mean(dg, axis=-1, keepdims=True)
    second = jnp.mean(dg * xhat, axis=-1, keepdims=True)
    return rstd * (dg - first - xhat * second)


def col_sum(values):
    return jnp.sum(values, axis=0, keepdims=True)


def half_mask(rows, half):
    lane = lax.broadcasted_iota(jnp.int32, (rows, PAIR), 1)
    return (lane >= HEAD_DIM) if half else (lane < HEAD_DIM)


def held_rows(ids, parts, stepped):
    me, section = ids[0], ids[1]
    for side in range(2):
        half = section ^ side
        by = (0, 1 + half, 2 - half, 3) if stepped else (0, 1, 2, 3)
        for k, part in zip(by, parts[side]):
            yield (me ^ k) * 2 + half, part


def place_rows(ids, full_ref, parts, stepped, first_col):
    width = full_ref.shape[1]
    for place, part in held_rows(ids, parts, stepped):
        rows = part.shape[0]
        at = pl.multiple_of(place * rows, rows)
        full_ref[pl.ds(at, rows), :] = part[:, first_col : first_col + width]


def pack_kernel(ids, out, up, down, stay_ref, swap_ref, sems):
    section = ids[1]
    rows = out.shape[0] // 2
    copies = []

    def move(source, target):
        copy = pltpu.make_async_copy(source, target, sems.at[len(copies)])
        copy.start()
        copies.append(copy)

    for half, ref in ((1 - section, swap_ref), (section, stay_ref)):
        at = pl.ds(pl.multiple_of(half * rows, rows), rows)
        move(out.at[at, :], ref.at[:, :D])
        move(up.at[at, :], ref.at[:, D : D + FF])
        for j in range(4):
            at = pl.ds(pl.multiple_of(half * (4 * rows) + j * rows, rows), rows)
            move(down.at[at, :], ref.at[:, D + FF + j * D : D + FF + (j + 1) * D])
    for copy in copies:
        copy.wait()


def small_kernel(gains, biases, up_b, small_ref):
    bias = up_b[...]
    small_ref[...] = jnp.concatenate(
        [gains[...], biases[...]]
        + [bias[:, j * D : (j + 1) * D] for j in range(4)]
        + [jnp.zeros((4, D), F32)],
        axis=0,
    )


def pick_kernel(ids, stay, got, zero_ref, one_ref):
    first = ids[1] == 0
    here, there = stay[...], got[...]
    zero_ref[...] = jnp.where(first, here, there)
    one_ref[...] = jnp.where(first, there, here)


def outgoing_kernel(ids, pair, block_ref, half_ref):
    section = ids[1]
    low = ids[0] < 2
    here = jnp.where(low, pair[0], pair[1])
    there = jnp.where(low, pair[1], pair[0])
    block_ref[...] = jnp.where(section == 0, here, there)
    cut = half_ref.shape[0]
    half_ref[...] = jnp.where(section == 0, there[:cut], there[cut:])


def arrange_kernel(ids, pair, mine, other, half_mine, half_other, own, core, near, across):
    section = ids[1]
    first = section == 0
    local = jnp.where(ids[0] < 2, pair[0], pair[1])
    beside = jnp.where(first, mine[...], other[...])
    far = jnp.where(first, other[...], mine[...])
    top, bottom = half_mine[...], half_other[...]
    diagonal = jnp.concatenate(
        [jnp.where(first, top, bottom), jnp.where(first, bottom, top)], axis=0
    )
    home = section == ids[0] >> 1
    own[...] = jnp.where(home, local, far)
    core[...] = jnp.where(home, far, local)
    near[...] = jnp.where(home, beside, diagonal)
    across[...] = jnp.where(home, diagonal, beside)


def away_kernel(ids, pair, out_ref):
    out_ref[...] = jnp.where(ids[0] < 2, pair[1], pair[0])


def home_kernel(ids, present, pair, got, out_ref):
    here = jnp.where(ids[0] < 2, pair[0], pair[1])
    value = jnp.where(ids[1] == ids[0] >> 1, here, got[...])
    mask = present[0, ids[0] >> 1].astype(F32)
    out_ref[...] = (value.astype(F32) * mask).astype(BF)


def order_kernel(ids, zero, one, same_ref, swap_ref):
    low = ids[0] < 2
    same_ref[...] = jnp.where(low, zero[...], one[...])
    swap_ref[...] = jnp.where(low, one[...], zero[...])


def clips_kernel(ids, same, swap, out_ref):
    first = ids[1] == 0
    out_ref[0, 0, 0] = jnp.where(first, same[...], swap[...])
    out_ref[0, 0, 1] = jnp.where(first, swap[...], same[...])


def choose_kernel(n, ids, mlp, attn, both, out_ref):
    first = ids[1] == 0
    out_ref[: 2 * n, :] = jnp.where(first, both[: 2 * n, :], mlp[...])
    out_ref[2 * n :, :] = jnp.where(first, both[2 * n : 3 * n, :], attn[:n, :])


def section_sum_kernel(stepped, *refs):
    parts = len(refs) // (6 if stepped else 7)
    outs = refs[3 * parts :]
    per = len(outs) // parts
    for part in range(parts):
        keep, got_one, got_two = refs[3 * part : 3 * part + 3]
        own_ref, *others = outs[per * part : per * part + per]
        sums = [
            keep[e].astype(F32) + (got_one, got_two)[e // 2][e % 2].astype(F32) for e in range(4)
        ]
        own_ref[...] = sums[0]
        if stepped:
            others[0][0] = sums[1].astype(BF)
            others[0][1] = sums[2].astype(BF)
            others[1][...] = sums[3]
        else:
            for ref, total in zip(others, sums[1:]):
                ref[...] = total.astype(BF)


def second_kernel(second, got, out_ref):
    out_ref[...] = (second[...] + got[1].astype(F32)).astype(BF)


def spread_kernel(groups, terms, ids, *refs):
    count = len(groups)
    outs = refs[terms * count :]
    size = len(outs)
    rows = D // SHARDS // size
    me = ids[3]
    base = 0
    for part in range(count):
        total = refs[terms * part][...]
        for ref in refs[terms * part + 1 : terms * part + terms]:
            total = total + (ref[0] if len(ref.shape) == 3 else ref[...]).astype(F32)
        end = base + groups[part] * rows
        tail = total[groups[part] * size * rows :, :]
        if tail.shape[0]:
            for ref in outs:
                ref[end : end + tail.shape[0], :] = tail.astype(ref.dtype)
        for r in range(size):
            block = jnp.concatenate(
                [
                    total[(g * size + r) * rows : (g * size + r + 1) * rows, :]
                    for g in range(groups[part])
                ],
                axis=0,
            )
            for k, ref in enumerate(outs):

                @pl.when(me ^ k == r)
                def _():
                    ref[base:end, :] = block.astype(ref.dtype)

        base = end + tail.shape[0]


def finish_kernel(
    ids, mlp_zero, attn_zero, both_one, got,
    qkv, out, up, down, gain, bias, up_vec,
):
    first = ids[1] == 0

    def sides(zero, one, other):
        own = jnp.where(first, zero, one)
        return jnp.where(first, own, other), jnp.where(first, other, own)

    n = mlp_zero.shape[0] // 2
    low, high = sides(mlp_zero[...], both_one[: 2 * n, :], got[: 2 * n, :])
    up[0, :, :HALF] = low[:n]
    up[0, :, HALF:] = high[:n]
    for t, side in enumerate((low, high)):
        for j in range(2):
            at = (2 * t + j) * n
            down[0, at : at + n, :] = side[n:, j * D : (j + 1) * D]
    low, high = sides(attn_zero[:n, :], both_one[2 * n : 3 * n, :], got[2 * n :, :])
    qkv[0, :, :HALF] = low
    qkv[0, :, HALF:] = high[:, :D]
    out[0] = high[:, D:]
    vec_zero, vec_one = attn_zero[n:, :], both_one[3 * n :, :]
    sums = jnp.where(first, vec_zero, vec_one)

    def taken(values, width):
        length = values.shape[1]
        source = lax.broadcasted_iota(jnp.int32, (length, width), 0)
        target = lax.broadcasted_iota(jnp.int32, (length, width), 1) + ids[2] * width
        spots = jnp.where(source == target, 1.0, 0.0)
        return lax.dot_general(
            values, spots, (((1,), (0,)), ((), ())),
            preferred_element_type=F32, precision=lax.Precision.HIGHEST,
        )

    rows = []
    for r in range(4):
        rows += [sums[r : r + 1, :D], sums[r : r + 1, D:]]
    vec = taken(jnp.concatenate(rows, axis=0), n)
    gain[0] = vec[:2]
    bias[0] = vec[2:]
    both = jnp.concatenate([sums[4:5], sums[5:6]], axis=1)
    up_vec[...] = taken(jnp.broadcast_to(both, (8, FF)), 4 * n)[:1]


def attend_kernel(
    layer, ids, x0, x1, x2, x3, w0, w1, w2, w3, o0, o1, o2, o3, small,
    w_ref, xhat_ref, q_ref, k_ref, v_ref, lse_ref, mixed_ref,
):
    me = ids[0]
    rows = x0.shape[0]
    own_layer = ids[1] == layer
    for k, (own, other) in enumerate(((w0, o0), (w1, o1), (w2, o2), (w3, o3))):
        count = own.shape[0]
        at = pl.multiple_of((me ^ k) * count, count)
        w_ref[pl.ds(at, count), :] = jnp.where(own_layer, own[...], other[...])
    gains, biases = small[0:2, :], small[2:8, :]
    gain, shift = gains[0:1, :], biases[0:1, :]
    for r, x in enumerate((x0, x1, x2, x3)):
        xhat, unused = normed(x[...].astype(F32))
        xhat_ref[r * rows : (r + 1) * rows, :] = xhat.astype(BF)
        a = (xhat * gain + shift).astype(BF)
        if r == 0:
            q = (dot(a, w_ref[:, :D]) + biases[1:2, :]).astype(BF)
            q_ref[...] = (q.astype(F32) * (HEAD_DIM ** (-0.5))).astype(BF)
        k_ref[r * rows : (r + 1) * rows, :] = dot(a, w_ref[:, D : 2 * D]).astype(BF)
        v_ref[r * rows : (r + 1) * rows, :] = (
            dot(a, w_ref[:, 2 * D :]) + biases[2:3, :]
        ).astype(BF)

    def one_pair(pair, carry):
        cols = pl.ds(pl.multiple_of(pair * PAIR, PAIR), PAIR)
        k_pair = k_ref[:, cols]
        v_t = v_ref[:, cols].T
        q_pair = q_ref[:, cols].astype(F32)
        mixed_t = []
        for half in range(2):
            qm = jnp.where(half_mask(rows, half), q_pair, 0.0).astype(BF)
            s = dot(k_pair, qm, NT)
            top = jnp.max(s, axis=0, keepdims=True)
            e = jnp.exp(s - top)
            total = jnp.sum(e, axis=0, keepdims=True)
            lse_ref[pl.ds(2 * pair + half, 1), :] = top + jnp.log(total)
            o = dot(v_t[half * HEAD_DIM : (half + 1) * HEAD_DIM, :], e.astype(BF))
            mixed_t.append(o * (1.0 / total))
        mixed_ref[:, cols] = jnp.concatenate(mixed_t, axis=0).T.astype(BF)
        return carry

    lax.fori_loop(0, HEADS // 2, one_pair, 0)


def mlp_kernel(stepped, ids, present, x0, mixed, *refs):
    out_ref, resid_ref, z_ref, slope_ref, wo_ref, w1_ref, w2_ref = refs[-7:]
    small = refs[-8]
    count = (len(refs) - 8) // 2
    parts = [refs[:count], refs[count : 2 * count]]
    if stepped:
        parts = [(own, got, pair.at[0], pair.at[1]) for own, got, pair in parts]
    place_rows(ids, wo_ref, parts, stepped, 0)
    place_rows(ids, w1_ref, parts, stepped, D)
    for place, part in held_rows(ids, parts, stepped):
        rows = part.shape[0]
        for j in range(4):
            at = pl.multiple_of((place * 4 + j) * rows, rows)
            left = D + FF + j * D
            w2_ref[pl.ds(at, rows), :] = part[:, left : left + D]
    gains, biases = small[0:2, :], small[2:8, :]
    up_b = jnp.concatenate([small[8 + j : 9 + j, :] for j in range(4)], axis=1)
    resid = x0[...].astype(F32) + (dot(mixed[...], wo_ref[...]) + biases[3:4, :])
    resid_ref[...] = resid
    xhat, unused = normed(resid)
    c = (xhat * gains[1:2, :] + biases[4:5, :]).astype(BF)
    upper = dot(c, w1_ref[...]) + up_b
    phi = 0.5 * (1.0 + lax.erf(upper * (2.0 ** -0.5)))
    z = (upper * phi).astype(BF)
    z_ref[...] = z
    bell = jnp.exp(-0.5 * upper * upper) * 0.3989422804014327
    slope_ref[...] = (phi + upper * bell).astype(BF)
    out = resid + (dot(z, w2_ref[...]) + biases[5:6, :])
    out_ref[...] = (out * present[0, ids[0] >> 1].astype(F32)).astype(BF)


def mlp_back_kernel(
    gout, z, slope, resid, wo, w1, w2, small,
    dresid_ref, ga_ref, du_ref, c_ref, dmixed_ref, vec_ref, upvec_ref,
):
    gains, biases = small[0:2, :], small[2:8, :]
    gm = gout[...]
    dz = dot(gm, w2[...], NT)
    du = (dz * slope[...].astype(F32)).astype(BF)
    du_ref[...] = du
    dc = dot(du, w1[...], NT)
    xhat, rstd = normed(resid[...])
    gain = gains[1:2, :]
    c_ref[...] = (xhat * gain + biases[4:5, :]).astype(BF)
    g_full = gm.astype(F32)
    dresid = g_full + norm_back(dc, xhat, rstd, gain)
    dresid_ref[...] = dresid
    ga = dresid.astype(BF)
    ga_ref[...] = ga
    dmixed_ref[...] = dot(ga, wo[...], NT).astype(BF)
    vec_ref[...] = jnp.concatenate(
        [
            col_sum(dc * xhat),
            col_sum(dc),
            col_sum(ga.astype(F32)),
            col_sum(g_full),
            jnp.zeros((4, D), F32),
        ],
        axis=0,
    )
    upvec_ref[...] = col_sum(du.astype(F32))


def attend_back_kernel(
    q_ref, k_ref, v_ref, lse, mixed, dmixed, xhat_ref, w_ref,
    own_ref, near_ref, swap_ref, dq_ref, dkv_ref, vec_ref,
):
    rows = q_ref.shape[0]

    def one_pair(pair, carry):
        cols = pl.ds(pl.multiple_of(pair * PAIR, PAIR), PAIR)
        k_pair, v_pair = k_ref[:, cols], v_ref[:, cols]
        k_t = k_pair.T
        q_pair = q_ref[:, cols].astype(F32)
        do_pair = dmixed[:, cols].astype(F32)
        prod_t = (mixed[:, cols].astype(F32) * do_pair).T
        dq_t, ps, dss, qms, doms = [], [], [], [], []
        for half in range(2):
            keep = half_mask(rows, half)
            qm = jnp.where(keep, q_pair, 0.0).astype(BF)
            dom = jnp.where(keep, do_pair, 0.0).astype(BF)
            p = jnp.exp(dot(k_pair, qm, NT) - lse[pl.ds(2 * pair + half, 1), :])
            dp = dot(v_pair, dom, NT)
            delta = col_sum(prod_t[half * HEAD_DIM : (half + 1) * HEAD_DIM, :])
            ds = (p * (dp - delta)).astype(BF)
            dq_t.append(
                dot(k_t[half * HEAD_DIM : (half + 1) * HEAD_DIM, :], ds) * (HEAD_DIM ** (-0.5))
            )
            ps.append(p.astype(BF))
            dss.append(ds)
            qms.append(qm)
            doms.append(dom)
        dkv_ref[:, cols] = dot(
            jnp.concatenate(dss, axis=1), jnp.concatenate(qms, axis=0)
        ).astype(BF)
        dkv_ref[:, pl.ds(pl.multiple_of(D + pair * PAIR, PAIR), PAIR)] = dot(
            jnp.concatenate(ps, axis=1), jnp.concatenate(doms, axis=0)
        ).astype(BF)
        dq_ref[:, cols] = jnp.concatenate(dq_t, axis=0).T.astype(BF)
        return carry

    lax.fori_loop(0, HEADS // 2, one_pair, 0)
    dq = dq_ref[...]
    gain_sum = jnp.zeros((1, D), F32)
    shift_sum = jnp.zeros((1, D), F32)
    outs = (own_ref, swap_ref.at[0], near_ref, swap_ref.at[1])
    for r, da_ref in enumerate(outs):
        at = slice(r * rows, (r + 1) * rows)
        da = dot(dkv_ref[at, :], w_ref[:, D:], NT)
        if r == 0:
            da = da + dot(dq, w_ref[:, :D], NT)
        gain_sum = gain_sum + col_sum(da * xhat_ref[at, :].astype(F32))
        shift_sum = shift_sum + col_sum(da)
        da_ref[...] = da.astype(da_ref.dtype)
    vec_ref[...] = jnp.concatenate(
        [
            gain_sum,
            shift_sum,
            col_sum(dq.astype(F32)),
            col_sum(dkv_ref[:, D:].astype(F32)),
            jnp.zeros((4, D), F32),
        ],
        axis=0,
    )


def norm_back_kernel(da_own, da_core, da_near, x0, dresid, small, out_ref):
    da = da_own[...] + da_core[0].astype(F32) + da_near[...].astype(F32)
    xhat, rstd = normed(x0[...].astype(F32))
    out_ref[...] = (dresid[...] + norm_back(da, xhat, rstd, small[0:1, :])).astype(BF)


def regroup(grad, s, replicas):
    rows = grad.shape[0] // (replicas * SHARDS)
    pieces = []
    for r in range(replicas):
        start = (r * SHARDS + s) * rows
        pieces.append(grad[start : start + rows, :])
    return pieces


def slot_of(ids, s, side):
    by = ids[0] ^ s
    if side is None:
        return by
    turned = jnp.where(side == 0, by, ((by & 1) << 1) | (by >> 1))
    return turned ^ (turned >> 1)


def put(refs, slot, at, block):
    @pl.when(slot < 2)
    def _():
        refs[0][slot, at, :] = block

    @pl.when(slot >= 2)
    def _():
        refs[1][slot - 2, at, :] = block


def grad_kernel(
    replicas, layer, ids, c, du, z, gm, xhat, dq, dkv, mixed, ga, small, vec_one, vec_two,
    upvec, *outs,
):
    section = ids[1]
    first = section == 0
    base = D // SHARDS
    start_of = 2 * base if layer == 1 else 0
    side = section if layer == 1 else None

    def store(refs, s, at, own, other):
        keep_ref, *send_refs = refs
        keep_ref[slot_of(ids, s, side), at, :] = own.astype(BF)
        away = None if side is None else 1 - side
        put(send_refs, slot_of(ids, s, away), at, other.astype(BF))

    def store_halves(refs, grad, at):
        left, right = grad[:, :HALF], grad[:, HALF:]
        own = jnp.where(first, left, right)
        other = jnp.where(first, right, left)
        for s in range(SHARDS):
            blocks = [
                jnp.concatenate(regroup(half, s, replicas), axis=0) for half in (own, other)
            ]
            store(refs, s, at, *blocks)

    store_halves(outs[:3], dot(c[...], du[...], TN), slice(0, base))
    grad = dot(z[...], gm[...], TN)
    rows = FF // (replicas * SHARDS)
    sub = rows // 4
    for s in range(SHARDS):
        sides = ([], [])
        for r in range(replicas):
            start = (r * SHARDS + s) * rows
            parts = [grad[start + j * sub : start + (j + 1) * sub, :] for j in range(4)]
            sides[0].append(jnp.concatenate(parts[:2], axis=1))
            sides[1].append(jnp.concatenate(parts[2:], axis=1))
        low, high = (jnp.concatenate(side, axis=0) for side in sides)
        own, other = jnp.where(first, low, high), jnp.where(first, high, low)
        store(outs[:3], s, slice(base, 2 * base), own, other)
    count = dq.shape[0]
    a = (xhat[...].astype(F32) * small[0:1, :] + small[2:3, :]).astype(BF)
    grad = jnp.concatenate(
        [
            dot(a[:count, :], dq[...], TN),
            dot(a, dkv[...], TN),
            dot(mixed[...], ga[...], TN),
        ],
        axis=1,
    )
    store_halves(outs[-3:], grad, slice(start_of, start_of + base))
    one, two, up = vec_one[...], vec_two[...], upvec[...]

    def wide(left, right):
        return jnp.concatenate([left, right], axis=1)

    vec = jnp.concatenate(
        [
            wide(one[0:1], two[0:1]),
            wide(one[1:2], one[2:3]),
            wide(one[3:4], two[2:3]),
            wide(two[1:2], two[3:4]),
            up[:, :HALF],
            up[:, HALF:],
            jnp.zeros((VEC_ROWS - 6, HALF), F32),
        ],
        axis=0,
    ).astype(BF)
    at = slice(start_of + base, start_of + base + VEC_ROWS)
    for s in range(SHARDS):
        outs[-3][s, at, :] = vec
        outs[-2 + s // 2][s % 2, at, :] = vec


def shard_spread(block):
    return [block] + [xor_pass(block, "shard", k) for k in (1, 2, 3)]


def stack_kernel(one, two, out_ref):
    out_ref[0] = one[...]
    out_ref[1] = two[...]


def shard_steps(block):
    return block, lax.ppermute(block, ("section", "shard"), split_pairs(1, 2))


def shard_steps_end(block, got, tie):
    (pair,) = call(
        stack_kernel,
        [sds((2,) + block.shape, BF)],
        [block, got],
        "stack",
        1_000_000,
        scalars=0,
        ties=(tie,),
    )
    return [block, got, lax.ppermute(pair, ("section", "shard"), split_pairs(2, 1))]


def both_cores(parts):
    return [*parts, *(xor_pass(part, "section", 1) for part in parts)]


def clip_frames(own):
    near = xor_pass(own, "shard", 1)
    return [own, xor_pass(own, "section", 1), near, xor_pass(near, "section", 1)]


def first_frames(ids, pair, weight):
    rows = sds(pair.shape[1:], BF)
    half = sds((pair.shape[1] // 2, pair.shape[2]), BF)
    block, part = call(outgoing_kernel, [rows, half], [ids, pair], "outgoing", 1_000_000)
    mine = lax.ppermute(block, ("section", "shard"), split_pairs(1, 2))
    half_mine = xor_pass(part, "shard", 3)
    parts = shard_spread(weight)
    mine, half_mine = after([mine, half_mine], *parts[1:])
    other, half_other = (xor_pass(got, "section", 1) for got in (mine, half_mine))
    frames = call(
        arrange_kernel,
        [rows] * 4,
        [ids, pair, mine, other, half_mine, half_other],
        "arrange",
        1_000_000,
    )
    return block, list(frames), both_cores(parts)


def to_clip(ids, present, pair):
    count = lax.axis_size("shard")
    pairs = [((i >> 1) * count + i, (i >> 1) * count + (i ^ 2)) for i in range(count)]
    rows = sds(pair.shape[1:], BF)
    (away,) = call(away_kernel, [rows], [ids, pair], "away", 1_000_000)
    got = lax.ppermute(away, ("section", "shard"), pairs)
    (home,) = call(
        home_kernel,
        [rows],
        [ids, present, pair, got],
        "home",
        1_000_000,
        scalars=2,
    )
    return home


def from_clip(ids, pair):
    count = lax.axis_size("shard")

    def pairs(flip):
        out = []
        for sec in range(2):
            for i in range(count):
                clip, low = i >> 1, i & 1
                out.append((sec * count + i, (clip ^ flip) * count + sec * 2 + low))
        return out

    both = ("section", "shard")
    rows = sds(pair[0].shape, BF)
    same, swap = call(order_kernel, [rows, rows], [ids, *pair], "order", 1_000_000)
    return lax.ppermute(same, both, pairs(0)), lax.ppermute(swap, both, pairs(1))


def clips_of(ids, same, swap):
    out = sds((1, 1, 2) + same.shape, BF)
    return call(clips_kernel, [out], [ids, same, swap], "clips", 1_000_000)[0]


def section_sum(parts, stepped, ties):
    args, outs = [], []
    for keep, *send in parts:
        rows = keep.shape[1]
        args += [keep, *(xor_pass(part, "section", 1) for part in send)]
        outs.append(sds((rows, HALF), F32))
        if stepped:
            outs += [sds((2, rows, HALF), BF), sds((rows, HALF), F32)]
        else:
            outs += [sds((rows, HALF), BF)] * 3
    sums = call(
        functools.partial(section_sum_kernel, stepped),
        outs,
        args,
        "section_sum",
        1_000_000,
        scalars=0,
        ties=ties,
    )
    per = len(outs) // len(parts)
    return [sums[i * per : (i + 1) * per] for i in range(len(parts))]


def split_pairs(low, high):
    count = lax.axis_size("shard")
    return [(i, i ^ low) for i in range(count)] + [
        (count + i, count + (i ^ high)) for i in range(count)
    ]


def shard_first(first_out, low):
    return lax.ppermute(first_out, ("section", "shard"), split_pairs(low, 3 - low))


def shard_second(second_out, got, low, ties):
    (message,) = call(
        second_kernel,
        [sds(second_out.shape, BF)],
        [second_out, got],
        "second",
        1_000_000,
        scalars=0,
        ties=ties,
    )
    return lax.ppermute(message, ("section", "shard"), split_pairs(3 - low, low))


def replica_sum(ids, parts, ties):
    size = lax.axis_size("replica")
    rows = D // SHARDS // size
    groups = [(part[1].shape[0] - part[0]) // (D // SHARDS) for part in parts]
    if size > SHARDS:
        pieces = []
        for (fixed, *terms), count in zip(parts, groups):
            summed = sum((t[0] if t.ndim == 3 else t).astype(F32) for t in terms)
            blocks = summed[: count * size * rows].reshape(count, size, rows, HALF)
            blocks = blocks.transpose(1, 0, 2, 3).reshape(size, count * rows, HALF)
            mine = lax.psum_scatter(blocks.astype(BF), "replica", scatter_dimension=0)
            pieces.append(mine.astype(F32))
            if fixed:
                pieces.append(lax.psum(summed[count * size * rows :], "replica"))
        return jnp.concatenate(pieces, axis=0)
    count = sum(groups) * rows + sum(part[0] for part in parts)
    own, *messages = call(
        functools.partial(spread_kernel, groups, len(parts[0]) - 1),
        [sds((count, HALF), F32)] + [sds((count, HALF), BF)] * (size - 1),
        [ids] + [array for part in parts for array in part[1:]],
        "spread",
        1_000_000,
        ties=ties,
    )
    for k, message in enumerate(messages):
        own = own + xor_pass(message, "replica", k + 1).astype(F32)
    return own


def local(
    inputs,
    cotangent,
    clip_present,
    qkv_weight,
    out_weight,
    up_weight,
    down_weight,
    norm_gains,
    biases,
    up_bias,
):
    section = lax.axis_index("section")
    shard = lax.axis_index("shard")
    replica = lax.axis_index("replica")
    replicas = lax.axis_size("replica")
    first = section == 0
    rows = inputs.shape[2]
    place = replica * SHARDS + shard
    ids = jnp.stack([shard, section, place, replica]).astype(jnp.int32)
    own_rows = D // SHARDS

    arrived, frames, qkv_part = first_frames(ids, inputs[0], qkv_weight[0])

    (late,) = after([cotangent[0]], arrived)
    gout_last = to_clip(ids, clip_present, late)

    half_rows = own_rows // 2
    packed = sds((half_rows, 9 * D), BF)
    stay, swap = call(
        pack_kernel,
        [packed, packed],
        [ids, out_weight[0], up_weight[0], down_weight[0]],
        "pack",
        1_000_000,
        raw=3,
        ties=(arrived,),
        scratch=[pltpu.SemaphoreType.DMA((12,))],
    )
    got = xor_pass(swap, "section", 1)
    (small,) = call(
        small_kernel,
        [sds((16, D), F32)],
        [norm_gains[0], biases[0], up_bias[0][None]],
        "small",
        1_000_000,
        scalars=0,
        ties=(arrived,),
    )
    other_small = xor_pass(small, "section", 1)
    both = sds((16, D), F32)
    small_layers = call(
        pick_kernel, [both, both], [ids, small, other_small], "small_pick", 1_000_000
    )
    rest_zero, rest_one = call(
        pick_kernel, [packed, packed], [ids, stay, got], "pick", 1_000_000,
        ties=(*qkv_part[1:4], gout_last),
    )
    rest_part = shard_spread(rest_zero)

    whole = SHARDS * rows
    saved = []
    outs = []
    for layer in range(2):
        small = small_layers[layer]
        w_qkv, xhat, q, k, v, lse, mixed = call(
            functools.partial(attend_kernel, layer),
            [
                sds((D, 3 * D), BF),
                sds((whole, D), BF),
                sds((rows, D), BF),
                sds((whole, D), BF),
                sds((whole, D), BF),
                sds((8, rows), F32),
                sds((rows, D), BF),
            ],
            [ids, *frames, *qkv_part, small],
            "attend",
            4_000_000_000,
        )
        if layer == 0:
            last_parts = shard_steps(after([rest_one], mixed)[0])
            rest_part = both_cores([rest_part[0], *after(rest_part[1:], mixed)])
        else:
            rest_part = both_cores([last_parts[0], *after(last_parts[1:], mixed)])
        out, resid, z, slope, w_out, w_up, w_down = call(
            functools.partial(mlp_kernel, layer == 1),
            [
                sds((rows, D), BF),
                sds((rows, D), F32),
                sds((rows, FF), BF),
                sds((rows, FF), BF),
                sds((D, D), BF),
                sds((D, FF), BF),
                sds((FF, D), BF),
            ],
            [ids, clip_present, frames[0], mixed, *rest_part, small],
            "mlp",
            2_000_000_000,
            scalars=2,
        )
        saved.append(
            (frames[0], w_qkv, xhat, q, k, v, lse, mixed, resid, z, slope, w_out, w_up, w_down)
        )
        outs.append(out)
        if layer == 0:
            frames = clip_frames(out)
            last_parts = shard_steps_end(*last_parts, frames[2])

    outs_back = from_clip(ids, outs)
    gout = gout_last
    shares = [None, None]
    grads = [None, None]
    before = ()
    for layer in (1, 0):
        small = small_layers[layer]
        x0, w_qkv, xhat, q, k, v, lse, mixed, resid, z, slope, w_out, w_up, w_down = saved[layer]
        dresid, ga, du, c, dmixed, vec_two, upvec = call(
            mlp_back_kernel,
            [
                sds((rows, D), F32),
                sds((rows, D), BF),
                sds((rows, FF), BF),
                sds((rows, D), BF),
                sds((rows, D), BF),
                sds((8, D), F32),
                sds((1, FF), F32),
            ],
            [gout, z, slope, resid, w_out, w_up, w_down, small],
            "mlp_back",
            2_000_000_000,
            scalars=0,
        )
        da_own, da_near, da_swap, dq, dkv, vec_one = call(
            attend_back_kernel,
            [
                sds((rows, D), F32),
                sds((rows, D), F32),
                sds((2, rows, D), BF),
                sds((rows, D), BF),
                sds((whole, 2 * D), BF),
                sds((8, D), F32),
            ],
            [q, k, v, lse, mixed, dmixed, xhat, w_qkv],
            "attend_back",
            8_000_000_000,
            scalars=0,
            ties=before,
        )
        got = xor_pass(da_swap, "section", 1)
        near = (da_near + got[1].astype(F32)).astype(BF)
        back = xor_pass(near, "shard", 1)
        counts = [3 * own_rows + VEC_ROWS]
        if layer == 0:
            counts = [2 * own_rows, own_rows + VEC_ROWS]
        shapes = []
        for count in counts:
            shapes += [sds((SHARDS, count, HALF), BF)] + [sds((2, count, HALF), BF)] * 2
        parts = call(
            functools.partial(grad_kernel, replicas, layer),
            shapes,
            [ids, c, du, z, gout, xhat, dq, dkv, mixed, ga, small, vec_one, vec_two, upvec],
            "grad",
            4_000_000_000,
            ties=(near,) if layer == 1 else (),
        )
        if layer == 1:
            keep, *send = parts
            parts = [(keep, *after(send, back, *outs_back))]
            ((own, first_out, second_out),) = section_sum(parts, True, ())
            before = (first_out,)
        else:
            parts = section_sum((parts[:3], parts[3:]), False, (back, late))
        (gin,) = call(
            norm_back_kernel,
            [sds((rows, D), BF)],
            [da_own, got, back, x0, dresid, small],
            "norm_back",
            100_000_000,
            scalars=0,
        )
        grads[layer] = gin
        gout = gin
        if layer == 1:
            got = shard_first(first_out, 1)
            late = shard_second(second_out, got, 1, ())
            shares[1] = replica_sum(ids, [(VEC_ROWS, own, got, late)], ())
        else:
            sums = []
            for (own, *messages), fixed in zip(parts, (0, VEC_ROWS)):
                gots = [xor_pass(m, "shard", k + 1) for k, m in enumerate(messages)]
                sums.append((fixed, own, *gots))
            shares[0] = [
                replica_sum(ids, sums[:1], (shares[1],)), replica_sum(ids, sums[1:], ())
            ]

    outputs_local = clips_of(ids, *outs_back)
    grads_local = clips_of(ids, *from_clip(ids, grads))
    n = own_rows // replicas
    (away,) = call(
        functools.partial(choose_kernel, n),
        [sds((3 * n, HALF), F32)],
        [ids, *shares[0], shares[1]],
        "choose",
        1_000_000,
        ties=(outputs_local, grads_local),
    )
    got = xor_pass(away, "section", 1)
    qkv_grad, out_grad, up_grad, down_grad, gain, bias, up_vec = call(
        finish_kernel,
        [
            sds((1, n, 3 * D), F32),
            sds((1, n, D), F32),
            sds((1, n, FF), F32),
            sds((1, 4 * n, D), F32),
            sds((1, 2, n), F32),
            sds((1, 6, n), F32),
            sds((1, 4 * n), F32),
        ],
        [ids, *shares[0], shares[1], got],
        "finish",
        1_000_000,
    )
    return (
        outputs_local,
        grads_local,
        qkv_grad,
        out_grad,
        up_grad,
        down_grad,
        gain,
        bias,
        up_vec,
    )


def solution(mesh):
    return jax.shard_map(
        local,
        mesh=mesh,
        in_specs=(
            P("replica", None, "shard", None),
            P("replica", None, "shard", None),
            P("replica", None),
            P("section", "shard", None),
            P("section", "shard", None),
            P("section", "shard", None),
            P("section", "shard", None),
            P("section", None, None),
            P("section", None, None),
            P("section", None),
        ),
        out_specs=(
            P("section", "replica", None, "shard", None),
            P("section", "replica", None, "shard", None),
            P("section", ("replica", "shard"), None),
            P("section", ("replica", "shard"), None),
            P("section", ("replica", "shard"), None),
            P("section", ("replica", "shard"), None),
            P("section", None, ("replica", "shard")),
            P("section", None, ("replica", "shard")),
            P("section", ("replica", "shard")),
        ),
        check_vma=False,
    )
```

```python
import functools

import jax
import jax.numpy as jnp
from jax import lax
from jax.experimental import pallas as pl
from jax.experimental.pallas import tpu as pltpu
from jax.sharding import PartitionSpec as P

D = 384
HEADS = 6
HEAD_DIM = 64
FF = 1536
PAIR = 2 * HEAD_DIM
HALF = 768
SHARDS = 4
BF = jnp.bfloat16
F32 = jnp.float32
VEC_ROWS = 16
COST = 1000
LARGEST_SUM = 1e30

NT = (((1,), (1,)), ((), ()))
TN = (((0,), (0,)), ((), ()))


def dot(left, right, dims=(((1,), (0,)), ((), ()))):
    return lax.dot_general(left, right, dims, preferred_element_type=F32)


def xor_pass(x, axis, by):
    pairs = [(i, i ^ by) for i in range(lax.axis_size(axis))]
    return lax.ppermute(x, axis, pairs)


def call(kernel, outs, args, name, flops, scalars=1, ties=(), raw=0, scratch=()):
    smem = pl.BlockSpec(memory_space=pltpu.SMEM)
    vmem = pl.BlockSpec(memory_space=pltpu.VMEM)
    apart = pl.BlockSpec(memory_space=pl.ANY)
    size = sum(a.size * a.dtype.itemsize for a in args)
    size += sum(o.size * o.dtype.itemsize for o in outs)
    count = len(args)

    def body(*refs):
        kernel(*refs[:count], *refs[count + len(ties) :])

    return pl.pallas_call(
        body,
        out_shape=outs,
        in_specs=[smem] * scalars
        + [vmem] * (count - scalars - raw)
        + [apart] * (raw + len(ties)),
        out_specs=[vmem] * len(outs),
        scratch_shapes=list(scratch),
        compiler_params=pltpu.CompilerParams(vmem_limit_bytes=20 * 1024 * 1024),
        cost_estimate=pl.CostEstimate(
            flops=flops // COST, bytes_accessed=size // COST, transcendentals=0
        ),
        name=name,
    )(*args, *ties)


def after(arrays, *ties):
    apart = pl.BlockSpec(memory_space=pl.ANY)
    count = len(arrays)
    return pl.pallas_call(
        lambda *refs: None,
        out_shape=[jax.ShapeDtypeStruct(x.shape, x.dtype) for x in arrays],
        in_specs=[apart] * (count + len(ties)),
        out_specs=[apart] * count,
        input_output_aliases={i: i for i in range(count)},
        compiler_params=pltpu.CompilerParams(vmem_limit_bytes=1024 * 1024),
        name="after",
    )(*arrays, *ties)


def sds(shape, dtype):
    return jax.ShapeDtypeStruct(shape, dtype)


def normed(values):
    center = values - jnp.mean(values, axis=-1, keepdims=True)
    spread = jnp.mean(center * center, axis=-1, keepdims=True)
    rstd = lax.rsqrt(spread + 1e-05)
    return center * rstd, rstd


def norm_back(d, xhat, rstd, gain):
    dg = d * gain
    first = jnp.mean(dg, axis=-1, keepdims=True)
    second = jnp.mean(dg * xhat, axis=-1, keepdims=True)
    return rstd * (dg - first - xhat * second)


def col_sum(values):
    return jnp.sum(values, axis=0, keepdims=True)


def half_mask(rows, half):
    lane = lax.broadcasted_iota(jnp.int32, (rows, PAIR), 1)
    return (lane >= HEAD_DIM) if half else (lane < HEAD_DIM)


def held_rows(ids, parts, stepped):
    me, section = ids[0], ids[1]
    for side in range(2):
        half = section ^ side
        by = (0, 1 + half, 2 - half, 3) if stepped else (0, 1, 2, 3)
        for k, part in zip(by, parts[side]):
            yield (me ^ k) * 2 + half, part


def place_rows(ids, full_ref, parts, stepped, first_col):
    width = full_ref.shape[1]
    for place, part in held_rows(ids, parts, stepped):
        rows = part.shape[0]
        at = pl.multiple_of(place * rows, rows)
        full_ref[pl.ds(at, rows), :] = part[:, first_col : first_col + width]


def pack_kernel(ids, out, up, down, stay_ref, swap_ref, sems):
    section = ids[1]
    rows = out.shape[0] // 2
    copies = []

    def move(source, target):
        copy = pltpu.make_async_copy(source, target, sems.at[len(copies)])
        copy.start()
        copies.append(copy)

    for half, ref in ((1 - section, swap_ref), (section, stay_ref)):
        at = pl.ds(pl.multiple_of(half * rows, rows), rows)
        move(out.at[at, :], ref.at[:, :D])
        move(up.at[at, :], ref.at[:, D : D + FF])
        for j in range(4):
            at = pl.ds(pl.multiple_of(half * (4 * rows) + j * rows, rows), rows)
            move(down.at[at, :], ref.at[:, D + FF + j * D : D + FF + (j + 1) * D])
    for copy in copies:
        copy.wait()


def small_kernel(gains, biases, up_b, small_ref):
    bias = up_b[...]
    small_ref[...] = jnp.concatenate(
        [gains[...], biases[...]]
        + [bias[:, j * D : (j + 1) * D] for j in range(4)]
        + [jnp.zeros((4, D), F32)],
        axis=0,
    )


def pick_kernel(ids, stay, got, zero_ref, one_ref):
    first = ids[1] == 0
    here, there = stay[...], got[...]
    zero_ref[...] = jnp.where(first, here, there)
    one_ref[...] = jnp.where(first, there, here)


def outgoing_kernel(ids, pair, gouts, block_ref, half_ref):
    section = ids[1]
    low = ids[0] < 2
    here = jnp.where(low, pair[0], pair[1])
    there = jnp.where(low, pair[1], pair[0])
    block_ref[0] = jnp.where(section == 0, here, there)
    block_ref[1] = jnp.where(low, gouts[1], gouts[0])
    cut = half_ref.shape[0]
    half_ref[...] = jnp.where(section == 0, there[:cut], there[cut:])


def arrange_kernel(
    ids, present, pair, gouts, mine, other, half_mine, half_other, own, core, near, across, gout
):
    section = ids[1]
    first = section == 0
    local = jnp.where(ids[0] < 2, pair[0], pair[1])
    beside = jnp.where(first, mine[0], other[0])
    far = jnp.where(first, other[0], mine[0])
    top, bottom = half_mine[...], half_other[...]
    diagonal = jnp.concatenate(
        [jnp.where(first, top, bottom), jnp.where(first, bottom, top)], axis=0
    )
    home = section == ids[0] >> 1
    own[...] = jnp.where(home, local, far)
    core[...] = jnp.where(home, far, local)
    near[...] = jnp.where(home, beside, diagonal)
    across[...] = jnp.where(home, diagonal, beside)
    mask = present[0, ids[0] >> 1].astype(F32)
    far = jnp.where(first, other[1], mine[1])
    local = jnp.where(ids[0] < 2, gouts[0], gouts[1])
    gout[...] = (jnp.where(home, local, far).astype(F32) * mask).astype(BF)


def order_kernel(ids, zero, one, same_ref, swap_ref):
    low = ids[0] < 2
    same_ref[...] = jnp.where(low, zero[...], one[...])
    swap_ref[...] = jnp.where(low, one[...], zero[...])


def clips_kernel(ids, same, swap, out_ref):
    first = ids[1] == 0
    out_ref[0, 0, 0] = jnp.where(first, same[...], swap[...])
    out_ref[0, 0, 1] = jnp.where(first, swap[...], same[...])


def choose_kernel(n, ids, mlp, attn, both, out_ref):
    first = ids[1] == 0
    out_ref[: 2 * n, :] = jnp.where(first, both[: 2 * n, :], mlp[...])
    out_ref[2 * n :, :] = jnp.where(first, both[2 * n : 3 * n, :], attn[:n, :])


def section_sum_kernel(stepped, *refs):
    parts = len(refs) // (6 if stepped else 7)
    outs = refs[3 * parts :]
    per = len(outs) // parts
    for part in range(parts):
        keep, got_one, got_two = refs[3 * part : 3 * part + 3]
        own_ref, *others = outs[per * part : per * part + per]
        sums = [
            keep[e].astype(F32) + (got_one, got_two)[e // 2][e % 2].astype(F32) for e in range(4)
        ]
        own_ref[...] = sums[0]
        if stepped:
            others[0][0] = sums[1].astype(BF)
            others[0][1] = sums[2].astype(BF)
            others[1][...] = sums[3]
        else:
            for ref, total in zip(others, sums[1:]):
                ref[...] = total.astype(BF)


def second_kernel(second, got, out_ref):
    out_ref[...] = (second[...] + got[1].astype(F32)).astype(BF)


def spread_kernel(groups, terms, ids, *refs):
    count = len(groups)
    outs = refs[terms * count :]
    size = len(outs)
    rows = D // SHARDS // size
    me = ids[3]
    base = 0
    for part in range(count):
        total = refs[terms * part][...]
        for ref in refs[terms * part + 1 : terms * part + terms]:
            total = total + (ref[0] if len(ref.shape) == 3 else ref[...]).astype(F32)
        end = base + groups[part] * rows
        tail = total[groups[part] * size * rows :, :]
        if tail.shape[0]:
            for ref in outs:
                ref[end : end + tail.shape[0], :] = tail.astype(ref.dtype)
        for r in range(size):
            block = jnp.concatenate(
                [
                    total[(g * size + r) * rows : (g * size + r + 1) * rows, :]
                    for g in range(groups[part])
                ],
                axis=0,
            )
            for k, ref in enumerate(outs):

                @pl.when(me ^ k == r)
                def _():
                    ref[base:end, :] = block.astype(ref.dtype)

        base = end + tail.shape[0]


def finish_kernel(
    ids, mlp_zero, attn_zero, both_one, got,
    qkv, out, up, down, gain, bias, up_vec,
):
    first = ids[1] == 0

    def sides(zero, one, other):
        own = jnp.where(first, zero, one)
        return jnp.where(first, own, other), jnp.where(first, other, own)

    n = mlp_zero.shape[0] // 2
    low, high = sides(mlp_zero[...], both_one[: 2 * n, :], got[: 2 * n, :])
    up[0, :, :HALF] = low[:n]
    up[0, :, HALF:] = high[:n]
    for t, side in enumerate((low, high)):
        for j in range(2):
            at = (2 * t + j) * n
            down[0, at : at + n, :] = side[n:, j * D : (j + 1) * D]
    low, high = sides(attn_zero[:n, :], both_one[2 * n : 3 * n, :], got[2 * n :, :])
    qkv[0, :, :HALF] = low
    qkv[0, :, HALF:] = high[:, :D]
    out[0] = high[:, D:]
    vec_zero, vec_one = attn_zero[n:, :], both_one[3 * n :, :]
    sums = jnp.where(first, vec_zero, vec_one)

    def taken(values, width):
        length = values.shape[1]
        turn = lax.rem(length - ids[2] * width, length)
        return pltpu.roll(values, turn, 1)[:, :width]

    rows = []
    for r in range(4):
        rows += [sums[r : r + 1, :D], sums[r : r + 1, D:]]
    vec = taken(jnp.concatenate(rows, axis=0), n)
    gain[0] = vec[:2]
    bias[0] = vec[2:]
    both = jnp.concatenate([sums[4:5], sums[5:6]], axis=1)
    up_vec[...] = taken(jnp.broadcast_to(both, (8, FF)), 4 * n)[:1]


def attend_kernel(
    layer, ids, x0, x1, x2, x3, w0, w1, w2, w3, o0, o1, o2, o3, small,
    w_ref, xhat_ref, q_ref, k_ref, v_ref, lse_ref, mixed_ref,
):
    me = ids[0]
    rows = x0.shape[0]
    own_layer = ids[1] == layer
    for k, (own, other) in enumerate(((w0, o0), (w1, o1), (w2, o2), (w3, o3))):
        count = own.shape[0]
        at = pl.multiple_of((me ^ k) * count, count)
        w_ref[pl.ds(at, count), :] = jnp.where(own_layer, own[...], other[...])
    gains, biases = small[0:2, :], small[2:8, :]
    gain, shift = gains[0:1, :], biases[0:1, :]
    for r, x in enumerate((x0, x1, x2, x3)):
        xhat, unused = normed(x[...].astype(F32))
        xhat_ref[r * rows : (r + 1) * rows, :] = xhat.astype(BF)
        a = (xhat * gain + shift).astype(BF)
        if r == 0:
            q = (dot(a, w_ref[:, :D]) + biases[1:2, :]).astype(BF)
            q_ref[...] = (q.astype(F32) * (HEAD_DIM ** (-0.5))).astype(BF)
        kv = dot(a, w_ref[:, D:])
        k_ref[r * rows : (r + 1) * rows, :] = kv[:, :D].astype(BF)
        v_ref[r * rows : (r + 1) * rows, :] = (kv[:, D:] + biases[2:3, :]).astype(BF)

    def one_pair(sample, pair, worst):
        cols = pl.ds(pl.multiple_of(pair * PAIR, PAIR), PAIR)
        k_pair = k_ref[:, cols]
        v_t = v_ref[:, cols].T
        q_pair = q_ref[:, cols].astype(F32)
        mixed_t = []
        for half in range(2):
            qm = jnp.where(half_mask(rows, half), q_pair, 0.0).astype(BF)
            s = dot(k_pair, qm, NT)
            top = jnp.max(s[:sample], axis=0, keepdims=True)
            e = jnp.exp(s - top)
            total = jnp.sum(e, axis=0, keepdims=True)
            worst = jnp.maximum(worst, total)
            lse_ref[pl.ds(2 * pair + half, 1), :] = top + jnp.log(total)
            o = dot(v_t[half * HEAD_DIM : (half + 1) * HEAD_DIM, :], e.astype(BF))
            mixed_t.append(o * (1.0 / total))
        mixed_ref[:, cols] = jnp.concatenate(mixed_t, axis=0).T.astype(BF)
        return worst

    keys = k_ref.shape[0]
    start = jnp.zeros((1, rows), F32)
    worst = lax.fori_loop(
        0, HEADS // 2, functools.partial(one_pair, keys // 4), start, unroll=True
    )

    @pl.when(jnp.max(worst) > LARGEST_SUM)
    def _():
        lax.fori_loop(0, HEADS // 2, functools.partial(one_pair, keys), start)


def mlp_kernel(stepped, ids, present, x0, mixed, *refs):
    out_ref, resid_ref, z_ref, slope_ref, wo_ref, w1_ref, w2_ref = refs[-7:]
    small = refs[-8]
    count = (len(refs) - 8) // 2
    parts = [refs[:count], refs[count : 2 * count]]
    if stepped:
        parts = [(own, got, pair.at[0], pair.at[1]) for own, got, pair in parts]
    place_rows(ids, wo_ref, parts, stepped, 0)
    place_rows(ids, w1_ref, parts, stepped, D)
    for place, part in held_rows(ids, parts, stepped):
        rows = part.shape[0]
        for j in range(4):
            at = pl.multiple_of((place * 4 + j) * rows, rows)
            left = D + FF + j * D
            w2_ref[pl.ds(at, rows), :] = part[:, left : left + D]
    gains, biases = small[0:2, :], small[2:8, :]
    up_b = jnp.concatenate([small[8 + j : 9 + j, :] for j in range(4)], axis=1)
    resid = x0[...].astype(F32) + (dot(mixed[...], wo_ref[...]) + biases[3:4, :])
    resid_ref[...] = resid
    xhat, unused = normed(resid)
    c = (xhat * gains[1:2, :] + biases[4:5, :]).astype(BF)
    upper = dot(c, w1_ref[...]) + up_b
    phi = 0.5 * (1.0 + lax.erf(upper * (2.0 ** -0.5)))
    z = (upper * phi).astype(BF)
    z_ref[...] = z
    bell = jnp.exp(-0.5 * upper * upper) * 0.3989422804014327
    slope_ref[...] = (phi + upper * bell).astype(BF)
    out = resid + (dot(z, w2_ref[...]) + biases[5:6, :])
    out_ref[...] = (out * present[0, ids[0] >> 1].astype(F32)).astype(BF)


def mlp_back_kernel(
    gout, z, slope, resid, wo, w1, w2, small,
    dresid_ref, ga_ref, du_ref, c_ref, dmixed_ref, vec_ref, upvec_ref,
):
    gains, biases = small[0:2, :], small[2:8, :]
    gm = gout[...]
    dz = dot(gm, w2[...], NT)
    du = (dz * slope[...].astype(F32)).astype(BF)
    du_ref[...] = du
    dc = dot(du, w1[...], NT)
    xhat, rstd = normed(resid[...])
    gain = gains[1:2, :]
    c_ref[...] = (xhat * gain + biases[4:5, :]).astype(BF)
    g_full = gm.astype(F32)
    dresid = g_full + norm_back(dc, xhat, rstd, gain)
    dresid_ref[...] = dresid
    ga = dresid.astype(BF)
    ga_ref[...] = ga
    dmixed_ref[...] = dot(ga, wo[...], NT).astype(BF)
    vec_ref[...] = jnp.concatenate(
        [
            col_sum(dc * xhat),
            col_sum(dc),
            col_sum(ga.astype(F32)),
            col_sum(g_full),
            jnp.zeros((4, D), F32),
        ],
        axis=0,
    )
    upvec_ref[...] = col_sum(du.astype(F32))


def attend_back_kernel(
    q_ref, k_ref, v_ref, lse, mixed, dmixed, xhat_ref, w_ref,
    own_ref, near_ref, swap_ref, dq_ref, dkv_ref, vec_ref,
):
    rows = q_ref.shape[0]

    def one_pair(pair, carry):
        cols = pl.ds(pl.multiple_of(pair * PAIR, PAIR), PAIR)
        k_pair, v_pair = k_ref[:, cols], v_ref[:, cols]
        k_t = k_pair.T
        q_pair = q_ref[:, cols].astype(F32)
        do_pair = dmixed[:, cols].astype(F32)
        prod_t = (mixed[:, cols].astype(F32) * do_pair).T
        dq_t, ps, dss, qms, doms = [], [], [], [], []
        for half in range(2):
            keep = half_mask(rows, half)
            qm = jnp.where(keep, q_pair, 0.0).astype(BF)
            dom = jnp.where(keep, do_pair, 0.0).astype(BF)
            p = jnp.exp(dot(k_pair, qm, NT) - lse[pl.ds(2 * pair + half, 1), :])
            dp = dot(v_pair, dom, NT)
            delta = col_sum(prod_t[half * HEAD_DIM : (half + 1) * HEAD_DIM, :])
            ds = (p * (dp - delta)).astype(BF)
            dq_t.append(
                dot(k_t[half * HEAD_DIM : (half + 1) * HEAD_DIM, :], ds) * (HEAD_DIM ** (-0.5))
            )
            ps.append(p.astype(BF))
            dss.append(ds)
            qms.append(qm)
            doms.append(dom)
        dkv_ref[:, cols] = dot(
            jnp.concatenate(dss, axis=1), jnp.concatenate(qms, axis=0)
        ).astype(BF)
        dkv_ref[:, pl.ds(pl.multiple_of(D + pair * PAIR, PAIR), PAIR)] = dot(
            jnp.concatenate(ps, axis=1), jnp.concatenate(doms, axis=0)
        ).astype(BF)
        dq_ref[:, cols] = jnp.concatenate(dq_t, axis=0).T.astype(BF)
        return carry

    lax.fori_loop(0, HEADS // 2, one_pair, 0)
    dq = dq_ref[...]
    gain_sum = jnp.zeros((1, D), F32)
    shift_sum = jnp.zeros((1, D), F32)
    outs = (own_ref, swap_ref.at[0], near_ref, swap_ref.at[1])
    for r, da_ref in enumerate(outs):
        at = slice(r * rows, (r + 1) * rows)
        da = dot(dkv_ref[at, :], w_ref[:, D:], NT)
        if r == 0:
            da = da + dot(dq, w_ref[:, :D], NT)
        gain_sum = gain_sum + col_sum(da * xhat_ref[at, :].astype(F32))
        shift_sum = shift_sum + col_sum(da)
        da_ref[...] = da.astype(da_ref.dtype)
    vec_ref[...] = jnp.concatenate(
        [
            gain_sum,
            shift_sum,
            col_sum(dq.astype(F32)),
            col_sum(dkv_ref[:, D:].astype(F32)),
            jnp.zeros((4, D), F32),
        ],
        axis=0,
    )


def norm_back_kernel(da_own, da_core, da_near, x0, dresid, small, out_ref):
    da = da_own[...] + da_core[0].astype(F32) + da_near[...].astype(F32)
    xhat, rstd = normed(x0[...].astype(F32))
    out_ref[...] = (dresid[...] + norm_back(da, xhat, rstd, small[0:1, :])).astype(BF)


def regroup(grad, s, replicas):
    rows = grad.shape[0] // (replicas * SHARDS)
    pieces = []
    for r in range(replicas):
        start = (r * SHARDS + s) * rows
        pieces.append(grad[start : start + rows, :])
    return pieces


def slot_of(ids, s, side):
    by = ids[0] ^ s
    if side is None:
        return by
    turned = jnp.where(side == 0, by, ((by & 1) << 1) | (by >> 1))
    return turned ^ (turned >> 1)


def put(refs, slot, at, block):
    @pl.when(slot < 2)
    def _():
        refs[0][slot, at, :] = block

    @pl.when(slot >= 2)
    def _():
        refs[1][slot - 2, at, :] = block


def grad_kernel(
    replicas, layer, ids, c, du, z, gm, xhat, dq, dkv, mixed, ga, small, vec_one, vec_two,
    upvec, *outs,
):
    section = ids[1]
    first = section == 0
    base = D // SHARDS
    start_of = 2 * base if layer == 1 else 0
    side = section if layer == 1 else None

    def store(refs, s, at, own, other):
        keep_ref, *send_refs = refs
        keep_ref[slot_of(ids, s, side), at, :] = own.astype(BF)
        away = None if side is None else 1 - side
        put(send_refs, slot_of(ids, s, away), at, other.astype(BF))

    def store_halves(refs, grad, at):
        left, right = grad[:, :HALF], grad[:, HALF:]
        own = jnp.where(first, left, right)
        other = jnp.where(first, right, left)
        for s in range(SHARDS):
            blocks = [
                jnp.concatenate(regroup(half, s, replicas), axis=0) for half in (own, other)
            ]
            store(refs, s, at, *blocks)

    store_halves(outs[:3], dot(c[...], du[...], TN), slice(0, base))
    grad = dot(z[...], gm[...], TN)
    rows = FF // (replicas * SHARDS)
    sub = rows // 4
    for s in range(SHARDS):
        sides = ([], [])
        for r in range(replicas):
            start = (r * SHARDS + s) * rows
            parts = [grad[start + j * sub : start + (j + 1) * sub, :] for j in range(4)]
            sides[0].append(jnp.concatenate(parts[:2], axis=1))
            sides[1].append(jnp.concatenate(parts[2:], axis=1))
        low, high = (jnp.concatenate(side, axis=0) for side in sides)
        own, other = jnp.where(first, low, high), jnp.where(first, high, low)
        store(outs[:3], s, slice(base, 2 * base), own, other)
    count = dq.shape[0]
    a = (xhat[...].astype(F32) * small[0:1, :] + small[2:3, :]).astype(BF)
    grad = jnp.concatenate(
        [
            dot(a[:count, :], dq[...], TN),
            dot(a, dkv[...], TN),
            dot(mixed[...], ga[...], TN),
        ],
        axis=1,
    )
    store_halves(outs[-3:], grad, slice(start_of, start_of + base))
    one, two, up = vec_one[...], vec_two[...], upvec[...]

    def wide(left, right):
        return jnp.concatenate([left, right], axis=1)

    vec = jnp.concatenate(
        [
            wide(one[0:1], two[0:1]),
            wide(one[1:2], one[2:3]),
            wide(one[3:4], two[2:3]),
            wide(two[1:2], two[3:4]),
            up[:, :HALF],
            up[:, HALF:],
            jnp.zeros((VEC_ROWS - 6, HALF), F32),
        ],
        axis=0,
    ).astype(BF)
    at = slice(start_of + base, start_of + base + VEC_ROWS)
    for s in range(SHARDS):
        outs[-3][s, at, :] = vec
        outs[-2 + s // 2][s % 2, at, :] = vec


def shard_spread(block):
    return [block] + [xor_pass(block, "shard", k) for k in (1, 2, 3)]


def stack_kernel(one, two, out_ref):
    out_ref[0] = one[...]
    out_ref[1] = two[...]


def shard_steps(block):
    return block, lax.ppermute(block, ("section", "shard"), split_pairs(1, 2))


def shard_steps_end(block, got, tie):
    (pair,) = call(
        stack_kernel,
        [sds((2,) + block.shape, BF)],
        [block, got],
        "stack",
        1_000_000,
        scalars=0,
        ties=(tie,),
    )
    return [block, got, lax.ppermute(pair, ("section", "shard"), split_pairs(2, 1))]


def both_cores(parts):
    return [*parts, *(xor_pass(part, "section", 1) for part in parts)]


def clip_frames(own):
    near = xor_pass(own, "shard", 1)
    return [own, xor_pass(own, "section", 1), near, xor_pass(near, "section", 1)]


def first_frames(ids, present, pair, gouts, weight):
    rows = sds(pair.shape[1:], BF)
    half = sds((pair.shape[1] // 2, pair.shape[2]), BF)
    block, part = call(
        outgoing_kernel, [sds(pair.shape, BF), half], [ids, pair, gouts], "outgoing", 1_000_000
    )
    mine = lax.ppermute(block, ("section", "shard"), split_pairs(1, 2))
    half_mine = xor_pass(part, "shard", 3)
    parts = shard_spread(weight)
    mine, half_mine = after([mine, half_mine], *parts[1:])
    other, half_other = (xor_pass(got, "section", 1) for got in (mine, half_mine))
    *frames, gout = call(
        arrange_kernel,
        [rows] * 5,
        [ids, present, pair, gouts, mine, other, half_mine, half_other],
        "arrange",
        1_000_000,
        scalars=2,
    )
    return block, frames, gout, both_cores(parts)


def from_clip(ids, pair, ties):
    count = lax.axis_size("shard")

    def pairs(flip):
        out = []
        for sec in range(2):
            for i in range(count):
                clip, low = i >> 1, i & 1
                out.append((sec * count + i, (clip ^ flip) * count + sec * 2 + low))
        return out

    both = ("section", "shard")
    rows = sds(pair[0].shape, BF)
    same, swap = call(order_kernel, [rows, rows], [ids, *pair], "order", 1_000_000, ties=ties)
    return lax.ppermute(same, both, pairs(0)), lax.ppermute(swap, both, pairs(1))


def clips_of(ids, same, swap):
    out = sds((1, 1, 2) + same.shape, BF)
    return call(clips_kernel, [out], [ids, same, swap], "clips", 1_000_000)[0]


def section_sum(parts, stepped, ties):
    args, outs = [], []
    for keep, *send in parts:
        rows = keep.shape[1]
        args += [keep, *(xor_pass(part, "section", 1) for part in send)]
        outs.append(sds((rows, HALF), F32))
        if stepped:
            outs += [sds((2, rows, HALF), BF), sds((rows, HALF), F32)]
        else:
            outs += [sds((rows, HALF), BF)] * 3
    sums = call(
        functools.partial(section_sum_kernel, stepped),
        outs,
        args,
        "section_sum",
        1_000_000,
        scalars=0,
        ties=ties,
    )
    per = len(outs) // len(parts)
    return [sums[i * per : (i + 1) * per] for i in range(len(parts))]


def split_pairs(low, high):
    count = lax.axis_size("shard")
    return [(i, i ^ low) for i in range(count)] + [
        (count + i, count + (i ^ high)) for i in range(count)
    ]


def shard_first(first_out, low):
    return lax.ppermute(first_out, ("section", "shard"), split_pairs(low, 3 - low))


def shard_second(second_out, got, low, ties):
    (message,) = call(
        second_kernel,
        [sds(second_out.shape, BF)],
        [second_out, got],
        "second",
        1_000_000,
        scalars=0,
        ties=ties,
    )
    return lax.ppermute(message, ("section", "shard"), split_pairs(3 - low, low))


def replica_sum(ids, parts, ties):
    size = lax.axis_size("replica")
    rows = D // SHARDS // size
    groups = [(part[1].shape[0] - part[0]) // (D // SHARDS) for part in parts]
    if size > SHARDS:
        pieces = []
        for (fixed, *terms), count in zip(parts, groups):
            summed = sum((t[0] if t.ndim == 3 else t).astype(F32) for t in terms)
            blocks = summed[: count * size * rows].reshape(count, size, rows, HALF)
            blocks = blocks.transpose(1, 0, 2, 3).reshape(size, count * rows, HALF)
            mine = lax.psum_scatter(blocks.astype(BF), "replica", scatter_dimension=0)
            pieces.append(mine.astype(F32))
            if fixed:
                pieces.append(lax.psum(summed[count * size * rows :], "replica"))
        return jnp.concatenate(pieces, axis=0)
    count = sum(groups) * rows + sum(part[0] for part in parts)
    own, *messages = call(
        functools.partial(spread_kernel, groups, len(parts[0]) - 1),
        [sds((count, HALF), F32)] + [sds((count, HALF), BF)] * (size - 1),
        [ids] + [array for part in parts for array in part[1:]],
        "spread",
        1_000_000,
        ties=ties,
    )
    for k, message in enumerate(messages):
        own = own + xor_pass(message, "replica", k + 1).astype(F32)
    return own


def local(
    inputs,
    cotangent,
    clip_present,
    qkv_weight,
    out_weight,
    up_weight,
    down_weight,
    norm_gains,
    biases,
    up_bias,
):
    section = lax.axis_index("section")
    shard = lax.axis_index("shard")
    replica = lax.axis_index("replica")
    replicas = lax.axis_size("replica")
    first = section == 0
    rows = inputs.shape[2]
    place = replica * SHARDS + shard
    ids = jnp.stack([shard, section, place, replica]).astype(jnp.int32)
    own_rows = D // SHARDS

    ready, frames, gout_last, qkv_part = first_frames(
        ids, clip_present, inputs[0], cotangent[0], qkv_weight[0]
    )


    half_rows = own_rows // 2
    packed = sds((half_rows, 9 * D), BF)
    stay, swap = call(
        pack_kernel,
        [packed, packed],
        [ids, out_weight[0], up_weight[0], down_weight[0]],
        "pack",
        1_000_000,
        raw=3,
        ties=(ready,),
        scratch=[pltpu.SemaphoreType.DMA((12,))],
    )
    got = xor_pass(swap, "section", 1)
    (small,) = call(
        small_kernel,
        [sds((16, D), F32)],
        [norm_gains[0], biases[0], up_bias[0][None]],
        "small",
        1_000_000,
        scalars=0,
        ties=(ready,),
    )
    other_small = xor_pass(small, "section", 1)
    both = sds((16, D), F32)
    small_layers = call(
        pick_kernel, [both, both], [ids, small, other_small], "small_pick", 1_000_000
    )
    rest_zero, rest_one = call(
        pick_kernel, [packed, packed], [ids, stay, got], "pick", 1_000_000,
        ties=(qkv_part[1],),
    )
    rest_part = shard_spread(rest_zero)

    whole = SHARDS * rows
    saved = []
    outs = []
    for layer in range(2):
        small = small_layers[layer]
        w_qkv, xhat, q, k, v, lse, mixed = call(
            functools.partial(attend_kernel, layer),
            [
                sds((D, 3 * D), BF),
                sds((whole, D), BF),
                sds((rows, D), BF),
                sds((whole, D), BF),
                sds((whole, D), BF),
                sds((8, rows), F32),
                sds((rows, D), BF),
            ],
            [ids, *frames, *qkv_part, small],
            "attend",
            4_000_000_000,
            ties=last_other if layer == 1 else (),
        )
        if layer == 0:
            last_parts = shard_steps(after([rest_one], mixed)[0])
            rest_part = both_cores([rest_part[0], *after(rest_part[1:], mixed)])
        else:
            (pair,) = after(last_parts[2:], mixed)
            rest_part = [*last_parts[:2], pair, *last_other, xor_pass(pair, "section", 1)]
        out, resid, z, slope, w_out, w_up, w_down = call(
            functools.partial(mlp_kernel, layer == 1),
            [
                sds((rows, D), BF),
                sds((rows, D), F32),
                sds((rows, FF), BF),
                sds((rows, FF), BF),
                sds((D, D), BF),
                sds((D, FF), BF),
                sds((FF, D), BF),
            ],
            [ids, clip_present, frames[0], mixed, *rest_part, small],
            "mlp",
            2_000_000_000,
            scalars=2,
        )
        saved.append(
            (frames[0], w_qkv, xhat, q, k, v, lse, mixed, resid, z, slope, w_out, w_up, w_down)
        )
        outs.append(out)
        if layer == 0:
            frames = clip_frames(out)
            last_other = tuple(xor_pass(part, "section", 1) for part in last_parts)
            last_parts = shard_steps_end(*last_parts, frames[2])

    gout = gout_last
    shares = [None, None]
    grads = [None, None]
    before = ()
    for layer in (1, 0):
        small = small_layers[layer]
        x0, w_qkv, xhat, q, k, v, lse, mixed, resid, z, slope, w_out, w_up, w_down = saved[layer]
        dresid, ga, du, c, dmixed, vec_two, upvec = call(
            mlp_back_kernel,
            [
                sds((rows, D), F32),
                sds((rows, D), BF),
                sds((rows, FF), BF),
                sds((rows, D), BF),
                sds((rows, D), BF),
                sds((8, D), F32),
                sds((1, FF), F32),
            ],
            [gout, z, slope, resid, w_out, w_up, w_down, small],
            "mlp_back",
            2_000_000_000,
            scalars=0,
        )
        da_own, da_near, da_swap, dq, dkv, vec_one = call(
            attend_back_kernel,
            [
                sds((rows, D), F32),
                sds((rows, D), F32),
                sds((2, rows, D), BF),
                sds((rows, D), BF),
                sds((whole, 2 * D), BF),
                sds((8, D), F32),
            ],
            [q, k, v, lse, mixed, dmixed, xhat, w_qkv],
            "attend_back",
            8_000_000_000,
            scalars=0,
            ties=before,
        )
        got = xor_pass(da_swap, "section", 1)
        near = (da_near + got[1].astype(F32)).astype(BF)
        back = xor_pass(near, "shard", 1)
        counts = [3 * own_rows + VEC_ROWS]
        if layer == 0:
            counts = [2 * own_rows, own_rows + VEC_ROWS]
        shapes = []
        for count in counts:
            shapes += [sds((SHARDS, count, HALF), BF)] + [sds((2, count, HALF), BF)] * 2
        parts = call(
            functools.partial(grad_kernel, replicas, layer),
            shapes,
            [ids, c, du, z, gout, xhat, dq, dkv, mixed, ga, small, vec_one, vec_two, upvec],
            "grad",
            4_000_000_000,
            ties=(near,) if layer == 1 else (),
        )
        if layer == 1:
            keep, *send = parts
            parts = [(keep, *after(send, back))]
            ((own, first_out, second_out),) = section_sum(parts, True, ())
            before = (first_out,)
        else:
            outs_back = from_clip(ids, outs, (da_swap,))
            parts = section_sum((parts[:3], parts[3:]), False, (back, late, *outs_back))
        (gin,) = call(
            norm_back_kernel,
            [sds((rows, D), BF)],
            [da_own, got, back, x0, dresid, small],
            "norm_back",
            100_000_000,
            scalars=0,
        )
        grads[layer] = gin
        gout = gin
        if layer == 1:
            got = shard_first(first_out, 1)
            late = shard_second(second_out, got, 1, ())
            shares[1] = replica_sum(ids, [(VEC_ROWS, own, got, late)], ())
        else:
            sums = []
            for (own, *messages), fixed in zip(parts, (0, VEC_ROWS)):
                gots = [xor_pass(m, "shard", k + 1) for k, m in enumerate(messages)]
                sums.append((fixed, own, *gots))
            shares[0] = [
                replica_sum(ids, sums[:1], (shares[1],)), replica_sum(ids, sums[1:], ())
            ]

    outputs_local = clips_of(ids, *outs_back)
    grads_local = clips_of(ids, *from_clip(ids, grads, ()))
    n = own_rows // replicas
    (away,) = call(
        functools.partial(choose_kernel, n),
        [sds((3 * n, HALF), F32)],
        [ids, *shares[0], shares[1]],
        "choose",
        1_000_000,
        ties=(outputs_local, grads_local),
    )
    got = xor_pass(away, "section", 1)
    qkv_grad, out_grad, up_grad, down_grad, gain, bias, up_vec = call(
        finish_kernel,
        [
            sds((1, n, 3 * D), F32),
            sds((1, n, D), F32),
            sds((1, n, FF), F32),
            sds((1, 4 * n, D), F32),
            sds((1, 2, n), F32),
            sds((1, 6, n), F32),
            sds((1, 4 * n), F32),
        ],
        [ids, *shares[0], shares[1], got],
        "finish",
        1_000_000,
    )
    return (
        outputs_local,
        grads_local,
        qkv_grad,
        out_grad,
        up_grad,
        down_grad,
        gain,
        bias,
        up_vec,
    )


def solution(mesh):
    return jax.shard_map(
        local,
        mesh=mesh,
        in_specs=(
            P("replica", None, "shard", None),
            P("replica", None, "shard", None),
            P("replica", None),
            P("section", "shard", None),
            P("section", "shard", None),
            P("section", "shard", None),
            P("section", "shard", None),
            P("section", None, None),
            P("section", None, None),
            P("section", None),
        ),
        out_specs=(
            P("section", "replica", None, "shard", None),
            P("section", "replica", None, "shard", None),
            P("section", ("replica", "shard"), None),
            P("section", ("replica", "shard"), None),
            P("section", ("replica", "shard"), None),
            P("section", ("replica", "shard"), None),
            P("section", None, ("replica", "shard")),
            P("section", None, ("replica", "shard")),
            P("section", ("replica", "shard")),
        ),
        check_vma=False,
    )
```

```python
import functools

import jax
import jax.numpy as jnp
from jax import lax
from jax.experimental import pallas as pl
from jax.experimental.pallas import tpu as pltpu
from jax.sharding import PartitionSpec as P

D = 384
HEADS = 6
HEAD_DIM = 64
FF = 1536
PAIR = 2 * HEAD_DIM
HALF = 768
SHARDS = 4
BF = jnp.bfloat16
F32 = jnp.float32
VEC_ROWS = 16
COST = 1000
LARGEST_SUM = 1e30

NT = (((1,), (1,)), ((), ()))
TN = (((0,), (0,)), ((), ()))


def dot(left, right, dims=(((1,), (0,)), ((), ()))):
    return lax.dot_general(left, right, dims, preferred_element_type=F32)


def xor_pass(x, axis, by):
    pairs = [(i, i ^ by) for i in range(lax.axis_size(axis))]
    return lax.ppermute(x, axis, pairs)


def call(kernel, outs, args, name, flops, scalars=1, ties=(), raw=0, scratch=()):
    smem = pl.BlockSpec(memory_space=pltpu.SMEM)
    vmem = pl.BlockSpec(memory_space=pltpu.VMEM)
    apart = pl.BlockSpec(memory_space=pl.ANY)
    size = sum(a.size * a.dtype.itemsize for a in args)
    size += sum(o.size * o.dtype.itemsize for o in outs)
    count = len(args)

    def body(*refs):
        kernel(*refs[:count], *refs[count + len(ties) :])

    return pl.pallas_call(
        body,
        out_shape=outs,
        in_specs=[smem] * scalars
        + [vmem] * (count - scalars - raw)
        + [apart] * (raw + len(ties)),
        out_specs=[vmem] * len(outs),
        scratch_shapes=list(scratch),
        compiler_params=pltpu.CompilerParams(vmem_limit_bytes=20 * 1024 * 1024),
        cost_estimate=pl.CostEstimate(
            flops=flops // COST, bytes_accessed=size // COST, transcendentals=0
        ),
        name=name,
    )(*args, *ties)


def after(arrays, *ties):
    apart = pl.BlockSpec(memory_space=pl.ANY)
    count = len(arrays)
    return pl.pallas_call(
        lambda *refs: None,
        out_shape=[jax.ShapeDtypeStruct(x.shape, x.dtype) for x in arrays],
        in_specs=[apart] * (count + len(ties)),
        out_specs=[apart] * count,
        input_output_aliases={i: i for i in range(count)},
        compiler_params=pltpu.CompilerParams(vmem_limit_bytes=1024 * 1024),
        name="after",
    )(*arrays, *ties)


def sds(shape, dtype):
    return jax.ShapeDtypeStruct(shape, dtype)


def normed(values):
    center = values - jnp.mean(values, axis=-1, keepdims=True)
    spread = jnp.mean(center * center, axis=-1, keepdims=True)
    rstd = lax.rsqrt(spread + 1e-05)
    return center * rstd, rstd


def norm_back(d, xhat, rstd, gain):
    dg = d * gain
    first = jnp.mean(dg, axis=-1, keepdims=True)
    second = jnp.mean(dg * xhat, axis=-1, keepdims=True)
    return rstd * (dg - first - xhat * second)


def col_sum(values):
    return jnp.sum(values, axis=0, keepdims=True)


def half_mask(rows, half):
    lane = lax.broadcasted_iota(jnp.int32, (rows, PAIR), 1)
    return (lane >= HEAD_DIM) if half else (lane < HEAD_DIM)


def held_rows(ids, parts, stepped):
    me, section = ids[0], ids[1]
    for side in range(2):
        half = section ^ side
        by = (0, 1 + half, 2 - half, 3) if stepped else (0, 1, 2, 3)
        for k, part in zip(by, parts[side]):
            yield (me ^ k) * 2 + half, part


def place_rows(ids, full_ref, parts, stepped, first_col):
    width = full_ref.shape[1]
    for place, part in held_rows(ids, parts, stepped):
        rows = part.shape[0]
        at = pl.multiple_of(place * rows, rows)
        full_ref[pl.ds(at, rows), :] = part[:, first_col : first_col + width]


def pack_kernel(ids, out, up, down, stay_ref, swap_ref, sems):
    section = ids[1]
    rows = out.shape[0] // 2
    copies = []

    def move(source, target):
        copy = pltpu.make_async_copy(source, target, sems.at[len(copies)])
        copy.start()
        copies.append(copy)

    for half, ref in ((1 - section, swap_ref), (section, stay_ref)):
        at = pl.ds(pl.multiple_of(half * rows, rows), rows)
        move(out.at[at, :], ref.at[:, :D])
        move(up.at[at, :], ref.at[:, D : D + FF])
        for j in range(4):
            at = pl.ds(pl.multiple_of(half * (4 * rows) + j * rows, rows), rows)
            move(down.at[at, :], ref.at[:, D + FF + j * D : D + FF + (j + 1) * D])
    for copy in copies:
        copy.wait()


def small_kernel(gains, biases, up_b, small_ref):
    bias = up_b[...]
    small_ref[...] = jnp.concatenate(
        [gains[...], biases[...]]
        + [bias[:, j * D : (j + 1) * D] for j in range(4)]
        + [jnp.zeros((4, D), F32)],
        axis=0,
    )


def pick_kernel(ids, stay, got, zero_ref, one_ref):
    first = ids[1] == 0
    here, there = stay[...], got[...]
    zero_ref[...] = jnp.where(first, here, there)
    one_ref[...] = jnp.where(first, there, here)


def outgoing_kernel(ids, pair, gouts, block_ref, half_ref):
    section = ids[1]
    low = ids[0] < 2
    here = jnp.where(low, pair[0], pair[1])
    there = jnp.where(low, pair[1], pair[0])
    block_ref[0] = jnp.where(section == 0, here, there)
    block_ref[1] = jnp.where(low, gouts[1], gouts[0])
    cut = half_ref.shape[0]
    half_ref[...] = jnp.where(section == 0, there[:cut], there[cut:])


def arrange_kernel(
    ids, present, pair, gouts, mine, other, half_mine, half_other, own, core, near, across, gout
):
    section = ids[1]
    first = section == 0
    local = jnp.where(ids[0] < 2, pair[0], pair[1])
    beside = jnp.where(first, mine[0], other[0])
    far = jnp.where(first, other[0], mine[0])
    top, bottom = half_mine[...], half_other[...]
    diagonal = jnp.concatenate(
        [jnp.where(first, top, bottom), jnp.where(first, bottom, top)], axis=0
    )
    home = section == ids[0] >> 1
    own[...] = jnp.where(home, local, far)
    core[...] = jnp.where(home, far, local)
    near[...] = jnp.where(home, beside, diagonal)
    across[...] = jnp.where(home, diagonal, beside)
    mask = present[0, ids[0] >> 1].astype(F32)
    far = jnp.where(first, other[1], mine[1])
    local = jnp.where(ids[0] < 2, gouts[0], gouts[1])
    gout[...] = (jnp.where(home, local, far).astype(F32) * mask).astype(BF)


def order_kernel(ids, zero, one, same_ref, swap_ref):
    low = ids[0] < 2
    same_ref[...] = jnp.where(low, zero[...], one[...])
    swap_ref[...] = jnp.where(low, one[...], zero[...])


def clips_kernel(ids, same, swap, out_ref):
    first = ids[1] == 0
    out_ref[0, 0, 0] = jnp.where(first, same[...], swap[...])
    out_ref[0, 0, 1] = jnp.where(first, swap[...], same[...])


def choose_kernel(n, ids, mlp, attn, both, out_ref):
    first = ids[1] == 0
    out_ref[: 2 * n, :] = jnp.where(first, both[: 2 * n, :], mlp[...])
    out_ref[2 * n :, :] = jnp.where(first, both[2 * n : 3 * n, :], attn[:n, :])


def section_sum_kernel(stepped, *refs):
    parts = len(refs) // (6 if stepped else 7)
    outs = refs[3 * parts :]
    per = len(outs) // parts
    for part in range(parts):
        keep, got_one, got_two = refs[3 * part : 3 * part + 3]
        own_ref, *others = outs[per * part : per * part + per]
        sums = [
            keep[e].astype(F32) + (got_one, got_two)[e // 2][e % 2].astype(F32) for e in range(4)
        ]
        own_ref[...] = sums[0]
        if stepped:
            others[0][0] = sums[1].astype(BF)
            others[0][1] = sums[2].astype(BF)
            others[1][...] = sums[3]
        else:
            for ref, total in zip(others, sums[1:]):
                ref[...] = total.astype(BF)


def second_kernel(second, got, out_ref):
    out_ref[...] = (second[...] + got[1].astype(F32)).astype(BF)


def spread_kernel(groups, terms, ids, *refs):
    count = len(groups)
    outs = refs[terms * count :]
    size = len(outs)
    rows = D // SHARDS // size
    me = ids[3]
    base = 0
    for part in range(count):
        total = refs[terms * part][...]
        for ref in refs[terms * part + 1 : terms * part + terms]:
            total = total + (ref[0] if len(ref.shape) == 3 else ref[...]).astype(F32)
        end = base + groups[part] * rows
        tail = total[groups[part] * size * rows :, :]
        if tail.shape[0]:
            for ref in outs:
                ref[end : end + tail.shape[0], :] = tail.astype(ref.dtype)
        for r in range(size):
            block = jnp.concatenate(
                [
                    total[(g * size + r) * rows : (g * size + r + 1) * rows, :]
                    for g in range(groups[part])
                ],
                axis=0,
            )
            for k, ref in enumerate(outs):

                @pl.when(me ^ k == r)
                def _():
                    ref[base:end, :] = block.astype(ref.dtype)

        base = end + tail.shape[0]


def finish_kernel(
    ids, mlp_zero, attn_zero, both_one, got,
    qkv, out, up, down, gain, bias, up_vec,
):
    first = ids[1] == 0

    def sides(zero, one, other):
        own = jnp.where(first, zero, one)
        return jnp.where(first, own, other), jnp.where(first, other, own)

    n = mlp_zero.shape[0] // 2
    low, high = sides(mlp_zero[...], both_one[: 2 * n, :], got[: 2 * n, :])
    up[0, :, :HALF] = low[:n]
    up[0, :, HALF:] = high[:n]
    for t, side in enumerate((low, high)):
        for j in range(2):
            at = (2 * t + j) * n
            down[0, at : at + n, :] = side[n:, j * D : (j + 1) * D]
    low, high = sides(attn_zero[:n, :], both_one[2 * n : 3 * n, :], got[2 * n :, :])
    qkv[0, :, :HALF] = low
    qkv[0, :, HALF:] = high[:, :D]
    out[0] = high[:, D:]
    vec_zero, vec_one = attn_zero[n:, :], both_one[3 * n :, :]
    sums = jnp.where(first, vec_zero, vec_one)

    def taken(values, width):
        length = values.shape[1]
        turn = lax.rem(length - ids[2] * width, length)
        return pltpu.roll(values, turn, 1)[:, :width]

    rows = []
    for r in range(4):
        rows += [sums[r : r + 1, :D], sums[r : r + 1, D:]]
    vec = taken(jnp.concatenate(rows, axis=0), n)
    gain[0] = vec[:2]
    for r in range(6):
        bias[r] = vec[2 + r : 3 + r]
    both = jnp.concatenate([sums[4:5], sums[5:6]], axis=1)
    up_vec[...] = taken(jnp.broadcast_to(both, (8, FF)), 4 * n)[:1]


def attend_kernel(
    layer, ids, x0, x1, x2, x3, w0, w1, w2, w3, o0, o1, o2, o3, small,
    w_ref, xhat_ref, q_ref, k_ref, v_ref, lse_ref, mixed_ref,
):
    me = ids[0]
    rows = x0.shape[0]
    own_layer = ids[1] == layer
    for k, (own, other) in enumerate(((w0, o0), (w1, o1), (w2, o2), (w3, o3))):
        count = own.shape[0]
        at = pl.multiple_of((me ^ k) * count, count)
        w_ref[pl.ds(at, count), :] = jnp.where(own_layer, own[...], other[...])
    gains, biases = small[0:2, :], small[2:8, :]
    gain, shift = gains[0:1, :], biases[0:1, :]
    for r, x in enumerate((x0, x1, x2, x3)):
        xhat, unused = normed(x[...].astype(F32))
        xhat_ref[r * rows : (r + 1) * rows, :] = xhat.astype(BF)
        a = (xhat * gain + shift).astype(BF)
        if r == 0:
            q = (dot(a, w_ref[:, :D]) + biases[1:2, :]).astype(BF)
            q_ref[...] = (q.astype(F32) * (HEAD_DIM ** (-0.5))).astype(BF)
        kv = dot(a, w_ref[:, D:])
        k_ref[r * rows : (r + 1) * rows, :] = kv[:, :D].astype(BF)
        v_ref[r * rows : (r + 1) * rows, :] = (kv[:, D:] + biases[2:3, :]).astype(BF)

    def one_pair(sample, pair, worst):
        cols = pl.ds(pl.multiple_of(pair * PAIR, PAIR), PAIR)
        k_pair = k_ref[:, cols]
        v_t = v_ref[:, cols].T
        q_pair = q_ref[:, cols].astype(F32)
        mixed_t = []
        for half in range(2):
            qm = jnp.where(half_mask(rows, half), q_pair, 0.0).astype(BF)
            s = dot(k_pair, qm, NT)
            top = jnp.max(s[:sample], axis=0, keepdims=True)
            e = jnp.exp(s - top)
            total = jnp.sum(e, axis=0, keepdims=True)
            worst = jnp.maximum(worst, total)
            lse_ref[pl.ds(2 * pair + half, 1), :] = top + jnp.log(total)
            o = dot(v_t[half * HEAD_DIM : (half + 1) * HEAD_DIM, :], e.astype(BF))
            mixed_t.append(o * (1.0 / total))
        mixed_ref[:, cols] = jnp.concatenate(mixed_t, axis=0).T.astype(BF)
        return worst

    keys = k_ref.shape[0]
    start = jnp.zeros((1, rows), F32)
    worst = lax.fori_loop(
        0, HEADS // 2, functools.partial(one_pair, keys // 8), start, unroll=True
    )

    @pl.when(jnp.max(worst) > LARGEST_SUM)
    def _():
        lax.fori_loop(0, HEADS // 2, functools.partial(one_pair, keys), start)


def mlp_kernel(stepped, ids, present, x0, mixed, *refs):
    out_ref, resid_ref, z_ref, slope_ref, wo_ref, w1_ref, w2_ref = refs[-7:]
    small = refs[-8]
    count = (len(refs) - 8) // 2
    parts = [refs[:count], refs[count : 2 * count]]
    if stepped:
        parts = [(own, got, pair.at[0], pair.at[1]) for own, got, pair in parts]
    place_rows(ids, wo_ref, parts, stepped, 0)
    place_rows(ids, w1_ref, parts, stepped, D)
    for place, part in held_rows(ids, parts, stepped):
        rows = part.shape[0]
        for j in range(4):
            at = pl.multiple_of((place * 4 + j) * rows, rows)
            left = D + FF + j * D
            w2_ref[pl.ds(at, rows), :] = part[:, left : left + D]
    gains, biases = small[0:2, :], small[2:8, :]
    up_b = jnp.concatenate([small[8 + j : 9 + j, :] for j in range(4)], axis=1)
    resid = x0[...].astype(F32) + (dot(mixed[...], wo_ref[...]) + biases[3:4, :])
    resid_ref[...] = resid
    xhat, unused = normed(resid)
    c = (xhat * gains[1:2, :] + biases[4:5, :]).astype(BF)
    upper = dot(c, w1_ref[...]) + up_b
    phi = 0.5 * (1.0 + lax.erf(upper * (2.0 ** -0.5)))
    z = (upper * phi).astype(BF)
    z_ref[...] = z
    bell = jnp.exp(-0.5 * upper * upper) * 0.3989422804014327
    slope_ref[...] = (phi + upper * bell).astype(BF)
    out = resid + (dot(z, w2_ref[...]) + biases[5:6, :])
    out_ref[...] = (out * present[0, ids[0] >> 1].astype(F32)).astype(BF)


def mlp_back_kernel(
    gout, z, slope, resid, wo, w1, w2, small,
    dresid_ref, ga_ref, du_ref, c_ref, dmixed_ref, vec_ref, upvec_ref,
):
    gains, biases = small[0:2, :], small[2:8, :]
    gm = gout[...]
    dz = dot(gm, w2[...], NT)
    du = (dz * slope[...].astype(F32)).astype(BF)
    du_ref[...] = du
    dc = dot(du, w1[...], NT)
    xhat, rstd = normed(resid[...])
    gain = gains[1:2, :]
    c_ref[...] = (xhat * gain + biases[4:5, :]).astype(BF)
    g_full = gm.astype(F32)
    dresid = g_full + norm_back(dc, xhat, rstd, gain)
    dresid_ref[...] = dresid
    ga = dresid.astype(BF)
    ga_ref[...] = ga
    dmixed_ref[...] = dot(ga, wo[...], NT).astype(BF)
    vec_ref[...] = jnp.concatenate(
        [
            col_sum(dc * xhat),
            col_sum(dc),
            col_sum(ga.astype(F32)),
            col_sum(g_full),
            jnp.zeros((4, D), F32),
        ],
        axis=0,
    )
    upvec_ref[...] = col_sum(du.astype(F32))


def attend_back_kernel(
    q_ref, k_ref, v_ref, lse, mixed, dmixed, xhat_ref, w_ref,
    own_ref, near_ref, swap_ref, dq_ref, dkv_ref, vec_ref,
):
    rows = q_ref.shape[0]

    def one_pair(pair, carry):
        cols = pl.ds(pl.multiple_of(pair * PAIR, PAIR), PAIR)
        k_pair, v_pair = k_ref[:, cols], v_ref[:, cols]
        k_t = k_pair.T
        q_pair = q_ref[:, cols].astype(F32)
        do_pair = dmixed[:, cols].astype(F32)
        prod_t = (mixed[:, cols].astype(F32) * do_pair).T
        dq_t, ps, dss, qms, doms = [], [], [], [], []
        for half in range(2):
            keep = half_mask(rows, half)
            qm = jnp.where(keep, q_pair, 0.0).astype(BF)
            dom = jnp.where(keep, do_pair, 0.0).astype(BF)
            p = jnp.exp(dot(k_pair, qm, NT) - lse[pl.ds(2 * pair + half, 1), :])
            dp = dot(v_pair, dom, NT)
            delta = col_sum(prod_t[half * HEAD_DIM : (half + 1) * HEAD_DIM, :])
            ds = (p * (dp - delta)).astype(BF)
            dq_t.append(
                dot(k_t[half * HEAD_DIM : (half + 1) * HEAD_DIM, :], ds) * (HEAD_DIM ** (-0.5))
            )
            ps.append(p.astype(BF))
            dss.append(ds)
            qms.append(qm)
            doms.append(dom)
        dkv_ref[:, cols] = dot(
            jnp.concatenate(dss, axis=1), jnp.concatenate(qms, axis=0)
        ).astype(BF)
        dkv_ref[:, pl.ds(pl.multiple_of(D + pair * PAIR, PAIR), PAIR)] = dot(
            jnp.concatenate(ps, axis=1), jnp.concatenate(doms, axis=0)
        ).astype(BF)
        dq_ref[:, cols] = jnp.concatenate(dq_t, axis=0).T.astype(BF)
        return carry

    lax.fori_loop(0, HEADS // 2, one_pair, 0)
    dq = dq_ref[...]
    gain_sum = jnp.zeros((1, D), F32)
    shift_sum = jnp.zeros((1, D), F32)
    outs = (own_ref, swap_ref.at[0], near_ref, swap_ref.at[1])
    for r, da_ref in enumerate(outs):
        at = slice(r * rows, (r + 1) * rows)
        da = dot(dkv_ref[at, :], w_ref[:, D:], NT)
        if r == 0:
            da = da + dot(dq, w_ref[:, :D], NT)
        gain_sum = gain_sum + col_sum(da * xhat_ref[at, :].astype(F32))
        shift_sum = shift_sum + col_sum(da)
        da_ref[...] = da.astype(da_ref.dtype)
    vec_ref[...] = jnp.concatenate(
        [
            gain_sum,
            shift_sum,
            col_sum(dq.astype(F32)),
            col_sum(dkv_ref[:, D:].astype(F32)),
            jnp.zeros((4, D), F32),
        ],
        axis=0,
    )


def norm_back_kernel(da_own, da_core, da_near, x0, dresid, small, out_ref):
    da = da_own[...] + da_core[0].astype(F32) + da_near[...].astype(F32)
    xhat, rstd = normed(x0[...].astype(F32))
    out_ref[...] = (dresid[...] + norm_back(da, xhat, rstd, small[0:1, :])).astype(BF)


def regroup(grad, s, replicas):
    rows = grad.shape[0] // (replicas * SHARDS)
    pieces = []
    for r in range(replicas):
        start = (r * SHARDS + s) * rows
        pieces.append(grad[start : start + rows, :])
    return pieces


def slot_of(ids, s, side):
    by = ids[0] ^ s
    if side is None:
        return by
    turned = jnp.where(side == 0, by, ((by & 1) << 1) | (by >> 1))
    return turned ^ (turned >> 1)


def put(refs, slot, at, block):
    @pl.when(slot < 2)
    def _():
        refs[0][slot, at, :] = block

    @pl.when(slot >= 2)
    def _():
        refs[1][slot - 2, at, :] = block


def grad_kernel(
    replicas, layer, ids, c, du, z, gm, xhat, dq, dkv, mixed, ga, small, vec_one, vec_two,
    upvec, *outs,
):
    section = ids[1]
    first = section == 0
    base = D // SHARDS
    start_of = 2 * base if layer == 1 else 0
    side = section if layer == 1 else None

    def store(refs, s, at, own, other):
        keep_ref, *send_refs = refs
        keep_ref[slot_of(ids, s, side), at, :] = own.astype(BF)
        away = None if side is None else 1 - side
        put(send_refs, slot_of(ids, s, away), at, other.astype(BF))

    def store_halves(refs, grad, at):
        left, right = grad[:, :HALF], grad[:, HALF:]
        own = jnp.where(first, left, right)
        other = jnp.where(first, right, left)
        for s in range(SHARDS):
            blocks = [
                jnp.concatenate(regroup(half, s, replicas), axis=0) for half in (own, other)
            ]
            store(refs, s, at, *blocks)

    store_halves(outs[:3], dot(c[...], du[...], TN), slice(0, base))
    grad = dot(z[...], gm[...], TN)
    rows = FF // (replicas * SHARDS)
    sub = rows // 4
    for s in range(SHARDS):
        sides = ([], [])
        for r in range(replicas):
            start = (r * SHARDS + s) * rows
            parts = [grad[start + j * sub : start + (j + 1) * sub, :] for j in range(4)]
            sides[0].append(jnp.concatenate(parts[:2], axis=1))
            sides[1].append(jnp.concatenate(parts[2:], axis=1))
        low, high = (jnp.concatenate(side, axis=0) for side in sides)
        own, other = jnp.where(first, low, high), jnp.where(first, high, low)
        store(outs[:3], s, slice(base, 2 * base), own, other)
    count = dq.shape[0]
    a = (xhat[...].astype(F32) * small[0:1, :] + small[2:3, :]).astype(BF)
    grad = jnp.concatenate(
        [
            dot(a[:count, :], dq[...], TN),
            dot(a, dkv[...], TN),
            dot(mixed[...], ga[...], TN),
        ],
        axis=1,
    )
    store_halves(outs[-3:], grad, slice(start_of, start_of + base))
    one, two, up = vec_one[...], vec_two[...], upvec[...]

    def wide(left, right):
        return jnp.concatenate([left, right], axis=1)

    vec = jnp.concatenate(
        [
            wide(one[0:1], two[0:1]),
            wide(one[1:2], one[2:3]),
            wide(one[3:4], two[2:3]),
            wide(two[1:2], two[3:4]),
            up[:, :HALF],
            up[:, HALF:],
            jnp.zeros((VEC_ROWS - 6, HALF), F32),
        ],
        axis=0,
    ).astype(BF)
    at = slice(start_of + base, start_of + base + VEC_ROWS)
    for s in range(SHARDS):
        outs[-3][s, at, :] = vec
        outs[-2 + s // 2][s % 2, at, :] = vec


def shard_spread(block):
    return [block] + [xor_pass(block, "shard", k) for k in (1, 2, 3)]


def stack_kernel(one, two, out_ref):
    out_ref[0] = one[...]
    out_ref[1] = two[...]


def shard_steps(block):
    return block, lax.ppermute(block, ("section", "shard"), split_pairs(1, 2))


def shard_steps_end(block, got, tie):
    (pair,) = call(
        stack_kernel,
        [sds((2,) + block.shape, BF)],
        [block, got],
        "stack",
        1_000_000,
        scalars=0,
        ties=(tie,),
    )
    return [block, got, lax.ppermute(pair, ("section", "shard"), split_pairs(2, 1))]


def both_cores(parts):
    return [*parts, *(xor_pass(part, "section", 1) for part in parts)]


def clip_frames(own):
    near = xor_pass(own, "shard", 1)
    return [own, xor_pass(own, "section", 1), near, xor_pass(near, "section", 1)]


def first_frames(ids, present, pair, gouts, weight):
    rows = sds(pair.shape[1:], BF)
    half = sds((pair.shape[1] // 2, pair.shape[2]), BF)
    block, part = call(
        outgoing_kernel, [sds(pair.shape, BF), half], [ids, pair, gouts], "outgoing", 1_000_000
    )
    mine = lax.ppermute(block, ("section", "shard"), split_pairs(1, 2))
    half_mine = xor_pass(part, "shard", 3)
    parts = shard_spread(weight)
    mine, half_mine = after([mine, half_mine], *parts[1:])
    other, half_other = (xor_pass(got, "section", 1) for got in (mine, half_mine))
    *frames, gout = call(
        arrange_kernel,
        [rows] * 5,
        [ids, present, pair, gouts, mine, other, half_mine, half_other],
        "arrange",
        1_000_000,
        scalars=2,
    )
    return block, frames, gout, both_cores(parts)


def from_clip(ids, pair, ties):
    count = lax.axis_size("shard")

    def pairs(flip):
        out = []
        for sec in range(2):
            for i in range(count):
                clip, low = i >> 1, i & 1
                out.append((sec * count + i, (clip ^ flip) * count + sec * 2 + low))
        return out

    both = ("section", "shard")
    rows = sds(pair[0].shape, BF)
    same, swap = call(order_kernel, [rows, rows], [ids, *pair], "order", 1_000_000, ties=ties)
    return lax.ppermute(same, both, pairs(0)), lax.ppermute(swap, both, pairs(1))


def clips_of(ids, same, swap):
    out = sds((1, 1, 2) + same.shape, BF)
    return call(clips_kernel, [out], [ids, same, swap], "clips", 1_000_000)[0]


def section_sum(parts, stepped, ties):
    args, outs = [], []
    for keep, *send in parts:
        rows = keep.shape[1]
        args += [keep, *(xor_pass(part, "section", 1) for part in send)]
        outs.append(sds((rows, HALF), F32))
        if stepped:
            outs += [sds((2, rows, HALF), BF), sds((rows, HALF), F32)]
        else:
            outs += [sds((rows, HALF), BF)] * 3
    sums = call(
        functools.partial(section_sum_kernel, stepped),
        outs,
        args,
        "section_sum",
        1_000_000,
        scalars=0,
        ties=ties,
    )
    per = len(outs) // len(parts)
    return [sums[i * per : (i + 1) * per] for i in range(len(parts))]


def split_pairs(low, high):
    count = lax.axis_size("shard")
    return [(i, i ^ low) for i in range(count)] + [
        (count + i, count + (i ^ high)) for i in range(count)
    ]


def shard_first(first_out, low):
    return lax.ppermute(first_out, ("section", "shard"), split_pairs(low, 3 - low))


def shard_second(second_out, got, low, ties):
    (message,) = call(
        second_kernel,
        [sds(second_out.shape, BF)],
        [second_out, got],
        "second",
        1_000_000,
        scalars=0,
        ties=ties,
    )
    return lax.ppermute(message, ("section", "shard"), split_pairs(3 - low, low))


def replica_sum(ids, parts, ties):
    size = lax.axis_size("replica")
    rows = D // SHARDS // size
    groups = [(part[1].shape[0] - part[0]) // (D // SHARDS) for part in parts]
    if size > SHARDS:
        pieces = []
        for (fixed, *terms), count in zip(parts, groups):
            summed = sum((t[0] if t.ndim == 3 else t).astype(F32) for t in terms)
            blocks = summed[: count * size * rows].reshape(count, size, rows, HALF)
            blocks = blocks.transpose(1, 0, 2, 3).reshape(size, count * rows, HALF)
            mine = lax.psum_scatter(blocks.astype(BF), "replica", scatter_dimension=0)
            pieces.append(mine.astype(F32))
            if fixed:
                pieces.append(lax.psum(summed[count * size * rows :], "replica"))
        return jnp.concatenate(pieces, axis=0)
    count = sum(groups) * rows + sum(part[0] for part in parts)
    own, *messages = call(
        functools.partial(spread_kernel, groups, len(parts[0]) - 1),
        [sds((count, HALF), F32)] + [sds((count, HALF), BF)] * (size - 1),
        [ids] + [array for part in parts for array in part[1:]],
        "spread",
        1_000_000,
        ties=ties,
    )
    for k, message in enumerate(messages):
        own = own + xor_pass(message, "replica", k + 1).astype(F32)
    return own


def local(
    inputs,
    cotangent,
    clip_present,
    qkv_weight,
    out_weight,
    up_weight,
    down_weight,
    norm_gains,
    biases,
    up_bias,
):
    section = lax.axis_index("section")
    shard = lax.axis_index("shard")
    replica = lax.axis_index("replica")
    replicas = lax.axis_size("replica")
    first = section == 0
    rows = inputs.shape[2]
    place = replica * SHARDS + shard
    ids = jnp.stack([shard, section, place, replica]).astype(jnp.int32)
    own_rows = D // SHARDS

    ready, frames, gout_last, qkv_part = first_frames(
        ids, clip_present, inputs[0], cotangent[0], qkv_weight[0]
    )


    half_rows = own_rows // 2
    packed = sds((half_rows, 9 * D), BF)
    stay, swap = call(
        pack_kernel,
        [packed, packed],
        [ids, out_weight[0], up_weight[0], down_weight[0]],
        "pack",
        1_000_000,
        raw=3,
        ties=(ready,),
        scratch=[pltpu.SemaphoreType.DMA((12,))],
    )
    got = xor_pass(swap, "section", 1)
    (small,) = call(
        small_kernel,
        [sds((16, D), F32)],
        [norm_gains[0], biases[0], up_bias[0][None]],
        "small",
        1_000_000,
        scalars=0,
        ties=(ready,),
    )
    other_small = xor_pass(small, "section", 1)
    both = sds((16, D), F32)
    small_layers = call(
        pick_kernel, [both, both], [ids, small, other_small], "small_pick", 1_000_000
    )
    rest_zero, rest_one = call(
        pick_kernel, [packed, packed], [ids, stay, got], "pick", 1_000_000,
        ties=(qkv_part[1],),
    )
    rest_part = shard_spread(rest_zero)

    whole = SHARDS * rows
    saved = []
    outs = []
    for layer in range(2):
        small = small_layers[layer]
        w_qkv, xhat, q, k, v, lse, mixed = call(
            functools.partial(attend_kernel, layer),
            [
                sds((D, 3 * D), BF),
                sds((whole, D), BF),
                sds((rows, D), BF),
                sds((whole, D), BF),
                sds((whole, D), BF),
                sds((8, rows), F32),
                sds((rows, D), BF),
            ],
            [ids, *frames, *qkv_part, small],
            "attend",
            4_000_000_000,
            ties=last_other if layer == 1 else (),
        )
        if layer == 0:
            last_parts = shard_steps(after([rest_one], mixed)[0])
            rest_part = both_cores([rest_part[0], *after(rest_part[1:], mixed)])
        else:
            (pair,) = after(last_parts[2:], mixed)
            rest_part = [*last_parts[:2], pair, *last_other, xor_pass(pair, "section", 1)]
        out, resid, z, slope, w_out, w_up, w_down = call(
            functools.partial(mlp_kernel, layer == 1),
            [
                sds((rows, D), BF),
                sds((rows, D), F32),
                sds((rows, FF), BF),
                sds((rows, FF), BF),
                sds((D, D), BF),
                sds((D, FF), BF),
                sds((FF, D), BF),
            ],
            [ids, clip_present, frames[0], mixed, *rest_part, small],
            "mlp",
            2_000_000_000,
            scalars=2,
        )
        saved.append(
            (frames[0], w_qkv, xhat, q, k, v, lse, mixed, resid, z, slope, w_out, w_up, w_down)
        )
        outs.append(out)
        if layer == 0:
            frames = clip_frames(out)
            last_other = tuple(xor_pass(part, "section", 1) for part in last_parts)
            last_parts = shard_steps_end(*last_parts, frames[2])

    gout = gout_last
    shares = [None, None]
    grads = [None, None]
    before = ()
    for layer in (1, 0):
        small = small_layers[layer]
        x0, w_qkv, xhat, q, k, v, lse, mixed, resid, z, slope, w_out, w_up, w_down = saved[layer]
        dresid, ga, du, c, dmixed, vec_two, upvec = call(
            mlp_back_kernel,
            [
                sds((rows, D), F32),
                sds((rows, D), BF),
                sds((rows, FF), BF),
                sds((rows, D), BF),
                sds((rows, D), BF),
                sds((8, D), F32),
                sds((1, FF), F32),
            ],
            [gout, z, slope, resid, w_out, w_up, w_down, small],
            "mlp_back",
            2_000_000_000,
            scalars=0,
        )
        da_own, da_near, da_swap, dq, dkv, vec_one = call(
            attend_back_kernel,
            [
                sds((rows, D), F32),
                sds((rows, D), F32),
                sds((2, rows, D), BF),
                sds((rows, D), BF),
                sds((whole, 2 * D), BF),
                sds((8, D), F32),
            ],
            [q, k, v, lse, mixed, dmixed, xhat, w_qkv],
            "attend_back",
            8_000_000_000,
            scalars=0,
            ties=before,
        )
        got = xor_pass(da_swap, "section", 1)
        near = (da_near + got[1].astype(F32)).astype(BF)
        back = xor_pass(near, "shard", 1)
        counts = [3 * own_rows + VEC_ROWS]
        if layer == 0:
            counts = [2 * own_rows, own_rows + VEC_ROWS]
        shapes = []
        for count in counts:
            shapes += [sds((SHARDS, count, HALF), BF)] + [sds((2, count, HALF), BF)] * 2
        parts = call(
            functools.partial(grad_kernel, replicas, layer),
            shapes,
            [ids, c, du, z, gout, xhat, dq, dkv, mixed, ga, small, vec_one, vec_two, upvec],
            "grad",
            4_000_000_000,
            ties=(near,) if layer == 1 else (),
        )
        if layer == 1:
            keep, *send = parts
            parts = [(keep, *after(send, back))]
            ((own, first_out, second_out),) = section_sum(parts, True, ())
            before = (first_out,)
        else:
            outs_back = from_clip(ids, outs, (da_swap,))
            parts = section_sum((parts[:3], parts[3:]), False, (back, late, *outs_back))
        (gin,) = call(
            norm_back_kernel,
            [sds((rows, D), BF)],
            [da_own, got, back, x0, dresid, small],
            "norm_back",
            100_000_000,
            scalars=0,
        )
        grads[layer] = gin
        gout = gin
        if layer == 1:
            got = shard_first(first_out, 1)
            late = shard_second(second_out, got, 1, ())
            shares[1] = replica_sum(ids, [(VEC_ROWS, own, got, late)], ())
        else:
            sums = []
            for (own, *messages), fixed in zip(parts, (0, VEC_ROWS)):
                gots = [xor_pass(m, "shard", k + 1) for k, m in enumerate(messages)]
                sums.append((fixed, own, *gots))
            shares[0] = [
                replica_sum(ids, sums[:1], (shares[1],)), replica_sum(ids, sums[1:], ())
            ]

    outputs_local = clips_of(ids, *outs_back)
    grads_local = clips_of(ids, *from_clip(ids, grads, ()))
    n = own_rows // replicas
    (away,) = call(
        functools.partial(choose_kernel, n),
        [sds((3 * n, HALF), F32)],
        [ids, *shares[0], shares[1]],
        "choose",
        1_000_000,
        ties=(outputs_local, grads_local),
    )
    got = xor_pass(away, "section", 1)
    qkv_grad, out_grad, up_grad, down_grad, gain, bias, up_vec = call(
        finish_kernel,
        [
            sds((1, n, 3 * D), F32),
            sds((1, n, D), F32),
            sds((1, n, FF), F32),
            sds((1, 4 * n, D), F32),
            sds((1, 2, n), F32),
            sds((6, 1, n), F32),
            sds((1, 4 * n), F32),
        ],
        [ids, *shares[0], shares[1], got],
        "finish",
        1_000_000,
    )
    return (
        outputs_local,
        grads_local,
        qkv_grad,
        out_grad,
        up_grad,
        down_grad,
        gain,
        bias.transpose(1, 0, 2),
        up_vec,
    )


def solution(mesh):
    return jax.shard_map(
        local,
        mesh=mesh,
        in_specs=(
            P("replica", None, "shard", None),
            P("replica", None, "shard", None),
            P("replica", None),
            P("section", "shard", None),
            P("section", "shard", None),
            P("section", "shard", None),
            P("section", "shard", None),
            P("section", None, None),
            P("section", None, None),
            P("section", None),
        ),
        out_specs=(
            P("section", "replica", None, "shard", None),
            P("section", "replica", None, "shard", None),
            P("section", ("replica", "shard"), None),
            P("section", ("replica", "shard"), None),
            P("section", ("replica", "shard"), None),
            P("section", ("replica", "shard"), None),
            P("section", None, ("replica", "shard")),
            P("section", None, ("replica", "shard")),
            P("section", ("replica", "shard")),
        ),
        check_vma=False,
    )
```
